32 devices in a mesh: tm: 4 (over y, x), pts: 8 (over z, core).
Axes of the slice: x: 2, y: 2, z: 4, core: 2. Of those that a mesh axis runs over, the one named last changes fastest.
Arguments:
- codes: bfloat16 [11520, 5120], P('tm', 'pts'), as said below
- scales: float32 [11520], P('tm'), may hold values from 0.005 to 0.015
- weights: float32 [5120], P('pts'), may hold values from 0.5 to 4
- freq_indices: int32 [64], replicated, may hold values from 0 to 127, as said below
Outputs:
- cross_spectral: float32 [64, 2, 89, 89], P('pts')
The draws below stay inside these ranges and needn't reach their ends.
Inputs may be any that keep to these rules, and one draw needn't show every extreme that they name: `codes`: whole numbers. `freq_indices`: distinct bins.
All inputs are finite; a program needn't handle non-finite values.
Results may differ from the reference program's by a relative error of at most 0.0011.
Values may be sent and summed in bfloat16 or wider, within the bound.
A program may use at most 64 MiB of HBM per device.

```python
import math
import jax
import jax.numpy as jnp
from jax import lax

NFFT = 256
NF = 64
NB = 89
HOP = 128
TIME = 11520
POINTS = 5120
N_PTS = 8


def walk_from(start_key, step_key, count, width, start_lo, start_hi, step_reach):
    start_value = jax.random.randint(start_key, (1, width), start_lo, start_hi)
    step_values = jax.random.randint(step_key, (count - 1, width), -step_reach, step_reach + 1)
    return jnp.concatenate([start_value, start_value + jnp.cumsum(step_values, axis=0)], axis=0)


def draw_codes(key, part):
    subkeys = jax.random.split(key, 12)
    fine_grid = NFFT * 16
    hop_count = TIME // HOP
    tone_freq = jax.random.randint(subkeys[0], (POINTS,), 16, NFFT // 2 * 16)
    tone_phase = walk_from(subkeys[1], subkeys[2], hop_count, POINTS, 0, fine_grid, fine_grid // 6) % fine_grid
    tone_amp = jnp.clip(walk_from(subkeys[3], subkeys[4], hop_count, POINTS, 8, 29, 5), 4, 32)
    mode_freq = jax.random.randint(subkeys[5], (2,), 16, NFFT // 2 * 16)
    mode_phase = walk_from(subkeys[6], subkeys[7], hop_count, 2, 0, fine_grid, fine_grid // 6) % fine_grid
    mode_amp = jnp.clip(walk_from(subkeys[8], subkeys[9], hop_count, 2, 1, 3, 1), 1, 2)
    mode_coef = jax.random.randint(subkeys[10], (2, POINTS), -1, 2)
    noise_codes = jax.random.randint(subkeys[11], (hop_count, HOP, POINTS), -16, 17)
    sample_times = jnp.arange(TIME, dtype=jnp.int32).reshape(hop_count, HOP, 1)
    tone_turns = (sample_times * tone_freq[None, None, :] + tone_phase[:, None, :]) % fine_grid
    tone_wave = jnp.where(tone_turns < fine_grid // 2, 1, -1) * tone_amp[:, None, :]
    mode_turns = (sample_times * mode_freq[None, None, :] + mode_phase[:, None, :]) % fine_grid
    mode_wave = jnp.where(mode_turns < fine_grid // 2, 1, -1) * mode_amp[:, None, :]
    shared_wave = mode_wave[:, :, 0:1] * mode_coef[0][None, None, :] + mode_wave[:, :, 1:2] * mode_coef[1][None, None, :]
    total = (tone_wave + shared_wave + noise_codes).astype(jnp.int32)
    return total.reshape(TIME, POINTS).astype(jnp.float32).astype(jnp.bfloat16)


def draw_freq_indices(key, part):
    shuffled = jax.random.permutation(key, NFFT // 2 - 2) + 1
    ends = jnp.array([0, NFFT // 2 - 1], dtype=jnp.int32)
    return jnp.concatenate([ends, shuffled[:NF - 2].astype(jnp.int32)]).astype(jnp.int32)


def shard_levels(key, shape, shards, smallest, top_value):
    factor_of = 1.0
    for axis_at, blocks in shards:
        heights = jax.random.uniform(jax.random.fold_in(jax.random.fold_in(key, 6), axis_at), (blocks,), jnp.float32, smallest / len(shards), top_value / len(shards))
        factor_of = factor_of * jnp.repeat(jnp.exp(heights), shape[axis_at] // blocks).reshape((-1,) + (1,) * (len(shape) - 1 - axis_at))
    return factor_of


def setup_inputs(seed: int = 0) -> dict:
    keys = jax.random.split(jax.random.key(seed), 5)
    codes = draw_codes(jax.random.fold_in(keys[4], 71), 0)
    scales = jnp.clip(0.005 + 0.01 * jax.random.uniform(keys[1], (TIME,), jnp.float32) ** shard_levels(keys[1], (TIME,), ((0, 4),), -0.2, 0.2), 0.005, 0.015)
    weights = jnp.clip(jnp.exp(math.log(4.0) - 2.0794415 * jax.random.uniform(keys[2], (POINTS,), jnp.float32) ** shard_levels(keys[2], (POINTS,), ((0, 8),), -0.2, 0.2)), 0.5, 4.0)
    freq_indices = draw_freq_indices(jax.random.fold_in(keys[4], 71), 0)
    return {"codes": codes, "scales": scales, "weights": weights, "freq_indices": freq_indices}


def make_tables(freq_indices):
    sample = jnp.arange(NFFT, dtype=jnp.int32)
    phases = freq_indices[:, None] * sample[None, :] % NFFT
    angles = phases.astype(jnp.float32) * (2.0 * math.pi / NFFT)
    hann_window = 0.5 - 0.5 * jnp.cos(sample.astype(jnp.float32) * (2.0 * math.pi / NFFT))
    cosine_table = (0.25 * hann_window[None, :] * jnp.cos(angles)).astype(jnp.bfloat16)
    sine_table = (-0.25 * hann_window[None, :] * jnp.sin(angles)).astype(jnp.bfloat16)
    return (cosine_table, sine_table)

def reference(codes, scales, weights, freq_indices):
    cosine_table, sine_table = make_tables(freq_indices)
    cosine_wide = cosine_table.astype(jnp.float32)
    sine_wide = sine_table.astype(jnp.float32)
    group = POINTS // N_PTS

    def accumulate(index, running):
        first_point = (index * group).astype(jnp.int32)
        block_codes = lax.dynamic_slice_in_dim(codes, first_point, group, 1)
        block_weights = lax.dynamic_slice_in_dim(weights, first_point, group, 0)
        values = (block_codes.astype(jnp.float32) * scales[:, None]).astype(jnp.bfloat16)
        hop_rows = values.reshape(NB + 1, HOP, group)
        windows = jnp.concatenate([hop_rows[:-1], hop_rows[1:]], axis=1).astype(jnp.float32)
        real_part = jnp.einsum('fn,bnp->fbp', cosine_wide, windows)
        imag_part = jnp.einsum('fn,bnp->fbp', sine_wide, windows)
        root_weight = jnp.sqrt(block_weights / POINTS)
        scaled_re = (real_part * root_weight[None, None, :]).astype(jnp.bfloat16)
        scaled_im = (imag_part * root_weight[None, None, :]).astype(jnp.bfloat16)
        stacked = jnp.concatenate([scaled_re, scaled_im], axis=1).astype(jnp.float32)
        products = jnp.einsum('fip,fjp->fij', stacked, stacked)
        matrix_re = products[:, :NB, :NB] + products[:, NB:, NB:]
        matrix_im = products[:, :NB, NB:] - products[:, NB:, :NB]
        return running + jnp.stack([matrix_re, matrix_im], axis=1)
    start_value = jnp.zeros((NF, 2, NB, NB), jnp.float32)
    return lax.fori_loop(0, N_PTS, accumulate, start_value)
```

```python
import functools
import math

import jax
import jax.numpy as jnp
from jax import lax
from jax.experimental import pallas as pl
from jax.experimental.pallas import tpu as pltpu
from jax.sharding import PartitionSpec as P

NFFT = 256
HOP = NFFT // 2
HALF = HOP // 2
LANES = 128
SLOTS = 96
NT = 4
NZ = 4
QUARTERS = 4
ZSETS = ((0, 3), (1, 2))
MESH = pl.DeviceIdType.MESH


def make_tables(freq_indices):
    sample = jnp.arange(NFFT, dtype=jnp.int32)
    phases = freq_indices[:, None] * sample[None, :] % NFFT
    angles = phases.astype(jnp.float32) * (2.0 * math.pi / NFFT)
    hann_window = 0.5 - 0.5 * jnp.cos(sample.astype(jnp.float32) * (2.0 * math.pi / NFFT))
    cosine_table = (0.25 * hann_window[None, :] * jnp.cos(angles)).astype(jnp.bfloat16)
    sine_table = (-0.25 * hann_window[None, :] * jnp.sin(angles)).astype(jnp.bfloat16)
    return (cosine_table, sine_table)


def turn_cosine(turn):
    left = 64 - jnp.minimum(turn, NFFT - turn)
    x = left.astype(jnp.float32) * (2.0 * math.pi / NFFT)
    y = x * x
    poly = jnp.full_like(x, -1.0 / 39916800.0)
    for c in (1.0 / 362880.0, -1.0 / 5040.0, 1.0 / 120.0, -1.0 / 6.0, 1.0):
        poly = poly * y + c
    return x * poly


def kernel(
    total_points,
    codes_hbm, scales_hbm, weights_hbm, freq_ref, out_ref,
    codes_ref, scales_v, weights_v, spread, vals, table, sbuf, rbuf, spbuf, sprecv, stage,
    part, corebuf, summed, zbuf, gath,
    load_s, halo_s, halo_r, tm_s, tm_r, sp_s, sp_r, core_s, core_r, z_s, z_r, g_s, g_r,
):
    rows, points = codes_ref.shape
    t = lax.axis_index("tm")
    p = lax.axis_index("pts")
    z = p // 2
    c = p % 2
    odd = t % 2
    partner = p + 1 - 2 * c
    lane_tiles = points // LANES
    blocks = rows // HOP
    pairs = blocks // 2
    padded = rows + HALF

    early = (10 * HOP)
    late = rows - early - HALF
    edge_at = (1 - odd) * (rows - HALF)
    early_at = odd * (rows - early)
    late_at = odd * HALF + (1 - odd) * early

    def load(at, count, sem):
        at = pl.ds(pl.multiple_of(at, HALF), count)
        return pltpu.make_async_copy(codes_hbm.at[at], codes_ref.at[at], load_s.at[sem])

    load_scales = pltpu.make_async_copy(scales_hbm, scales_v, load_s.at[3])
    load_weights = pltpu.make_async_copy(weights_hbm, weights_v, load_s.at[4])
    load_edge = load(edge_at, HALF, 0)
    load_early = load(early_at, early, 1)
    load_late = load(late_at, late, 2)
    barrier = pltpu.get_barrier_semaphore()
    for d in range(1, NT):
        pl.semaphore_signal(barrier, inc=1, device_id=(t ^ d, p), device_id_type=MESH)
    pl.semaphore_signal(barrier, inc=1, device_id=(t, partner), device_id_type=MESH)
    for d in range(1, NZ):
        pl.semaphore_signal(barrier, inc=1, device_id=(t, (z + d) % NZ * 2 + c), device_id_type=MESH)
    load_scales.start()
    load_edge.start()
    load_early.start()
    load_weights.start()
    load_late.start()

    sample = lax.broadcasted_iota(jnp.int32, (8, NFFT), 1)
    sub = lax.broadcasted_iota(jnp.int32, (8, NFFT), 0)
    window_shape = 0.25 * (0.5 - 0.5 * turn_cosine(sample))
    shift = (sub % 2) * (NFFT // 4)

    def octet_table(dest, q):
        bins = jnp.zeros((8, NFFT), jnp.int32)
        for j in range(4):
            dest_p = ZSETS[q % 2][j // 2] * 2 + j % 2
            bins = jnp.where(sub // 2 == j, freq_ref[dest_p * 2 * NT + dest * 2 + q // 2], bins)
        return window_shape * turn_cosine((bins * sample + shift) % NFFT)

    for dest in range(NT):
        for half in range(2):
            at = dest * 32 + half * 16
            pair = [octet_table(dest, 2 * half), octet_table(dest, 2 * half + 1)]
            table[at:at + 16, :] = jnp.concatenate(pair, axis=0).astype(jnp.bfloat16)

    load_scales.wait()
    for g in range(-(-rows // HOP)):
        count = min(HOP, rows - g * HOP)
        line = scales_v[g * HOP:g * HOP + count].reshape(1, count)
        spread[g * HOP:g * HOP + count, :] = jnp.broadcast_to(line, (LANES, count)).T

    offset = odd * HALF

    def dequantize(i, carry):
        at = pl.ds(pl.multiple_of(i * HALF, HALF), HALF)
        to = pl.ds(pl.multiple_of(i * HALF + offset, HALF), HALF)
        scale = spread[at, :]
        for lane in range(lane_tiles):
            cols = slice(lane * LANES, (lane + 1) * LANES)
            vals[to, cols] = (codes_ref[at, cols].astype(jnp.float32) * scale).astype(jnp.bfloat16)
        return carry

    load_edge.wait()
    dequantize(edge_at // HALF, 0)
    halo_from = (1 - odd) * (rows - HALF) + odd * HALF
    halo_to = odd * rows
    halo_mine = (1 - odd) * rows

    def halo_copy(dst):
        return pltpu.make_async_remote_copy(
            src_ref=vals.at[pl.ds(pl.multiple_of(halo_from, HALF), HALF)],
            dst_ref=vals.at[pl.ds(pl.multiple_of(dst, HALF), HALF)],
            send_sem=halo_s, recv_sem=halo_r,
            device_id=(t ^ 1, p), device_id_type=MESH,
        )

    pl.semaphore_wait(barrier, NT + NZ - 1)
    halo_copy(halo_to).start()

    load_early.wait()
    lax.fori_loop(early_at // HALF, (early_at + early) // HALF, dequantize, 0)
    load_weights.wait()
    root_weight = jnp.sqrt(weights_v[...].reshape(1, points) / total_points)

    def spectrum(i):
        window = vals[pl.ds(pl.multiple_of(i * HOP, HOP), NFFT), :]
        return jnp.dot(table[...], window, preferred_element_type=jnp.float32) * root_weight

    def spectra(j, carry):
        jj = odd * (pairs - 1 - j) + (1 - odd) * j
        first = spectrum(2 * jj)
        second = spectrum(2 * jj + 1)
        for dest in range(NT):
            for q in range(QUARTERS):
                at = slice(dest * 32 + q * 8, dest * 32 + q * 8 + 8)
                both = jnp.concatenate([first[at], second[at]], axis=0)
                sbuf[q, dest, jj] = both.astype(jnp.bfloat16)
        return carry

    cuts = (0, 4, pairs - 1, pairs)
    partners = (3, 1, 2)

    def tiles_of(who, piece):
        count = cuts[piece + 1] - cuts[piece]
        flip = who % 2
        return flip * (pairs - cuts[piece + 1]) + (1 - flip) * cuts[piece], count

    def exchange(q, piece, d, source):
        at, count = tiles_of(source, piece)
        return pltpu.make_async_remote_copy(
            src_ref=sbuf.at[q, t ^ d, pl.ds(at, count)],
            dst_ref=rbuf.at[q, source, pl.ds(at, count)],
            send_sem=tm_s.at[q, piece, d - 1], recv_sem=tm_r.at[q, piece, d - 1],
            device_id=(t ^ d, p), device_id_type=MESH,
        )

    def straddle(h, d, source):
        return pltpu.make_async_remote_copy(
            src_ref=spbuf.at[h, t ^ d],
            dst_ref=sprecv.at[h, source - 1],
            send_sem=sp_s.at[h, d - 1], recv_sem=sp_r.at[h, d - 1],
            device_id=(t ^ d, p), device_id_type=MESH,
        )

    middle = (t == 1) | (t == 2)

    def send_straddle(h):
        @pl.when(middle)
        def _():
            for d in partners:
                straddle(h, d, t).start()

    def send(q, piece):
        for d in partners:
            exchange(q, piece, d, t).start()

    lax.fori_loop(cuts[0], cuts[1], spectra, 0)
    send(0, 0)
    load_late.wait()
    lax.fori_loop(late_at // HALF, (late_at + late) // HALF, dequantize, 0)
    lax.fori_loop(cuts[1], cuts[2], spectra, 0)
    send(0, 1)
    halo_copy(halo_mine).wait_recv()
    lax.fori_loop(cuts[2], cuts[3], spectra, 0)
    send(0, 2)

    @pl.when(middle)
    def _():
        hop = pl.ds(pl.multiple_of(odd * (padded - HOP), HOP), HOP)
        side = jnp.where(odd == 1, table[:, :HOP].astype(jnp.float32), table[:, HOP:].astype(jnp.float32))
        result = jnp.dot(side.astype(jnp.bfloat16), vals[hop, :], preferred_element_type=jnp.float32)
        result = (result * root_weight).astype(jnp.bfloat16)
        for dest in range(NT):
            for h in range(2):
                spbuf[h, dest] = result[dest * 32 + h * 16:dest * 32 + h * 16 + 16]
        for h in range(2):
            sprecv[h, t - 1] = spbuf[h, t]

    for h in range(2):
        send_straddle(h)
    for piece in range(3):
        send(1, piece)

    for lane in range(lane_tiles):
        for s in range(8):
            stage[lane, s * SLOTS + SLOTS - 8:(s + 1) * SLOTS, :] = jnp.zeros((8, LANES), jnp.float32)

    def place(b, octet):
        for lane in range(lane_tiles):
            stage[lane, pl.ds(b, 8, stride=SLOTS), :] = octet[:, lane * LANES:(lane + 1) * LANES]

    def unpack(source_ref, q, who, piece):
        at, count = tiles_of(who, piece)
        base = who * blocks + who // 2

        def one(i, carry):
            tile = source_ref[q, who, i].astype(jnp.float32)
            place(base + 2 * i, tile[:8])
            place(base + 2 * i + 1, tile[8:])
            return carry

        lax.fori_loop(at, at + count, one, 0)

    def gram(q, j):
        at = slice(j * 2 * SLOTS, (j + 1) * 2 * SLOTS)
        stacked = jnp.concatenate(
            [stage[lane, at, :].astype(jnp.bfloat16) for lane in range(lane_tiles)], axis=1
        )
        fill = jnp.zeros((LANES - SLOTS, points), jnp.bfloat16)
        wide = jnp.concatenate([stacked[:SLOTS], fill, stacked[SLOTS:], fill], axis=0)
        prod = lax.dot_general(
            stacked, wide, (((1,), (1,)), ((), ())), preferred_element_type=jnp.float32
        )
        real = prod[:SLOTS, :LANES] + prod[SLOTS:, LANES:]
        imag = prod[:SLOTS, LANES:] - prod[SLOTS:, :LANES]
        part[q, j % 2, j // 2] = real + imag

    def to_core(q):
        return pltpu.make_async_remote_copy(
            src_ref=part.at[q, 1 - c], dst_ref=corebuf.at[q],
            send_sem=core_s.at[q], recv_sem=core_r.at[q],
            device_id=(t, partner), device_id_type=MESH,
        )

    def to_z(q, s, source):
        return pltpu.make_async_remote_copy(
            src_ref=summed.at[q, s], dst_ref=zbuf.at[q, source],
            send_sem=z_s.at[q, s], recv_sem=z_r.at[q, source],
            device_id=(t, ZSETS[q % 2][s] * 2 + c), device_id_type=MESH,
        )

    def to_tm(k, d, source):
        return pltpu.make_async_remote_copy(
            src_ref=gath.at[source, k], dst_ref=gath.at[source, k],
            send_sem=g_s.at[k, d - 1], recv_sem=g_r.at[k, d - 1],
            device_id=(t ^ d, p), device_id_type=MESH,
        )

    def receive(q):
        for piece in range(3):
            unpack(sbuf, q, t, piece)
        for piece in range(3):
            for d in partners:
                exchange(q, piece, d, t ^ d).wait_recv()
                unpack(rbuf, q, t ^ d, piece)
        h = q // 2
        if q % 2 == 0:
            for d in partners:
                source = t ^ d

                @pl.when((source == 1) | (source == 2))
                def _():
                    straddle(h, d, source).wait_recv()
        both = sprecv[h, 0].astype(jnp.float32) + sprecv[h, 1].astype(jnp.float32)
        at = q % 2 * 8
        place(2 * blocks, both[at:at + 8])

    def core_stage(q):
        to_core(q).wait()
        for s in range(2):
            summed[q, s] = part[q, c, s] + corebuf[q, s]

            @pl.when(z != ZSETS[q % 2][s])
            def _():
                to_z(q, s, z).start()

    def z_stage(q):
        for s in range(2):
            home = ZSETS[q % 2][s]

            @pl.when(z == home)
            def _():
                total = summed[q, s]
                for other in range(NZ):
                    if other != home:
                        to_z(q, s, other).wait_recv()
                        total = total + zbuf[q, other]
                gath[t, q // 2] = total
                for d in partners:
                    to_tm(q // 2, d, t).start()

    def finish(k):
        for d in partners:
            to_tm(k, d, t ^ d).wait_recv()

        def one(s, carry):
            ordered = gath[s, k]
            fill = jnp.zeros((LANES - SLOTS, LANES), jnp.float32)
            mirrored = jnp.concatenate([ordered, fill], axis=0).T[:SLOTS]
            out_ref[s * 2 + k, 0] = 0.5 * (ordered + mirrored)
            out_ref[s * 2 + k, 1] = 0.5 * (ordered - mirrored)
            return carry

        lax.fori_loop(0, NT, one, 0)

    for q in range(QUARTERS):
        if 0 < q < QUARTERS - 1:
            for piece in range(3):
                send(q + 1, piece)
        receive(q)
        for j in (0, 2, 1, 3):
            gram(q, j)
        to_core(q).start()
        if q >= 1:
            z_stage(q - 1)
        core_stage(q)
    z_stage(QUARTERS - 1)
    finish(0)
    finish(1)

    halo_copy(halo_to).wait_send()
    for q in range(QUARTERS):
        for piece in range(3):
            for d in partners:
                exchange(q, piece, d, t).wait_send()
        for s in range(2):
            @pl.when(z != ZSETS[q % 2][s])
            def _():
                to_z(q, s, z).wait_send()
    for k in range(2):
        for d in partners:
            to_tm(k, d, t).wait_send()

    @pl.when(middle)
    def _():
        for h in range(2):
            for d in partners:
                straddle(h, d, t).wait_send()


def fused(codes, scales, weights, freq_indices, total_points):
    rows, points = codes.shape
    blocks = rows // HOP
    pairs = blocks // 2
    f32, bf16 = jnp.float32, jnp.bfloat16
    dma = pltpu.SemaphoreType.DMA
    hbm = pl.BlockSpec(memory_space=pl.ANY)
    full = pl.pallas_call(
        functools.partial(kernel, total_points),
        out_shape=jax.ShapeDtypeStruct((2 * NT, 2, SLOTS, LANES), f32),
        in_specs=[hbm, hbm, hbm, pl.BlockSpec(memory_space=pltpu.SMEM)],
        out_specs=pl.BlockSpec(memory_space=pltpu.VMEM),
        scratch_shapes=[
            pltpu.VMEM((rows, points), bf16),
            pltpu.VMEM((rows,), f32),
            pltpu.VMEM((points,), f32),
            pltpu.VMEM((rows, LANES), f32),
            pltpu.VMEM((rows + HALF, points), bf16),
            pltpu.VMEM((2 * NT * QUARTERS * 4, NFFT), bf16),
            pltpu.VMEM((QUARTERS, NT, pairs, 16, points), bf16),
            pltpu.VMEM((QUARTERS, NT, pairs, 16, points), bf16),
            pltpu.VMEM((2, NT, 16, points), bf16),
            pltpu.VMEM((2, 2, 16, points), bf16),
            pltpu.VMEM((points // LANES, 8 * SLOTS, LANES), f32),
            pltpu.VMEM((QUARTERS, 2, 2, SLOTS, LANES), f32),
            pltpu.VMEM((QUARTERS, 2, SLOTS, LANES), f32),
            pltpu.VMEM((QUARTERS, 2, SLOTS, LANES), f32),
            pltpu.VMEM((QUARTERS, NZ, SLOTS, LANES), f32),
            pltpu.VMEM((NT, 2, SLOTS, LANES), f32),
            dma((5,)),
            dma, dma,
            dma((QUARTERS, 3, NT - 1)), dma((QUARTERS, 3, NT - 1)),
            dma((2, NT - 1)), dma((2, NT - 1)),
            dma((QUARTERS,)), dma((QUARTERS,)),
            dma((QUARTERS, 2)), dma((QUARTERS, NZ)),
            dma((2, NT - 1)), dma((2, NT - 1)),
        ],
        compiler_params=pltpu.CompilerParams(
            collective_id=0, has_side_effects=True, vmem_limit_bytes=52 * 2**20
        ),
        name="spectra_cross",
    )(codes, scales, weights, freq_indices)
    count = rows * NT // HOP - 1
    return full[:, :, :count, :count]


def cross_matrices(stacked):
    blocks = stacked.shape[1] // 2
    products = jnp.einsum("fip,fjp->fij", stacked, stacked, preferred_element_type=jnp.float32)
    matrix_re = products[:, :blocks, :blocks] + products[:, blocks:, blocks:]
    matrix_im = products[:, :blocks, blocks:] - products[:, blocks:, :blocks]
    return jnp.stack([matrix_re, matrix_im], axis=1)


def general(codes, scales, weights, freq_indices):
    values = (codes.astype(jnp.float32) * scales[:, None]).astype(jnp.bfloat16)
    regrouped = lax.all_to_all(values, "tm", split_axis=1, concat_axis=0, tiled=True)
    point_count = regrouped.shape[1]
    own_weights = lax.dynamic_slice_in_dim(
        weights, lax.axis_index("tm") * point_count, point_count, 0
    )
    total_points = weights.shape[0] * lax.axis_size("pts")
    root_weight = jnp.sqrt(own_weights / total_points)
    cosine_table, sine_table = make_tables(freq_indices)
    hop_rows = regrouped.reshape(-1, NFFT // 2, point_count)
    windows = jnp.concatenate([hop_rows[:-1], hop_rows[1:]], axis=1)
    real_part = jnp.einsum("fn,bnp->fbp", cosine_table, windows, preferred_element_type=jnp.float32)
    imag_part = jnp.einsum("fn,bnp->fbp", sine_table, windows, preferred_element_type=jnp.float32)
    scaled_re = (real_part * root_weight[None, None, :]).astype(jnp.bfloat16)
    scaled_im = (imag_part * root_weight[None, None, :]).astype(jnp.bfloat16)
    stacked = jnp.concatenate([scaled_re, scaled_im], axis=1)
    partial_value = lax.psum_scatter(
        cross_matrices(stacked), "pts", scatter_dimension=0, tiled=True
    )
    return lax.psum(partial_value, "tm")


def solution(mesh):
    nt, np_ = mesh.shape["tm"], mesh.shape["pts"]

    def per_device(codes, scales, weights, freq_indices):
        rows, points = codes.shape
        fits = (
            nt == NT
            and np_ == 2 * NZ
            and freq_indices.shape[0] == 2 * nt * np_
            and points % LANES == 0
            and rows % NFFT == HALF
            and rows >= 16 * HOP
            and 4 * (rows // HOP) + 1 <= SLOTS
        )
        if fits:
            return fused(codes, scales, weights, freq_indices, points * np_)
        return general(codes, scales, weights, freq_indices)

    return jax.shard_map(
        per_device,
        mesh=mesh,
        in_specs=(P("tm", "pts"), P("tm"), P("pts"), P()),
        out_specs=P("pts", None, None, None),
        check_vma=False,
    )
```

```python
import functools
import math

import jax
import jax.numpy as jnp
from jax import lax
from jax.experimental import pallas as pl
from jax.experimental.pallas import tpu as pltpu
from jax.sharding import PartitionSpec as P

NFFT = 256
HOP = NFFT // 2
HALF = HOP // 2
LANES = 128
SLOTS = 96
NT = 4
NZ = 4
QUARTERS = 4
PIECES = 2
ZSETS = ((0, 3), (1, 2))
MESH = pl.DeviceIdType.MESH


def make_tables(freq_indices):
    sample = jnp.arange(NFFT, dtype=jnp.int32)
    phases = freq_indices[:, None] * sample[None, :] % NFFT
    angles = phases.astype(jnp.float32) * (2.0 * math.pi / NFFT)
    hann_window = 0.5 - 0.5 * jnp.cos(sample.astype(jnp.float32) * (2.0 * math.pi / NFFT))
    cosine_table = (0.25 * hann_window[None, :] * jnp.cos(angles)).astype(jnp.bfloat16)
    sine_table = (-0.25 * hann_window[None, :] * jnp.sin(angles)).astype(jnp.bfloat16)
    return (cosine_table, sine_table)


def turn_waves(turn):
    angle = turn.astype(jnp.float32) * (2.0 * math.pi / NFFT)
    quarter = (turn + NFFT // 8) // (NFFT // 4)
    count = quarter.astype(jnp.float32)
    x = ((angle - count * 1.5703125) - count * 4.837512969970703125e-4) - count * 7.549789948768648e-8
    y = x * x
    sine = x + x * y * (-1.0 / 6.0 + y * (1.0 / 120.0 + y * (-1.0 / 5040.0 + y * (1.0 / 362880.0))))
    cosine = 1.0 + y * (-0.5 + y * (1.0 / 24.0 + y * (-1.0 / 720.0 + y * (1.0 / 40320.0))))
    swap = quarter % 2 == 1
    low = jnp.where(swap, sine, cosine)
    high = jnp.where(swap, cosine, sine)
    return (
        jnp.where((quarter + 1) % 4 >= 2, -low, low),
        jnp.where(quarter % 4 >= 2, -high, high),
    )


def kernel(
    total_points,
    codes_hbm, scales_hbm, weights_hbm, freq_hbm, out_ref,
    codes_ref, scales_v, weights_v, freq_ref, spread, vals, table, sbuf, rbuf, spbuf, sprecv, stage,
    part, corebuf, summed, zbuf, gath,
    load_s, halo_s, halo_r, tm_s, tm_r, sp_s, sp_r, core_s, core_r, z_s, z_r, g_s, g_r,
):
    rows, points = codes_ref.shape
    t = lax.axis_index("tm")
    p = lax.axis_index("pts")
    z = p // 2
    c = p % 2
    odd = t % 2
    partner = p + 1 - 2 * c
    lane_tiles = points // LANES
    blocks = rows // HOP
    pairs = blocks // 2
    padded = rows + HALF

    early = (10 * HOP)
    late = rows - early - HALF
    edge_at = (1 - odd) * (rows - HALF)
    early_at = odd * (rows - early)
    late_at = odd * HALF + (1 - odd) * early

    def load(at, count, sem):
        at = pl.ds(pl.multiple_of(at, HALF), count)
        return pltpu.make_async_copy(codes_hbm.at[at], codes_ref.at[at], load_s.at[sem])

    load_scales = pltpu.make_async_copy(scales_hbm, scales_v, load_s.at[3])
    load_weights = pltpu.make_async_copy(weights_hbm, weights_v, load_s.at[4])
    load_freq = pltpu.make_async_copy(freq_hbm, freq_ref, load_s.at[5])
    load_edge = load(edge_at, HALF, 0)
    load_early = load(early_at, early, 1)
    load_late = load(late_at, late, 2)
    barrier = pltpu.get_barrier_semaphore()
    for d in range(1, NT):
        pl.semaphore_signal(barrier, inc=1, device_id=(t ^ d, p), device_id_type=MESH)
    pl.semaphore_signal(barrier, inc=1, device_id=(t, partner), device_id_type=MESH)
    for d in range(1, NZ):
        pl.semaphore_signal(barrier, inc=1, device_id=(t, (z + d) % NZ * 2 + c), device_id_type=MESH)
    load_freq.start()
    load_scales.start()
    load_edge.start()
    load_early.start()
    load_weights.start()
    load_late.start()

    sample = lax.broadcasted_iota(jnp.int32, (8, NFFT), 1)
    sub = lax.broadcasted_iota(jnp.int32, (8, NFFT), 0)
    window_shape = 0.25 * (0.5 - 0.5 * turn_waves(sample)[0])

    def octet_table(dest, q):
        bins = jnp.zeros((8, NFFT), jnp.int32)
        for j in range(4):
            dest_p = ZSETS[q % 2][j // 2] * 2 + j % 2
            bins = jnp.where(sub // 2 == j, freq_ref[dest_p * 2 * NT + dest * 2 + q // 2], bins)
        cosine, sine = turn_waves(bins * sample % NFFT)
        return window_shape * jnp.where(sub % 2 == 0, cosine, -sine)

    load_freq.wait()
    for dest in range(NT):
        for half in range(2):
            at = dest * 32 + half * 16
            pair = [octet_table(dest, 2 * half), octet_table(dest, 2 * half + 1)]
            table[at:at + 16, :] = jnp.concatenate(pair, axis=0).astype(jnp.bfloat16)

    load_scales.wait()
    for g in range(-(-rows // HOP)):
        size = min(HOP, rows - g * HOP)
        line = scales_v[g * HOP:g * HOP + size].reshape(1, size)
        spread[g * HOP:g * HOP + size, :] = jnp.broadcast_to(line, (LANES, size)).T

    offset = odd * HALF

    def dequantize(i, carry):
        at = pl.ds(pl.multiple_of(i * HALF, HALF), HALF)
        to = pl.ds(pl.multiple_of(i * HALF + offset, HALF), HALF)
        scale = spread[at, :]
        for lane in range(lane_tiles):
            cols = slice(lane * LANES, (lane + 1) * LANES)
            vals[to, cols] = (codes_ref[at, cols].astype(jnp.float32) * scale).astype(jnp.bfloat16)
        return carry

    load_edge.wait()
    dequantize(edge_at // HALF, 0)
    halo_from = (1 - odd) * (rows - HALF) + odd * HALF
    halo_to = odd * rows
    halo_mine = (1 - odd) * rows

    def halo_copy(dst):
        return pltpu.make_async_remote_copy(
            src_ref=vals.at[pl.ds(pl.multiple_of(halo_from, HALF), HALF)],
            dst_ref=vals.at[pl.ds(pl.multiple_of(dst, HALF), HALF)],
            send_sem=halo_s, recv_sem=halo_r,
            device_id=(t ^ 1, p), device_id_type=MESH,
        )

    pl.semaphore_wait(barrier, NT + NZ - 1)
    halo_copy(halo_to).start()

    load_early.wait()
    lax.fori_loop(early_at // HALF, (early_at + early) // HALF, dequantize, 0)
    load_weights.wait()
    root_weight = jnp.sqrt(weights_v[...].reshape(1, points) / total_points)

    def spectrum(i):
        window = vals[pl.ds(pl.multiple_of(i * HOP, HOP), NFFT), :]
        return jnp.dot(table[...], window, preferred_element_type=jnp.float32) * root_weight

    def spectra(j, carry):
        jj = odd * (pairs - 1 - j) + (1 - odd) * j
        first = spectrum(2 * jj)
        second = spectrum(2 * jj + 1)
        for dest in range(NT):
            for q in range(QUARTERS):
                at = slice(dest * 32 + q * 8, dest * 32 + q * 8 + 8)
                both = jnp.concatenate([first[at], second[at]], axis=0)
                sbuf[q, dest, jj] = both.astype(jnp.bfloat16)
        return carry

    cuts = (0, 4, pairs - 1, pairs)
    partners = (3, 1, 2)

    def tiles_of(who, piece):
        count = cuts[piece + 1] - cuts[piece]
        flip = who % 2
        return flip * (pairs - cuts[piece + 1]) + (1 - flip) * cuts[piece], count

    def exchange(q, piece, d, source):
        at, count = tiles_of(source, piece)
        return pltpu.make_async_remote_copy(
            src_ref=sbuf.at[q, t ^ d, pl.ds(at, count)],
            dst_ref=rbuf.at[q, source, pl.ds(at, count)],
            send_sem=tm_s.at[q, piece, d - 1], recv_sem=tm_r.at[q, piece, d - 1],
            device_id=(t ^ d, p), device_id_type=MESH,
        )

    def straddle(h, d, source):
        return pltpu.make_async_remote_copy(
            src_ref=spbuf.at[h, t ^ d],
            dst_ref=sprecv.at[h, source - 1],
            send_sem=sp_s.at[h, d - 1], recv_sem=sp_r.at[h, d - 1],
            device_id=(t ^ d, p), device_id_type=MESH,
        )

    middle = (t == 1) | (t == 2)

    def send_straddle(h):
        @pl.when(middle)
        def _():
            for d in partners:
                straddle(h, d, t).start()

    def send(q, piece):
        for d in partners:
            exchange(q, piece, d, t).start()

    lax.fori_loop(cuts[0], cuts[1], spectra, 0)
    send(0, 0)
    load_late.wait()
    lax.fori_loop(late_at // HALF, (late_at + late) // HALF, dequantize, 0)
    lax.fori_loop(cuts[1], cuts[2], spectra, 0)
    send(0, 1)
    halo_copy(halo_mine).wait_recv()
    lax.fori_loop(cuts[2], cuts[3], spectra, 0)
    send(0, 2)

    @pl.when(middle)
    def _():
        hop = pl.ds(pl.multiple_of(odd * (padded - HOP), HOP), HOP)
        side = jnp.where(odd == 1, table[:, :HOP].astype(jnp.float32), table[:, HOP:].astype(jnp.float32))
        result = jnp.dot(side.astype(jnp.bfloat16), vals[hop, :], preferred_element_type=jnp.float32)
        result = (result * root_weight).astype(jnp.bfloat16)
        for dest in range(NT):
            for h in range(2):
                spbuf[h, dest] = result[dest * 32 + h * 16:dest * 32 + h * 16 + 16]
        for h in range(2):
            sprecv[h, t - 1] = spbuf[h, t]

    for h in range(2):
        send_straddle(h)
    for piece in range(3):
        send(1, piece)

    for lane in range(lane_tiles):
        for s in range(8):
            stage[lane, s * SLOTS + SLOTS - 8:(s + 1) * SLOTS, :] = jnp.zeros((8, LANES), jnp.float32)

    def place(b, octet):
        for lane in range(lane_tiles):
            stage[lane, pl.ds(b, 8, stride=SLOTS), :] = octet[:, lane * LANES:(lane + 1) * LANES]

    def unpack(source_ref, q, who, piece):
        at, count = tiles_of(who, piece)
        base = who * blocks + who // 2

        def one(i, carry):
            tile = source_ref[q, who, i].astype(jnp.float32)
            place(base + 2 * i, tile[:8])
            place(base + 2 * i + 1, tile[8:])
            return carry

        lax.fori_loop(at, at + count, one, 0)

    def gram(q, s, side):
        j = s * 2 + side
        at = pl.ds(pl.multiple_of(j * 2 * SLOTS, 2 * SLOTS), 2 * SLOTS)
        stacked = jnp.concatenate(
            [stage[lane, at, :].astype(jnp.bfloat16) for lane in range(lane_tiles)], axis=1
        )
        fill = jnp.zeros((LANES - SLOTS, points), jnp.bfloat16)
        wide = jnp.concatenate([stacked[:SLOTS], fill, stacked[SLOTS:], fill], axis=0)
        prod = lax.dot_general(
            stacked, wide, (((1,), (1,)), ((), ())), preferred_element_type=jnp.float32
        )
        real = prod[:SLOTS, :LANES] + prod[SLOTS:, LANES:]
        imag = prod[:SLOTS, LANES:] - prod[SLOTS:, :LANES]
        part[q, side, s] = real + imag

    def rows_of(h):
        return pl.ds(h * SLOTS // PIECES, SLOTS // PIECES)

    def to_core(q, h):
        return pltpu.make_async_remote_copy(
            src_ref=part.at[q, 1 - c, :, rows_of(h)], dst_ref=corebuf.at[q, :, rows_of(h)],
            send_sem=core_s.at[q, h], recv_sem=core_r.at[q, h],
            device_id=(t, partner), device_id_type=MESH,
        )

    def to_z(q, s, h, source):
        return pltpu.make_async_remote_copy(
            src_ref=summed.at[q, s, rows_of(h)], dst_ref=zbuf.at[q, source, rows_of(h)],
            send_sem=z_s.at[q, s, h], recv_sem=z_r.at[q, source, h],
            device_id=(t, ZSETS[q % 2][s] * 2 + c), device_id_type=MESH,
        )

    def to_tm(k, h, d, source):
        return pltpu.make_async_remote_copy(
            src_ref=gath.at[source, k, rows_of(h)], dst_ref=gath.at[source, k, rows_of(h)],
            send_sem=g_s.at[k, h, d - 1], recv_sem=g_r.at[k, h, d - 1],
            device_id=(t ^ d, p), device_id_type=MESH,
        )

    def receive(q, pieces):
        for piece in pieces:
            for d in partners:
                exchange(q, piece, d, t ^ d).wait_recv()
                unpack(rbuf, q, t ^ d, piece)

    def own(q):
        for piece in range(3):
            unpack(sbuf, q, t, piece)

    def straddling(q):
        if q % 2 == 0:
            for d in partners:
                source = t ^ d

                @pl.when((source == 1) | (source == 2))
                def _():
                    straddle(q // 2, d, source).wait_recv()
        both = sprecv[q // 2, 0].astype(jnp.float32) + sprecv[q // 2, 1].astype(jnp.float32)
        at = q % 2 * 8
        place(2 * blocks, both[at:at + 8])

    def core_stage(q, h):
        to_core(q, h).wait()
        for s in range(2):
            at = rows_of(h)
            summed[q, s, at] = part[q, c, s, at] + corebuf[q, s, at]

            @pl.when(z != ZSETS[q % 2][s])
            def _():
                to_z(q, s, h, z).start()

    def at_home(q):
        return (z == ZSETS[q % 2][0]) | (z == ZSETS[q % 2][1])

    def z_stage(q, h):
        for s in range(2):
            home = ZSETS[q % 2][s]

            @pl.when(z == home)
            def _():
                at = rows_of(h)
                total = summed[q, s, at]
                for other in range(NZ):
                    if other != home:
                        to_z(q, s, h, other).wait_recv()
                        total = total + zbuf[q, other, at]
                gath[t, q // 2, at] = total

    def spread_result(q, h):
        @pl.when(at_home(q))
        def _():
            for d in partners:
                to_tm(q // 2, h, d, t).start()

    for q in range(QUARTERS):
        last = q == QUARTERS - 1
        if 0 < q < QUARTERS - 1:
            for piece in range(3):
                send(q + 1, piece)
        own(q)
        receive(q, (0,))
        straddling(q)
        if q >= 1:
            for h in range(PIECES):
                z_stage(q - 1, h)
        receive(q, (1, 2))
        if last:
            for early_q in range(QUARTERS - 1):
                for h in range(PIECES):
                    spread_result(early_q, h)
        for s in range(2):
            gram(q, s, 1 - c)
        for h in range(PIECES):
            to_core(q, h).start()
        for s in range(2):
            gram(q, s, c)
        for h in range(PIECES):
            core_stage(q, h)
    for h in range(PIECES):
        z_stage(QUARTERS - 1, h)
        spread_result(QUARTERS - 1, h)

    for k in range(2):
        for h in range(PIECES):
            for d in partners:
                to_tm(k, h, d, t ^ d).wait_recv()
        for s in range(NT):
            out_ref[s * 2 + k] = gath[s, k]

    halo_copy(halo_to).wait_send()
    for q in range(QUARTERS):
        for piece in range(3):
            for d in partners:
                exchange(q, piece, d, t).wait_send()
        for s in range(2):
            @pl.when(z != ZSETS[q % 2][s])
            def _():
                for h in range(PIECES):
                    to_z(q, s, h, z).wait_send()
    for k in range(2):
        for h in range(PIECES):
            for d in partners:
                to_tm(k, h, d, t).wait_send()

    @pl.when(middle)
    def _():
        for h in range(2):
            for d in partners:
                straddle(h, d, t).wait_send()


def finish(sums_ref, out_hbm, both, sems):
    freqs = sums_ref.shape[0]
    count = out_hbm.shape[1]

    def copy(part):
        size = freqs // 2 * 2 * count
        at = pl.ds(part * size, size)
        return pltpu.make_async_copy(both.at[at], out_hbm.at[at], sems.at[part])

    for part in range(2):
        for f in range(part * freqs // 2, (part + 1) * freqs // 2):
            ordered = sums_ref[f]
            fill = jnp.zeros((LANES - SLOTS, LANES), jnp.float32)
            mirrored = jnp.concatenate([ordered, fill], axis=0).T[:SLOTS]
            first = f * 2 * count
            both[pl.ds(first, count, stride=2), :] = 0.5 * (ordered + mirrored)[:count, :count]
            both[pl.ds(first + 1, count, stride=2), :] = 0.5 * (ordered - mirrored)[:count, :count]
        copy(part).start()
    for part in range(2):
        copy(part).wait()


def fused(codes, scales, weights, freq_indices, total_points):
    rows, points = codes.shape
    blocks = rows // HOP
    pairs = blocks // 2
    count = rows * NT // HOP - 1
    f32, bf16 = jnp.float32, jnp.bfloat16
    dma = pltpu.SemaphoreType.DMA
    hbm = pl.BlockSpec(memory_space=pltpu.HBM)
    vmem = pl.BlockSpec(memory_space=pltpu.VMEM)
    sums = pl.pallas_call(
        functools.partial(kernel, total_points),
        out_shape=jax.ShapeDtypeStruct((2 * NT, SLOTS, LANES), f32),
        in_specs=[hbm, hbm, hbm, hbm],
        out_specs=vmem,
        scratch_shapes=[
            pltpu.VMEM((rows, points), bf16),
            pltpu.VMEM((rows,), f32),
            pltpu.VMEM((points,), f32),
            pltpu.SMEM(freq_indices.shape, jnp.int32),
            pltpu.VMEM((rows, LANES), f32),
            pltpu.VMEM((rows + HALF, points), bf16),
            pltpu.VMEM((2 * NT * QUARTERS * 4, NFFT), bf16),
            pltpu.VMEM((QUARTERS, NT, pairs, 16, points), bf16),
            pltpu.VMEM((QUARTERS, NT, pairs, 16, points), bf16),
            pltpu.VMEM((2, NT, 16, points), bf16),
            pltpu.VMEM((2, 2, 16, points), bf16),
            pltpu.VMEM((points // LANES, 8 * SLOTS, LANES), f32),
            pltpu.VMEM((QUARTERS, 2, 2, SLOTS, LANES), f32),
            pltpu.VMEM((QUARTERS, 2, SLOTS, LANES), f32),
            pltpu.VMEM((QUARTERS, 2, SLOTS, LANES), f32),
            pltpu.VMEM((QUARTERS, NZ, SLOTS, LANES), f32),
            pltpu.VMEM((NT, 2, SLOTS, LANES), f32),
            dma((6,)),
            dma, dma,
            dma((QUARTERS, 3, NT - 1)), dma((QUARTERS, 3, NT - 1)),
            dma((2, NT - 1)), dma((2, NT - 1)),
            dma((QUARTERS, PIECES)), dma((QUARTERS, PIECES)),
            dma((QUARTERS, 2, PIECES)), dma((QUARTERS, NZ, PIECES)),
            dma((2, PIECES, NT - 1)), dma((2, PIECES, NT - 1)),
        ],
        compiler_params=pltpu.CompilerParams(
            collective_id=0, has_side_effects=True, vmem_limit_bytes=56 * 2**20
        ),
        name="spectra_cross",
    )(codes, scales, weights, freq_indices)
    full = pl.pallas_call(
        finish,
        out_shape=jax.ShapeDtypeStruct((2 * NT * 2 * count, count), f32),
        in_specs=[vmem],
        out_specs=hbm,
        scratch_shapes=[pltpu.VMEM((2 * NT * 2 * count, count), f32), dma((2,))],
        name="hermitian_parts",
    )(sums)
    return full.reshape(2 * NT, count, 2, count).transpose(0, 2, 1, 3)


def cross_matrices(stacked):
    blocks = stacked.shape[1] // 2
    products = jnp.einsum("fip,fjp->fij", stacked, stacked, preferred_element_type=jnp.float32)
    matrix_re = products[:, :blocks, :blocks] + products[:, blocks:, blocks:]
    matrix_im = products[:, :blocks, blocks:] - products[:, blocks:, :blocks]
    return jnp.stack([matrix_re, matrix_im], axis=1)


def general(codes, scales, weights, freq_indices):
    values = (codes.astype(jnp.float32) * scales[:, None]).astype(jnp.bfloat16)
    regrouped = lax.all_to_all(values, "tm", split_axis=1, concat_axis=0, tiled=True)
    point_count = regrouped.shape[1]
    own_weights = lax.dynamic_slice_in_dim(
        weights, lax.axis_index("tm") * point_count, point_count, 0
    )
    total_points = weights.shape[0] * lax.axis_size("pts")
    root_weight = jnp.sqrt(own_weights / total_points)
    cosine_table, sine_table = make_tables(freq_indices)
    hop_rows = regrouped.reshape(-1, NFFT // 2, point_count)
    windows = jnp.concatenate([hop_rows[:-1], hop_rows[1:]], axis=1)
    real_part = jnp.einsum("fn,bnp->fbp", cosine_table, windows, preferred_element_type=jnp.float32)
    imag_part = jnp.einsum("fn,bnp->fbp", sine_table, windows, preferred_element_type=jnp.float32)
    scaled_re = (real_part * root_weight[None, None, :]).astype(jnp.bfloat16)
    scaled_im = (imag_part * root_weight[None, None, :]).astype(jnp.bfloat16)
    stacked = jnp.concatenate([scaled_re, scaled_im], axis=1)
    partial_value = lax.psum_scatter(
        cross_matrices(stacked), "pts", scatter_dimension=0, tiled=True
    )
    return lax.psum(partial_value, "tm")


def solution(mesh):
    nt, np_ = mesh.shape["tm"], mesh.shape["pts"]

    def per_device(codes, scales, weights, freq_indices):
        rows, points = codes.shape
        fits = (
            nt == NT
            and np_ == 2 * NZ
            and freq_indices.shape[0] == 2 * nt * np_
            and points % LANES == 0
            and rows % NFFT == HALF
            and rows >= 16 * HOP
            and 4 * (rows // HOP) + 1 <= SLOTS
        )
        if fits:
            return fused(codes, scales, weights, freq_indices, points * np_)
        return general(codes, scales, weights, freq_indices)

    return jax.shard_map(
        per_device,
        mesh=mesh,
        in_specs=(P("tm", "pts"), P("tm"), P("pts"), P()),
        out_specs=P("pts", None, None, None),
        check_vma=False,
    )
```

```python
import functools
import math

import jax
import jax.numpy as jnp
from jax import lax
from jax.experimental import pallas as pl
from jax.experimental.pallas import tpu as pltpu
from jax.sharding import PartitionSpec as P

NFFT = 256
HOP = NFFT // 2
HALF = HOP // 2
LANES = 128
SLOTS = 96
NT = 4
NZ = 4
QUARTERS = 4
PIECES = 2
ZSETS = ((0, 3), (1, 2))
MESH = pl.DeviceIdType.MESH


def make_tables(freq_indices):
    sample = jnp.arange(NFFT, dtype=jnp.int32)
    phases = freq_indices[:, None] * sample[None, :] % NFFT
    angles = phases.astype(jnp.float32) * (2.0 * math.pi / NFFT)
    hann_window = 0.5 - 0.5 * jnp.cos(sample.astype(jnp.float32) * (2.0 * math.pi / NFFT))
    cosine_table = (0.25 * hann_window[None, :] * jnp.cos(angles)).astype(jnp.bfloat16)
    sine_table = (-0.25 * hann_window[None, :] * jnp.sin(angles)).astype(jnp.bfloat16)
    return (cosine_table, sine_table)


def turn_waves(turn):
    angle = turn.astype(jnp.float32) * (2.0 * math.pi / NFFT)
    quarter = (turn + NFFT // 8) // (NFFT // 4)
    count = quarter.astype(jnp.float32)
    x = ((angle - count * 1.5703125) - count * 4.837512969970703125e-4) - count * 7.549789948768648e-8
    y = x * x
    sine = x + x * y * (-1.0 / 6.0 + y * (1.0 / 120.0 + y * (-1.0 / 5040.0 + y * (1.0 / 362880.0))))
    cosine = 1.0 + y * (-0.5 + y * (1.0 / 24.0 + y * (-1.0 / 720.0 + y * (1.0 / 40320.0))))
    swap = quarter % 2 == 1
    low = jnp.where(swap, sine, cosine)
    high = jnp.where(swap, cosine, sine)
    return (
        jnp.where((quarter + 1) % 4 >= 2, -low, low),
        jnp.where(quarter % 4 >= 2, -high, high),
    )


def kernel(
    total_points,
    codes_hbm, scales_hbm, weights_hbm, freq_hbm, out_ref,
    codes_ref, scales_v, weights_v, freq_ref, spread, vals, table, sbuf, rbuf, hops, spbuf, sprecv, stage,
    part, corebuf, summed, zbuf, gath,
    load_s, halo_s, halo_r, tm_s, tm_r, hop_s, hop_r, sp_s, sp_r, core_s, core_r, z_s, z_r, g_s, g_r,
):
    rows, points = codes_ref.shape
    t = lax.axis_index("tm")
    p = lax.axis_index("pts")
    z = p // 2
    c = p % 2
    odd = t % 2
    partner = p + 1 - 2 * c
    lane_tiles = points // LANES
    blocks = rows // HOP
    pairs = blocks // 2
    padded = rows + HALF

    early = (10 * HOP)
    late = rows - early - HALF
    edge_at = (1 - odd) * (rows - HALF)
    early_at = odd * (rows - early)
    late_at = odd * HALF + (1 - odd) * early

    def load(at, count, sem):
        at = pl.ds(pl.multiple_of(at, HALF), count)
        return pltpu.make_async_copy(codes_hbm.at[at], codes_ref.at[at], load_s.at[sem])

    load_scales = pltpu.make_async_copy(scales_hbm, scales_v, load_s.at[3])
    load_weights = pltpu.make_async_copy(weights_hbm, weights_v, load_s.at[4])
    load_freq = pltpu.make_async_copy(freq_hbm, freq_ref, load_s.at[5])
    load_edge = load(edge_at, HALF, 0)
    load_early = load(early_at, early, 1)
    load_late = load(late_at, late, 2)
    barrier = pltpu.get_barrier_semaphore()
    for d in range(1, NT):
        pl.semaphore_signal(barrier, inc=1, device_id=(t ^ d, p), device_id_type=MESH)
    pl.semaphore_signal(barrier, inc=1, device_id=(t, partner), device_id_type=MESH)
    for d in range(1, NZ):
        pl.semaphore_signal(barrier, inc=1, device_id=(t, (z + d) % NZ * 2 + c), device_id_type=MESH)
    load_freq.start()
    load_scales.start()
    load_edge.start()
    load_early.start()
    load_weights.start()
    load_late.start()

    sample = lax.broadcasted_iota(jnp.int32, (8, NFFT), 1)
    sub = lax.broadcasted_iota(jnp.int32, (8, NFFT), 0)
    window_shape = 0.25 * (0.5 - 0.5 * turn_waves(sample)[0])

    def octet_table(dest, q):
        bins = jnp.zeros((8, NFFT), jnp.int32)
        for j in range(4):
            dest_p = ZSETS[q % 2][j // 2] * 2 + j % 2
            bins = jnp.where(sub // 2 == j, freq_ref[dest_p * 2 * NT + dest * 2 + q // 2], bins)
        cosine, sine = turn_waves(bins * sample % NFFT)
        return window_shape * jnp.where(sub % 2 == 0, cosine, -sine)

    load_freq.wait()
    for dest in range(NT):
        for half in range(2):
            at = dest * 32 + half * 16
            pair = [octet_table(dest, 2 * half), octet_table(dest, 2 * half + 1)]
            table[at:at + 16, :] = jnp.concatenate(pair, axis=0).astype(jnp.bfloat16)

    load_scales.wait()
    for g in range(-(-rows // HOP)):
        size = min(HOP, rows - g * HOP)
        line = scales_v[g * HOP:g * HOP + size].reshape(1, size)
        spread[g * HOP:g * HOP + size, :] = jnp.broadcast_to(line, (LANES, size)).T

    offset = odd * HALF

    def dequantize(i, carry):
        at = pl.ds(pl.multiple_of(i * HALF, HALF), HALF)
        to = pl.ds(pl.multiple_of(i * HALF + offset, HALF), HALF)
        scale = spread[at, :]
        for lane in range(lane_tiles):
            cols = slice(lane * LANES, (lane + 1) * LANES)
            vals[to, cols] = (codes_ref[at, cols].astype(jnp.float32) * scale).astype(jnp.bfloat16)
        return carry

    load_edge.wait()
    dequantize(edge_at // HALF, 0)
    halo_from = (1 - odd) * (rows - HALF) + odd * HALF
    halo_to = odd * rows
    halo_mine = (1 - odd) * rows

    def halo_copy(dst):
        return pltpu.make_async_remote_copy(
            src_ref=vals.at[pl.ds(pl.multiple_of(halo_from, HALF), HALF)],
            dst_ref=vals.at[pl.ds(pl.multiple_of(dst, HALF), HALF)],
            send_sem=halo_s, recv_sem=halo_r,
            device_id=(t ^ 1, p), device_id_type=MESH,
        )

    pl.semaphore_wait(barrier, NT + NZ - 1)
    halo_copy(halo_to).start()

    load_early.wait()
    lax.fori_loop(early_at // HALF, (early_at + early) // HALF, dequantize, 0)
    load_weights.wait()
    root_weight = jnp.sqrt(weights_v[...].reshape(1, points) / total_points)

    def spectrum(i):
        window = vals[pl.ds(pl.multiple_of(i * HOP, HOP), NFFT), :]
        return jnp.dot(table[...], window, preferred_element_type=jnp.float32) * root_weight

    def spectra(j, carry):
        jj = odd * (pairs - 1 - j) + (1 - odd) * j
        first = spectrum(2 * jj)
        second = spectrum(2 * jj + 1)
        for dest in range(NT):
            for q in range(QUARTERS):
                at = slice(dest * 32 + q * 8, dest * 32 + q * 8 + 8)
                both = jnp.concatenate([first[at], second[at]], axis=0)
                sbuf[q, dest, jj] = both.astype(jnp.bfloat16)
        return carry

    cuts = (0, 4, pairs - 1, pairs)
    partners = (3, 1, 2)

    def tiles_of(who, piece):
        count = cuts[piece + 1] - cuts[piece]
        flip = who % 2
        return flip * (pairs - cuts[piece + 1]) + (1 - flip) * cuts[piece], count

    def exchange(q, piece, d, source):
        at, count = tiles_of(source, piece)
        return pltpu.make_async_remote_copy(
            src_ref=sbuf.at[q, t ^ d, pl.ds(at, count)],
            dst_ref=rbuf.at[q, source, pl.ds(at, count)],
            send_sem=tm_s.at[q, piece, d - 1], recv_sem=tm_r.at[q, piece, d - 1],
            device_id=(t ^ d, p), device_id_type=MESH,
        )

    middle = (t == 1) | (t == 2)
    outer = (t == 0) | (t == 3)

    def owner(lane):
        if 2 * lane + 1 == lane_tiles:
            return (NT - 1) * (1 - c)
        return (NT - 1) * int(2 * lane + 1 > lane_tiles)

    def lanes(lane):
        return pl.ds(lane * LANES, LANES)

    def hop_copy(lane, source, dest):
        return pltpu.make_async_remote_copy(
            src_ref=vals.at[pl.ds(pl.multiple_of(odd * (padded - HOP), HOP), HOP), lanes(lane)],
            dst_ref=hops.at[pl.ds(pl.multiple_of((source - 1) * HOP, HOP), HOP), lanes(lane)],
            send_sem=hop_s.at[lane], recv_sem=hop_r.at[source - 1, lane],
            device_id=(dest, p), device_id_type=MESH,
        )

    def straddle(lane, d):
        return pltpu.make_async_remote_copy(
            src_ref=spbuf.at[t ^ d, :, :, lanes(lane)],
            dst_ref=sprecv.at[:, :, lanes(lane)],
            send_sem=sp_s.at[lane, d - 1], recv_sem=sp_r.at[lane],
            device_id=(t ^ d, p), device_id_type=MESH,
        )

    def send(q, piece):
        for d in partners:
            exchange(q, piece, d, t).start()


    @pl.when(middle)
    def _():
        for lane in range(lane_tiles):
            hop_copy(lane, t, owner(lane)).start()

    lax.fori_loop(cuts[0], cuts[1], spectra, 0)
    send(0, 0)
    load_late.wait()
    lax.fori_loop(late_at // HALF, (late_at + late) // HALF, dequantize, 0)
    lax.fori_loop(cuts[1], cuts[2], spectra, 0)
    send(0, 1)
    halo_copy(halo_mine).wait_recv()
    lax.fori_loop(cuts[2], cuts[3], spectra, 0)
    send(0, 2)

    @pl.when(outer)
    def _():
        for lane in range(lane_tiles):
            @pl.when(t == owner(lane))
            def _():
                for source in (1, 2):
                    hop_copy(lane, source, owner(lane)).wait_recv()
        result = jnp.dot(table[...], hops[...], preferred_element_type=jnp.float32)
        result = (result * root_weight).astype(jnp.bfloat16)
        for dest in range(NT):
            for h in range(2):
                spbuf[dest, h] = result[dest * 32 + h * 16:dest * 32 + h * 16 + 16]
        for lane in range(lane_tiles):
            @pl.when(t == owner(lane))
            def _():
                for d in partners:
                    straddle(lane, d).start()
                sprecv[:, :, lanes(lane)] = spbuf[t, :, :, lanes(lane)]

    for piece in range(3):
        send(1, piece)

    for lane in range(lane_tiles):
        for s in range(8):
            stage[lane, s * SLOTS + SLOTS - 8:(s + 1) * SLOTS, :] = jnp.zeros((8, LANES), jnp.float32)

    def place(b, octet):
        for lane in range(lane_tiles):
            stage[lane, pl.ds(b, 8, stride=SLOTS), :] = octet[:, lane * LANES:(lane + 1) * LANES]

    def unpack(source_ref, q, who, piece):
        at, count = tiles_of(who, piece)
        base = who * blocks + who // 2

        def one(i, carry):
            tile = source_ref[q, who, i].astype(jnp.float32)
            place(base + 2 * i, tile[:8])
            place(base + 2 * i + 1, tile[8:])
            return carry

        lax.fori_loop(at, at + count, one, 0)

    def gram(q, s, side):
        j = s * 2 + side
        at = pl.ds(pl.multiple_of(j * 2 * SLOTS, 2 * SLOTS), 2 * SLOTS)
        stacked = jnp.concatenate(
            [stage[lane, at, :].astype(jnp.bfloat16) for lane in range(lane_tiles)], axis=1
        )
        fill = jnp.zeros((LANES - SLOTS, points), jnp.bfloat16)
        wide = jnp.concatenate([stacked[:SLOTS], fill, stacked[SLOTS:], fill], axis=0)
        prod = lax.dot_general(
            stacked, wide, (((1,), (1,)), ((), ())), preferred_element_type=jnp.float32
        )
        real = prod[:SLOTS, :LANES] + prod[SLOTS:, LANES:]
        imag = prod[:SLOTS, LANES:] - prod[SLOTS:, :LANES]
        part[q, side, s] = real + imag

    def rows_of(h):
        return pl.ds(h * SLOTS // PIECES, SLOTS // PIECES)

    def to_core(q, h):
        return pltpu.make_async_remote_copy(
            src_ref=part.at[q, 1 - c, :, rows_of(h)], dst_ref=corebuf.at[q, :, rows_of(h)],
            send_sem=core_s.at[q, h], recv_sem=core_r.at[q, h],
            device_id=(t, partner), device_id_type=MESH,
        )

    def to_z(q, s, h, source):
        return pltpu.make_async_remote_copy(
            src_ref=summed.at[q, s, rows_of(h)], dst_ref=zbuf.at[q, source, rows_of(h)],
            send_sem=z_s.at[q, s, h], recv_sem=z_r.at[q, source, h],
            device_id=(t, ZSETS[q % 2][s] * 2 + c), device_id_type=MESH,
        )

    def to_tm(k, h, d, source):
        return pltpu.make_async_remote_copy(
            src_ref=gath.at[source, k, rows_of(h)], dst_ref=gath.at[source, k, rows_of(h)],
            send_sem=g_s.at[k, h, d - 1], recv_sem=g_r.at[k, h, d - 1],
            device_id=(t ^ d, p), device_id_type=MESH,
        )

    def receive(q, pieces):
        for piece in pieces:
            for d in partners:
                exchange(q, piece, d, t ^ d).wait_recv()
                unpack(rbuf, q, t ^ d, piece)

    def own(q):
        for piece in range(3):
            unpack(sbuf, q, t, piece)

    def straddling(q):
        if q == 0:
            for lane in range(lane_tiles):
                @pl.when(t != owner(lane))
                def _():
                    straddle(lane, 1).wait_recv()
        at = q % 2 * 8
        place(2 * blocks, sprecv[q // 2].astype(jnp.float32)[at:at + 8])

    def core_stage(q, h):
        to_core(q, h).wait()
        for s in range(2):
            at = rows_of(h)
            summed[q, s, at] = part[q, c, s, at] + corebuf[q, s, at]

            @pl.when(z != ZSETS[q % 2][s])
            def _():
                to_z(q, s, h, z).start()

    def at_home(q):
        return (z == ZSETS[q % 2][0]) | (z == ZSETS[q % 2][1])

    def z_stage(q, h):
        for s in range(2):
            home = ZSETS[q % 2][s]

            @pl.when(z == home)
            def _():
                at = rows_of(h)
                total = summed[q, s, at]
                for other in range(NZ):
                    if other != home:
                        to_z(q, s, h, other).wait_recv()
                        total = total + zbuf[q, other, at]
                gath[t, q // 2, at] = total

    def spread_result(q, h):
        @pl.when(at_home(q))
        def _():
            for d in partners:
                to_tm(q // 2, h, d, t).start()

    for q in range(QUARTERS):
        last = q == QUARTERS - 1
        if 0 < q < QUARTERS - 1:
            for piece in range(3):
                send(q + 1, piece)
        own(q)
        receive(q, (0,))
        straddling(q)
        if q >= 1:
            for h in range(PIECES):
                z_stage(q - 1, h)
        receive(q, (1, 2))
        if last:
            for early_q in range(QUARTERS - 1):
                for h in range(PIECES):
                    spread_result(early_q, h)
        for s in range(2):
            gram(q, s, 1 - c)
        for h in range(PIECES):
            to_core(q, h).start()
        for s in range(2):
            gram(q, s, c)
        for h in range(PIECES):
            core_stage(q, h)
    for h in range(PIECES):
        z_stage(QUARTERS - 1, h)
        spread_result(QUARTERS - 1, h)

    for k in range(2):
        for h in range(PIECES):
            for d in partners:
                to_tm(k, h, d, t ^ d).wait_recv()
        for s in range(NT):
            out_ref[s * 2 + k] = gath[s, k]

    halo_copy(halo_to).wait_send()
    for q in range(QUARTERS):
        for piece in range(3):
            for d in partners:
                exchange(q, piece, d, t).wait_send()
        for s in range(2):
            @pl.when(z != ZSETS[q % 2][s])
            def _():
                for h in range(PIECES):
                    to_z(q, s, h, z).wait_send()
    for k in range(2):
        for h in range(PIECES):
            for d in partners:
                to_tm(k, h, d, t).wait_send()

    for lane in range(lane_tiles):
        @pl.when(middle)
        def _():
            hop_copy(lane, t, owner(lane)).wait_send()

        @pl.when(t == owner(lane))
        def _():
            for d in partners:
                straddle(lane, d).wait_send()


def finish(sums_ref, out_hbm, both, sems):
    freqs = sums_ref.shape[0]
    count = out_hbm.shape[1]

    def copy(part):
        size = freqs // 2 * 2 * count
        at = pl.ds(part * size, size)
        return pltpu.make_async_copy(both.at[at], out_hbm.at[at], sems.at[part])

    for part in range(2):
        for f in range(part * freqs // 2, (part + 1) * freqs // 2):
            ordered = sums_ref[f]
            fill = jnp.zeros((LANES - SLOTS, LANES), jnp.float32)
            mirrored = jnp.concatenate([ordered, fill], axis=0).T[:SLOTS]
            first = f * 2 * count
            both[pl.ds(first, count, stride=2), :] = 0.5 * (ordered + mirrored)[:count, :count]
            both[pl.ds(first + 1, count, stride=2), :] = 0.5 * (ordered - mirrored)[:count, :count]
        copy(part).start()
    for part in range(2):
        copy(part).wait()


def fused(codes, scales, weights, freq_indices, total_points):
    rows, points = codes.shape
    blocks = rows // HOP
    pairs = blocks // 2
    lane_tiles = points // LANES
    count = rows * NT // HOP - 1
    f32, bf16 = jnp.float32, jnp.bfloat16
    dma = pltpu.SemaphoreType.DMA
    hbm = pl.BlockSpec(memory_space=pltpu.HBM)
    vmem = pl.BlockSpec(memory_space=pltpu.VMEM)
    pinned = [
        pltpu.with_memory_space_constraint(x, pltpu.HBM) for x in (codes, scales, weights, freq_indices)
    ]
    sums = pl.pallas_call(
        functools.partial(kernel, total_points),
        out_shape=jax.ShapeDtypeStruct((2 * NT, SLOTS, LANES), f32),
        in_specs=[hbm, hbm, hbm, hbm],
        out_specs=vmem,
        scratch_shapes=[
            pltpu.VMEM((rows, points), bf16),
            pltpu.VMEM((rows,), f32),
            pltpu.VMEM((points,), f32),
            pltpu.SMEM(freq_indices.shape, jnp.int32),
            pltpu.VMEM((rows, LANES), f32),
            pltpu.VMEM((rows + HALF, points), bf16),
            pltpu.VMEM((2 * NT * QUARTERS * 4, NFFT), bf16),
            pltpu.VMEM((QUARTERS, NT, pairs, 16, points), bf16),
            pltpu.VMEM((QUARTERS, NT, pairs, 16, points), bf16),
            pltpu.VMEM((NFFT, points), bf16),
            pltpu.VMEM((NT, 2, 16, points), bf16),
            pltpu.VMEM((2, 16, points), bf16),
            pltpu.VMEM((points // LANES, 8 * SLOTS, LANES), f32),
            pltpu.VMEM((QUARTERS, 2, 2, SLOTS, LANES), f32),
            pltpu.VMEM((QUARTERS, 2, SLOTS, LANES), f32),
            pltpu.VMEM((QUARTERS, 2, SLOTS, LANES), f32),
            pltpu.VMEM((QUARTERS, NZ, SLOTS, LANES), f32),
            pltpu.VMEM((NT, 2, SLOTS, LANES), f32),
            dma((6,)),
            dma, dma,
            dma((QUARTERS, 3, NT - 1)), dma((QUARTERS, 3, NT - 1)),
            dma((lane_tiles,)), dma((2, lane_tiles)),
            dma((lane_tiles, NT - 1)), dma((lane_tiles,)),
            dma((QUARTERS, PIECES)), dma((QUARTERS, PIECES)),
            dma((QUARTERS, 2, PIECES)), dma((QUARTERS, NZ, PIECES)),
            dma((2, PIECES, NT - 1)), dma((2, PIECES, NT - 1)),
        ],
        compiler_params=pltpu.CompilerParams(
            collective_id=0, has_side_effects=True, vmem_limit_bytes=40 * 2**20
        ),
        name="spectra_cross",
    )(*pinned)
    full = pl.pallas_call(
        finish,
        out_shape=jax.ShapeDtypeStruct((2 * NT * 2 * count, count), f32),
        in_specs=[vmem],
        out_specs=hbm,
        scratch_shapes=[pltpu.VMEM((2 * NT * 2 * count, count), f32), dma((2,))],
        name="hermitian_parts",
    )(pltpu.with_memory_space_constraint(sums, pltpu.VMEM))
    return full.reshape(2 * NT, count, 2, count).transpose(0, 2, 1, 3)


def cross_matrices(stacked):
    blocks = stacked.shape[1] // 2
    products = jnp.einsum("fip,fjp->fij", stacked, stacked, preferred_element_type=jnp.float32)
    matrix_re = products[:, :blocks, :blocks] + products[:, blocks:, blocks:]
    matrix_im = products[:, :blocks, blocks:] - products[:, blocks:, :blocks]
    return jnp.stack([matrix_re, matrix_im], axis=1)


def general(codes, scales, weights, freq_indices):
    values = (codes.astype(jnp.float32) * scales[:, None]).astype(jnp.bfloat16)
    regrouped = lax.all_to_all(values, "tm", split_axis=1, concat_axis=0, tiled=True)
    point_count = regrouped.shape[1]
    own_weights = lax.dynamic_slice_in_dim(
        weights, lax.axis_index("tm") * point_count, point_count, 0
    )
    total_points = weights.shape[0] * lax.axis_size("pts")
    root_weight = jnp.sqrt(own_weights / total_points)
    cosine_table, sine_table = make_tables(freq_indices)
    hop_rows = regrouped.reshape(-1, NFFT // 2, point_count)
    windows = jnp.concatenate([hop_rows[:-1], hop_rows[1:]], axis=1)
    real_part = jnp.einsum("fn,bnp->fbp", cosine_table, windows, preferred_element_type=jnp.float32)
    imag_part = jnp.einsum("fn,bnp->fbp", sine_table, windows, preferred_element_type=jnp.float32)
    scaled_re = (real_part * root_weight[None, None, :]).astype(jnp.bfloat16)
    scaled_im = (imag_part * root_weight[None, None, :]).astype(jnp.bfloat16)
    stacked = jnp.concatenate([scaled_re, scaled_im], axis=1)
    partial_value = lax.psum_scatter(
        cross_matrices(stacked), "pts", scatter_dimension=0, tiled=True
    )
    return lax.psum(partial_value, "tm")


def solution(mesh):
    nt, np_ = mesh.shape["tm"], mesh.shape["pts"]

    def per_device(codes, scales, weights, freq_indices):
        rows, points = codes.shape
        fits = (
            nt == NT
            and np_ == 2 * NZ
            and freq_indices.shape[0] == 2 * nt * np_
            and points % LANES == 0
            and rows % NFFT == HALF
            and rows >= 16 * HOP
            and 4 * (rows // HOP) + 1 <= SLOTS
        )
        if fits:
            return fused(codes, scales, weights, freq_indices, points * np_)
        return general(codes, scales, weights, freq_indices)

    return jax.shard_map(
        per_device,
        mesh=mesh,
        in_specs=(P("tm", "pts"), P("tm"), P("pts"), P()),
        out_specs=P("pts", None, None, None),
        check_vma=False,
    )
```

```python
import functools
import math

import jax
import jax.numpy as jnp
from jax import lax
from jax.experimental import pallas as pl
from jax.experimental.pallas import tpu as pltpu
from jax.sharding import PartitionSpec as P

NFFT = 256
HOP = NFFT // 2
HALF = HOP // 2
LANES = 128
SLOTS = 96
KEPT = 72
NT = 4
NZ = 4
QUARTERS = 4
FULL = 3
ROW_PARTS = ((0, 72),)
PIECES = len(ROW_PARTS)
ZSETS = ((0, 3), (1, 2))
ORDERS = (
    ((0, 0), (0, 1), (3, 0), (3, 1)),
    ((1, 0), (1, 1), (2, 0), (2, 1)),
    ((0, 0), (0, 1), (3, 0), (3, 1)),
    ((1, 1), (2, 0), (1, 0), (2, 1)),
)
MESH = pl.DeviceIdType.MESH


def make_tables(freq_indices):
    sample = jnp.arange(NFFT, dtype=jnp.int32)
    phases = freq_indices[:, None] * sample[None, :] % NFFT
    angles = phases.astype(jnp.float32) * (2.0 * math.pi / NFFT)
    hann_window = 0.5 - 0.5 * jnp.cos(sample.astype(jnp.float32) * (2.0 * math.pi / NFFT))
    cosine_table = (0.25 * hann_window[None, :] * jnp.cos(angles)).astype(jnp.bfloat16)
    sine_table = (-0.25 * hann_window[None, :] * jnp.sin(angles)).astype(jnp.bfloat16)
    return (cosine_table, sine_table)


def turn_waves(turn):
    angle = turn.astype(jnp.float32) * (2.0 * math.pi / NFFT)
    quarter = (turn + NFFT // 8) // (NFFT // 4)
    count = quarter.astype(jnp.float32)
    x = ((angle - count * 1.5703125) - count * 4.837512969970703125e-4) - count * 7.549789948768648e-8
    y = x * x
    sine = x + x * y * (-1.0 / 6.0 + y * (1.0 / 120.0 + y * (-1.0 / 5040.0 + y * (1.0 / 362880.0))))
    cosine = 1.0 + y * (-0.5 + y * (1.0 / 24.0 + y * (-1.0 / 720.0 + y * (1.0 / 40320.0))))
    swap = quarter % 2 == 1
    low = jnp.where(swap, sine, cosine)
    high = jnp.where(swap, cosine, sine)
    return (
        jnp.where((quarter + 1) % 4 >= 2, -low, low),
        jnp.where(quarter % 4 >= 2, -high, high),
    )


def fold(matrix):
    lane = lax.broadcasted_iota(jnp.int32, (KEPT, LANES), 1)
    rest = jnp.zeros((LANES - (SLOTS - KEPT), LANES), jnp.float32)
    turned = jnp.concatenate([matrix[KEPT:], rest], axis=0).T
    corner = turned[KEPT:SLOTS]
    corners = jnp.concatenate([pltpu.roll(corner, LANES - 8 * m, 1) for m in (1, 2, 3)], axis=0)
    side = pltpu.roll(turned[:KEPT], SLOTS, 1)
    return jnp.where(lane < SLOTS, matrix[:KEPT], jnp.where(lane < LANES - 8, side, corners))


def unfold(folded):
    lane = lax.broadcasted_iota(jnp.int32, (KEPT, LANES), 1)
    top = jnp.where(lane < SLOTS, folded, 0.0)
    side = jnp.where(lane < SLOTS - KEPT, pltpu.roll(folded, LANES - SLOTS, 1), 0.0)
    size = SLOTS - KEPT
    corner = jnp.zeros((size, LANES), jnp.float32)
    for m in (1, 2, 3):
        moved = pltpu.roll(folded[(m - 1) * size:m * size], 8 * m, 1)
        here = lane[:size]
        corner = jnp.where((here >= 8 * m - 8) & (here < 8 * m), moved, corner)
    rest = jnp.zeros((LANES - SLOTS, LANES), jnp.float32)
    turned = jnp.concatenate([side, corner, rest], axis=0).T
    return jnp.concatenate([top, turned[:size]], axis=0)


def kernel(
    total_points,
    codes_hbm, scales_hbm, weights_hbm, freq_hbm, out_ref,
    codes_ref, scales_v, weights_v, freq_ref, spread, vals, table, sbuf, rbuf, sfirst, rfirst, slast, rlast, hops, spbuf, sprecv, stage,
    part, corebuf, summed, zbuf, part2, corebuf2, summed2, zbuf2, homebuf, gath,
    load_s, halo_s, halo_r, tm_s, tm_r, first_s, first_r, last_s, last_r, hop_s, hop_r, sp_s, sp_r, core_s, core_r, z_s, z_r, core2_s, core2_r, z2_s, z2_r, home_s, home_r, g_s, g_r,
):
    rows, points = codes_ref.shape
    t = lax.axis_index("tm")
    p = lax.axis_index("pts")
    z = p // 2
    c = p % 2
    odd = t % 2
    partner = p + 1 - 2 * c
    lane_tiles = points // LANES
    blocks = rows // HOP
    pairs = blocks // 2
    padded = rows + HALF

    early = (10 * HOP)
    late = rows - early - HALF
    edge_at = (1 - odd) * (rows - HALF)
    early_at = odd * (rows - early)
    late_at = odd * HALF + (1 - odd) * early

    def load(at, count, sem):
        at = pl.ds(pl.multiple_of(at, HALF), count)
        return pltpu.make_async_copy(codes_hbm.at[at], codes_ref.at[at], load_s.at[sem])

    load_scales = pltpu.make_async_copy(scales_hbm, scales_v, load_s.at[3])
    load_weights = pltpu.make_async_copy(weights_hbm, weights_v, load_s.at[4])
    load_freq = pltpu.make_async_copy(freq_hbm, freq_ref, load_s.at[5])
    load_edge = load(edge_at, HALF, 0)
    load_early = load(early_at, early, 1)
    load_late = load(late_at, late, 2)
    barrier = pltpu.get_barrier_semaphore()
    for d in range(1, NT):
        pl.semaphore_signal(barrier, inc=1, device_id=(t ^ d, p), device_id_type=MESH)
    pl.semaphore_signal(barrier, inc=1, device_id=(t, partner), device_id_type=MESH)
    for d in range(1, NZ):
        pl.semaphore_signal(barrier, inc=1, device_id=(t, (z + d) % NZ * 2 + c), device_id_type=MESH)
    load_freq.start()
    load_scales.start()
    load_edge.start()
    load_early.start()
    load_weights.start()
    load_late.start()

    sample = lax.broadcasted_iota(jnp.int32, (8, NFFT), 1)
    sub = lax.broadcasted_iota(jnp.int32, (8, NFFT), 0)
    window_shape = 0.25 * (0.5 - 0.5 * turn_waves(sample)[0])

    def octet_table(dest, q):
        bins = jnp.zeros((8, NFFT), jnp.int32)
        for j in range(4):
            dest_p = ORDERS[q][j][0] * 2 + ORDERS[q][j][1]
            bins = jnp.where(sub // 2 == j, freq_ref[dest_p * 2 * NT + dest * 2 + q // 2], bins)
        cosine, sine = turn_waves(bins * sample % NFFT)
        return window_shape * jnp.where(sub % 2 == 0, cosine, -sine)

    load_freq.wait()
    for dest in range(NT):
        for half in range(2):
            at = dest * 32 + half * 16
            pair = [octet_table(dest, 2 * half), octet_table(dest, 2 * half + 1)]
            table[at:at + 16, :] = jnp.concatenate(pair, axis=0).astype(jnp.bfloat16)

    load_scales.wait()
    for g in range(-(-rows // HOP)):
        size = min(HOP, rows - g * HOP)
        line = scales_v[g * HOP:g * HOP + size].reshape(1, size)
        spread[g * HOP:g * HOP + size, :] = jnp.broadcast_to(line, (LANES, size)).T

    offset = odd * HALF

    def dequantize(i, carry):
        at = pl.ds(pl.multiple_of(i * HALF, HALF), HALF)
        to = pl.ds(pl.multiple_of(i * HALF + offset, HALF), HALF)
        scale = spread[at, :]
        for lane in range(lane_tiles):
            cols = slice(lane * LANES, (lane + 1) * LANES)
            vals[to, cols] = (codes_ref[at, cols].astype(jnp.float32) * scale).astype(jnp.bfloat16)
        return carry

    load_edge.wait()
    dequantize(edge_at // HALF, 0)
    halo_from = (1 - odd) * (rows - HALF) + odd * HALF
    halo_to = odd * rows
    halo_mine = (1 - odd) * rows

    def halo_copy(dst):
        return pltpu.make_async_remote_copy(
            src_ref=vals.at[pl.ds(pl.multiple_of(halo_from, HALF), HALF)],
            dst_ref=vals.at[pl.ds(pl.multiple_of(dst, HALF), HALF)],
            send_sem=halo_s, recv_sem=halo_r,
            device_id=(t ^ 1, p), device_id_type=MESH,
        )

    pl.semaphore_wait(barrier, NT + NZ - 1)
    halo_copy(halo_to).start()

    load_early.wait()
    lax.fori_loop(early_at // HALF, (early_at + early) // HALF, dequantize, 0)
    load_weights.wait()
    root_weight = jnp.sqrt(weights_v[...].reshape(1, points) / total_points)

    def spectrum(i):
        window = vals[pl.ds(pl.multiple_of(i * HOP, HOP), NFFT), :]
        return jnp.dot(table[...], window, preferred_element_type=jnp.float32) * root_weight

    def octets(result, dest, q):
        return result[dest * 32 + q * 8:dest * 32 + q * 8 + 8]

    def pair_tiles(jj, first, second):
        for dest in range(NT):
            for q in range(FULL):
                both = jnp.concatenate([octets(first, dest, q), octets(second, dest, q)], axis=0)
                sbuf[q, dest, jj] = both.astype(jnp.bfloat16)

    def spectra(u, carry):
        low = odd * (pairs - 2 - 2 * u) + (1 - odd) * 2 * u
        results = [spectrum(2 * low + r) for r in range(4)]
        pair_tiles(low, results[0], results[1])
        pair_tiles(low + 1, results[2], results[3])
        v = odd * (quads - 1 - u) + (1 - odd) * u
        for dest in range(NT):
            last = [octets(r, dest, FULL) for r in results]
            sfirst[dest, v] = jnp.concatenate([o[:4] for o in last], axis=0).astype(jnp.bfloat16)
            slast[dest, v] = jnp.concatenate([o[4:] for o in last], axis=0).astype(jnp.bfloat16)
        return carry

    def spectra_pair():
        jj = (1 - odd) * (pairs - 1)
        first, second = spectrum(2 * jj), spectrum(2 * jj + 1)
        pair_tiles(jj, first, second)
        for dest in range(NT):
            one, two = octets(first, dest, FULL), octets(second, dest, FULL)
            mixed = jnp.concatenate([one[:4], two[:4], one[4:], two[4:]], axis=0)
            sfirst[dest, quads] = mixed.astype(jnp.bfloat16)

    quads = pairs // 2
    q_cut = 2
    cuts = (0, 2 * q_cut, pairs - 1, pairs)
    partners = (3, 1, 2)

    def tiles_of(who, piece):
        count = cuts[piece + 1] - cuts[piece]
        flip = who % 2
        return flip * (pairs - cuts[piece + 1]) + (1 - flip) * cuts[piece], count

    def exchange(q, piece, d, source):
        at, count = tiles_of(source, piece)
        return pltpu.make_async_remote_copy(
            src_ref=sbuf.at[q, t ^ d, pl.ds(at, count)],
            dst_ref=rbuf.at[q, source, pl.ds(at, count)],
            send_sem=tm_s.at[q, piece, d - 1], recv_sem=tm_r.at[q, piece, d - 1],
            device_id=(t ^ d, p), device_id_type=MESH,
        )

    def exchange_first(d, source):
        return pltpu.make_async_remote_copy(
            src_ref=sfirst.at[t ^ d], dst_ref=rfirst.at[source],
            send_sem=first_s.at[d - 1], recv_sem=first_r.at[d - 1],
            device_id=(t ^ d, p), device_id_type=MESH,
        )

    last_cuts = (0, 3, quads)

    def exchange_last(piece, d, source):
        at = pl.ds(last_cuts[piece], last_cuts[piece + 1] - last_cuts[piece])
        return pltpu.make_async_remote_copy(
            src_ref=slast.at[t ^ d, at], dst_ref=rlast.at[source, at],
            send_sem=last_s.at[piece, d - 1], recv_sem=last_r.at[piece, d - 1],
            device_id=(t ^ d, p), device_id_type=MESH,
        )

    middle = (t == 1) | (t == 2)
    outer = (t == 0) | (t == 3)

    def owner(lane):
        if 2 * lane + 1 == lane_tiles:
            return (NT - 1) * (1 - c)
        return (NT - 1) * int(2 * lane + 1 > lane_tiles)

    def lanes(lane):
        return pl.ds(lane * LANES, LANES)

    def hop_copy(lane, source, dest):
        return pltpu.make_async_remote_copy(
            src_ref=vals.at[pl.ds(pl.multiple_of(odd * (padded - HOP), HOP), HOP), lanes(lane)],
            dst_ref=hops.at[pl.ds(pl.multiple_of((source - 1) * HOP, HOP), HOP), lanes(lane)],
            send_sem=hop_s.at[lane], recv_sem=hop_r.at[source - 1, lane],
            device_id=(dest, p), device_id_type=MESH,
        )

    def straddle(lane, d):
        return pltpu.make_async_remote_copy(
            src_ref=spbuf.at[t ^ d, :, :, lanes(lane)],
            dst_ref=sprecv.at[:, :, lanes(lane)],
            send_sem=sp_s.at[lane, d - 1], recv_sem=sp_r.at[lane],
            device_id=(t ^ d, p), device_id_type=MESH,
        )

    def send(q, piece):
        for d in partners:
            exchange(q, piece, d, t).start()


    @pl.when(middle)
    def _():
        for lane in range(lane_tiles):
            hop_copy(lane, t, owner(lane)).start()

    lax.fori_loop(0, q_cut, spectra, 0)
    send(0, 0)
    load_late.wait()
    lax.fori_loop(late_at // HALF, (late_at + late) // HALF, dequantize, 0)
    lax.fori_loop(q_cut, quads, spectra, 0)
    send(0, 1)
    halo_copy(halo_mine).wait_recv()
    spectra_pair()
    send(0, 2)

    @pl.when(outer)
    def _():
        for lane in range(lane_tiles):
            @pl.when(t == owner(lane))
            def _():
                for source in (1, 2):
                    hop_copy(lane, source, owner(lane)).wait_recv()
        result = jnp.dot(table[...], hops[...], preferred_element_type=jnp.float32)
        result = (result * root_weight).astype(jnp.bfloat16)
        for dest in range(NT):
            for h in range(2):
                spbuf[dest, h] = result[dest * 32 + h * 16:dest * 32 + h * 16 + 16]
        for lane in range(lane_tiles):
            @pl.when(t == owner(lane))
            def _():
                for d in partners:
                    straddle(lane, d).start()
                sprecv[:, :, lanes(lane)] = spbuf[t, :, :, lanes(lane)]

    for piece in range(3):
        send(1, piece)

    for lane in range(lane_tiles):
        for s in range(8):
            stage[lane, s * SLOTS + SLOTS - 8:(s + 1) * SLOTS, :] = jnp.zeros((8, LANES), jnp.float32)

    def place(b, octet):
        for lane in range(lane_tiles):
            stage[lane, pl.ds(b, 8, stride=SLOTS), :] = octet[:, lane * LANES:(lane + 1) * LANES]

    def unpack(source_ref, q, who, piece):
        at, count = tiles_of(who, piece)
        base = who * blocks + who // 2

        def one(i, carry):
            tile = source_ref[q, who, i].astype(jnp.float32)
            place(base + 2 * i, tile[:8])
            place(base + 2 * i + 1, tile[8:])
            return carry

        lax.fori_loop(at, at + count, one, 0)

    def place_four(half, b, octet):
        for lane in range(lane_tiles):
            at = pl.ds(half * 4 * SLOTS + b, 4, stride=SLOTS)
            stage[lane, at, :] = octet[:, lane * LANES:(lane + 1) * LANES]

    def unpack_fours(source_ref, half, who, first, last):
        base = who * blocks + who // 2 + 2 * (who % 2)

        def one(v, carry):
            tile = source_ref[who, v].astype(jnp.float32)
            for r in range(4):
                place_four(half, base + 4 * v + r, tile[4 * r:4 * r + 4])
            return carry

        lax.fori_loop(first, last, one, 0)

    def unpack_mixed(source_ref, who):
        base = who * blocks + who // 2 + (1 - who % 2) * 2 * (pairs - 1)
        tile = source_ref[who, quads].astype(jnp.float32)
        for r in range(4):
            place_four(r // 2, base + r % 2, tile[4 * r:4 * r + 4])

    def gram(j):
        at = pl.ds(pl.multiple_of(j * 2 * SLOTS, 2 * SLOTS), 2 * SLOTS)
        stacked = jnp.concatenate(
            [stage[lane, at, :].astype(jnp.bfloat16) for lane in range(lane_tiles)], axis=1
        )
        fill = jnp.zeros((LANES - SLOTS, points), jnp.bfloat16)
        wide = jnp.concatenate([stacked[:SLOTS], fill, stacked[SLOTS:], fill], axis=0)
        prod = lax.dot_general(
            stacked, wide, (((1,), (1,)), ((), ())), preferred_element_type=jnp.float32
        )
        real = prod[:SLOTS, :LANES] + prod[SLOTS:, LANES:]
        imag = prod[:SLOTS, LANES:] - prod[SLOTS:, :LANES]
        return fold(real + imag)

    def rows_of(h):
        return pl.ds(*ROW_PARTS[h])

    def to_core(q, h):
        return pltpu.make_async_remote_copy(
            src_ref=part.at[q, 1 - c, :, rows_of(h)], dst_ref=corebuf.at[q, :, rows_of(h)],
            send_sem=core_s.at[q, h], recv_sem=core_r.at[q, h],
            device_id=(t, partner), device_id_type=MESH,
        )

    def to_z(q, s, h, source):
        return pltpu.make_async_remote_copy(
            src_ref=summed.at[q, s, rows_of(h)], dst_ref=zbuf.at[q, source, rows_of(h)],
            send_sem=z_s.at[q, s, h], recv_sem=z_r.at[q, source, h],
            device_id=(t, ZSETS[q % 2][s] * 2 + c), device_id_type=MESH,
        )

    def home_of(e):
        return (1 - e) * (2 - c) + e * (1 + c)

    def to_core2(e, h):
        return pltpu.make_async_remote_copy(
            src_ref=part2.at[e, 1 - c, rows_of(h)], dst_ref=corebuf2.at[e, rows_of(h)],
            send_sem=core2_s.at[e, h], recv_sem=core2_r.at[e, h],
            device_id=(t, partner), device_id_type=MESH,
        )

    def to_z2(h, source):
        return pltpu.make_async_remote_copy(
            src_ref=summed2.at[0, rows_of(h)], dst_ref=zbuf2.at[source, rows_of(h)],
            send_sem=z2_s.at[h], recv_sem=z2_r.at[source, h],
            device_id=(t, home_of(0) * 2 + c), device_id_type=MESH,
        )

    def to_home(d, source_z, source_t):
        return pltpu.make_async_remote_copy(
            src_ref=summed2.at[1], dst_ref=homebuf.at[source_z, source_t],
            send_sem=home_s.at[d], recv_sem=home_r.at[source_z, source_t],
            device_id=(t ^ d, home_of(1) * 2 + c), device_id_type=MESH,
        )

    def gram2(e, side):
        part2[e, side] = gram((1 - e) * (1 - side) + e * (2 + side))

    def core_sum2(e, h):
        to_core2(e, h).wait_recv()
        at = rows_of(h)
        summed2[e, at] = part2[e, c, at] + corebuf2[e, at]

    def core_stage2(h):
        core_sum2(0, h)

        @pl.when(z != home_of(0))
        def _():
            to_z2(h, z).start()

    def home_stage():
        for h in range(PIECES):
            core_sum2(1, h)
        for d in partners:
            to_home(d, z, t).start()

        @pl.when(z != home_of(1))
        def _():
            to_home(0, z, t).start()

    def z_stage2(h):
        @pl.when(z == home_of(0))
        def _():
            at = rows_of(h)
            total = summed2[0, at]
            for d in range(1, NZ):
                other = (z + d) % NZ
                to_z2(h, other).wait_recv()
                total = total + zbuf2[other, at]
            gath[t, 1, at] = total
            for d in partners:
                to_tm(1, h, d, t).start()

    def to_tm(k, h, d, source):
        return pltpu.make_async_remote_copy(
            src_ref=gath.at[source, k, rows_of(h)], dst_ref=gath.at[source, k, rows_of(h)],
            send_sem=g_s.at[k, h, d - 1], recv_sem=g_r.at[k, h, d - 1],
            device_id=(t ^ d, p), device_id_type=MESH,
        )

    def receive(q, pieces):
        for piece in pieces:
            for d in partners:
                exchange(q, piece, d, t ^ d).wait_recv()
                unpack(rbuf, q, t ^ d, piece)

    def own(q):
        for piece in range(3):
            unpack(sbuf, q, t, piece)

    def straddling(q):
        if q == 0:
            for lane in range(lane_tiles):
                @pl.when(t != owner(lane))
                def _():
                    straddle(lane, 1).wait_recv()
        at = q % 2 * 8
        place(2 * blocks, sprecv[q // 2].astype(jnp.float32)[at:at + 8])

    def core_stage(q, h):
        to_core(q, h).wait_recv()
        for s in range(2):
            at = rows_of(h)
            summed[q, s, at] = part[q, c, s, at] + corebuf[q, s, at]

            @pl.when(z != ZSETS[q % 2][s])
            def _():
                to_z(q, s, h, z).start()

    def at_home(q):
        return (z == ZSETS[q % 2][0]) | (z == ZSETS[q % 2][1])

    def z_stage(q, h):
        for s in range(2):
            home = ZSETS[q % 2][s]

            @pl.when(z == home)
            def _():
                at = rows_of(h)
                total = summed[q, s, at]
                for other in range(NZ):
                    if other != home:
                        to_z(q, s, h, other).wait_recv()
                        total = total + zbuf[q, other, at]
                gath[t, q // 2, at] = total

    def spread_result(q, h):
        @pl.when(at_home(q))
        def _():
            for d in partners:
                to_tm(q // 2, h, d, t).start()

    def send_first():
        for d in partners:
            exchange_first(d, t).start()

    def send_last():
        for piece in range(2):
            for d in partners:
                exchange_last(piece, d, t).start()

    for q in range(FULL):
        if q == 1:
            for piece in range(3):
                send(2, piece)
        if q == 2:
            send_first()
        own(q)
        receive(q, (0,))
        straddling(q)
        if q >= 1:
            for h in range(PIECES):
                z_stage(q - 1, h)
        receive(q, (1, 2))
        for s in range(2):
            part[q, 1 - c, s] = gram(2 * s + 1 - c)
        for h in range(PIECES):
            to_core(q, h).start()
        for s in range(2):
            part[q, c, s] = gram(2 * s + c)
        for h in range(PIECES):
            core_stage(q, h)

    send_last()
    unpack_fours(sfirst, 0, t, 0, quads)
    unpack_mixed(sfirst, t)
    unpack_fours(slast, 1, t, 0, quads)
    straddling(FULL)
    for d in partners:
        exchange_first(d, t ^ d).wait_recv()
        unpack_fours(rfirst, 0, t ^ d, 0, quads)
        unpack_mixed(rfirst, t ^ d)
    gram2(0, 1 - c)
    for h in range(PIECES):
        to_core2(0, h).start()
    gram2(0, c)
    for piece in range(2):
        for d in partners:
            exchange_last(piece, d, t ^ d).wait_recv()
            unpack_fours(rlast, 1, t ^ d, last_cuts[piece], last_cuts[piece + 1])
        if piece == 0:
            for h in range(PIECES):
                core_stage2(h)
                spread_result(0, h)
                spread_result(1, h)
    gram2(1, 1 - c)
    for h in range(PIECES):
        to_core2(1, h).start()
    gram2(1, c)
    home_stage()
    for h in range(PIECES):
        z_stage(2, h)
        spread_result(2, h)
    for h in range(PIECES):
        z_stage2(h)
    halo_copy(halo_to).wait_send()
    for d in partners:
        exchange_first(d, t).wait_send()
        for piece in range(2):
            exchange_last(piece, d, t).wait_send()
    for q in range(FULL):
        for piece in range(3):
            for d in partners:
                exchange(q, piece, d, t).wait_send()
        for h in range(PIECES):
            to_core(q, h).wait_send()
        for s in range(2):
            @pl.when(z != ZSETS[q % 2][s])
            def _():
                for h in range(PIECES):
                    to_z(q, s, h, z).wait_send()
    for lane in range(lane_tiles):
        @pl.when(middle)
        def _():
            hop_copy(lane, t, owner(lane)).wait_send()

        @pl.when(t == owner(lane))
        def _():
            for d in partners:
                straddle(lane, d).wait_send()

    for h in range(PIECES):
        to_core2(0, h).wait_send()

        @pl.when(z != home_of(0))
        def _():
            to_z2(h, z).wait_send()

        for d in partners:
            to_tm(0, h, d, t).wait_send()

    def gathered(k):
        out_ref[t * 2 + k] = unfold(gath[t, k])
        for d in (1, 2, 3):
            for h in range(PIECES):
                to_tm(k, h, d, t ^ d).wait_recv()
            out_ref[(t ^ d) * 2 + k] = unfold(gath[t ^ d, k])

    gathered(0)

    @pl.when(z != home_of(1))
    def _():
        gathered(1)
        for h in range(PIECES):
            for d in partners:
                to_tm(1, h, d, t).wait_send()

    @pl.when(z == home_of(1))
    def _():
        for d in range(NT):
            source = t ^ d
            if d == 0:
                total = summed2[1]
            else:
                to_home(d, z, source).wait_recv()
                total = homebuf[z, source]
            for step in range(1, NZ):
                other = (z + step) % NZ
                to_home(d, other, source).wait_recv()
                total = total + homebuf[other, source]
            out_ref[source * 2 + 1] = unfold(total)

    for h in range(PIECES):
        to_core2(1, h).wait_send()
    for d in partners:
        to_home(d, z, t).wait_send()

    @pl.when(z != home_of(1))
    def _():
        to_home(0, z, t).wait_send()


def finish(sums_ref, out_hbm, both, sems):
    freqs = sums_ref.shape[0]
    count = out_hbm.shape[1]

    def copy(part):
        size = freqs // 2 * 2 * count
        at = pl.ds(part * size, size)
        return pltpu.make_async_copy(both.at[at], out_hbm.at[at], sems.at[part])

    for part in range(2):
        for f in range(part * freqs // 2, (part + 1) * freqs // 2):
            ordered = sums_ref[f]
            fill = jnp.zeros((LANES - SLOTS, LANES), jnp.float32)
            mirrored = jnp.concatenate([ordered, fill], axis=0).T[:SLOTS]
            first = f * 2 * count
            both[pl.ds(first, count, stride=2), :] = 0.5 * (ordered + mirrored)[:count, :count]
            both[pl.ds(first + 1, count, stride=2), :] = 0.5 * (ordered - mirrored)[:count, :count]
        copy(part).start()
    for part in range(2):
        copy(part).wait()


def fused(codes, scales, weights, freq_indices, total_points):
    rows, points = codes.shape
    blocks = rows // HOP
    pairs = blocks // 2
    lane_tiles = points // LANES
    count = rows * NT // HOP - 1
    f32, bf16 = jnp.float32, jnp.bfloat16
    dma = pltpu.SemaphoreType.DMA
    hbm = pl.BlockSpec(memory_space=pltpu.HBM)
    vmem = pl.BlockSpec(memory_space=pltpu.VMEM)
    pinned = [
        pltpu.with_memory_space_constraint(x, pltpu.HBM) for x in (codes, scales, weights, freq_indices)
    ]
    sums = pl.pallas_call(
        functools.partial(kernel, total_points),
        out_shape=jax.ShapeDtypeStruct((2 * NT, SLOTS, LANES), f32),
        in_specs=[hbm, hbm, hbm, hbm],
        out_specs=vmem,
        scratch_shapes=[
            pltpu.VMEM((rows, points), bf16),
            pltpu.VMEM((rows,), f32),
            pltpu.VMEM((points,), f32),
            pltpu.SMEM(freq_indices.shape, jnp.int32),
            pltpu.VMEM((rows, LANES), f32),
            pltpu.VMEM((rows + HALF, points), bf16),
            pltpu.VMEM((2 * NT * QUARTERS * 4, NFFT), bf16),
            pltpu.VMEM((FULL, NT, pairs, 16, points), bf16),
            pltpu.VMEM((FULL, NT, pairs, 16, points), bf16),
            pltpu.VMEM((NT, pairs // 2 + 1, 16, points), bf16),
            pltpu.VMEM((NT, pairs // 2 + 1, 16, points), bf16),
            pltpu.VMEM((NT, pairs // 2, 16, points), bf16),
            pltpu.VMEM((NT, pairs // 2, 16, points), bf16),
            pltpu.VMEM((NFFT, points), bf16),
            pltpu.VMEM((NT, 2, 16, points), bf16),
            pltpu.VMEM((2, 16, points), bf16),
            pltpu.VMEM((points // LANES, 8 * SLOTS, LANES), f32),
            pltpu.VMEM((FULL, 2, 2, KEPT, LANES), f32),
            pltpu.VMEM((FULL, 2, KEPT, LANES), f32),
            pltpu.VMEM((FULL, 2, KEPT, LANES), f32),
            pltpu.VMEM((FULL, NZ, KEPT, LANES), f32),
            pltpu.VMEM((2, 2, KEPT, LANES), f32),
            pltpu.VMEM((2, KEPT, LANES), f32),
            pltpu.VMEM((2, KEPT, LANES), f32),
            pltpu.VMEM((NZ, KEPT, LANES), f32),
            pltpu.VMEM((NZ, NT, KEPT, LANES), f32),
            pltpu.VMEM((NT, 2, KEPT, LANES), f32),
            dma((6,)),
            dma, dma,
            dma((FULL, 3, NT - 1)), dma((FULL, 3, NT - 1)),
            dma((NT - 1,)), dma((NT - 1,)),
            dma((2, NT - 1)), dma((2, NT - 1)),
            dma((lane_tiles,)), dma((2, lane_tiles)),
            dma((lane_tiles, NT - 1)), dma((lane_tiles,)),
            dma((FULL, PIECES)), dma((FULL, PIECES)),
            dma((FULL, 2, PIECES)), dma((FULL, NZ, PIECES)),
            dma((2, PIECES)), dma((2, PIECES)),
            dma((PIECES,)), dma((NZ, PIECES)),
            dma((NT,)), dma((NZ, NT)),
            dma((2, PIECES, NT - 1)), dma((2, PIECES, NT - 1)),
        ],
        compiler_params=pltpu.CompilerParams(
            collective_id=0, has_side_effects=True, vmem_limit_bytes=40 * 2**20
        ),
        name="spectra_cross",
    )(*pinned)
    full = pl.pallas_call(
        finish,
        out_shape=jax.ShapeDtypeStruct((2 * NT * 2 * count, count), f32),
        in_specs=[vmem],
        out_specs=hbm,
        scratch_shapes=[pltpu.VMEM((2 * NT * 2 * count, count), f32), dma((2,))],
        name="hermitian_parts",
    )(pltpu.with_memory_space_constraint(sums, pltpu.VMEM))
    return full.reshape(2 * NT, count, 2, count).transpose(0, 2, 1, 3)


def cross_matrices(stacked):
    blocks = stacked.shape[1] // 2
    products = jnp.einsum("fip,fjp->fij", stacked, stacked, preferred_element_type=jnp.float32)
    matrix_re = products[:, :blocks, :blocks] + products[:, blocks:, blocks:]
    matrix_im = products[:, :blocks, blocks:] - products[:, blocks:, :blocks]
    return jnp.stack([matrix_re, matrix_im], axis=1)


def general(codes, scales, weights, freq_indices):
    values = (codes.astype(jnp.float32) * scales[:, None]).astype(jnp.bfloat16)
    regrouped = lax.all_to_all(values, "tm", split_axis=1, concat_axis=0, tiled=True)
    point_count = regrouped.shape[1]
    own_weights = lax.dynamic_slice_in_dim(
        weights, lax.axis_index("tm") * point_count, point_count, 0
    )
    total_points = weights.shape[0] * lax.axis_size("pts")
    root_weight = jnp.sqrt(own_weights / total_points)
    cosine_table, sine_table = make_tables(freq_indices)
    hop_rows = regrouped.reshape(-1, NFFT // 2, point_count)
    windows = jnp.concatenate([hop_rows[:-1], hop_rows[1:]], axis=1)
    real_part = jnp.einsum("fn,bnp->fbp", cosine_table, windows, preferred_element_type=jnp.float32)
    imag_part = jnp.einsum("fn,bnp->fbp", sine_table, windows, preferred_element_type=jnp.float32)
    scaled_re = (real_part * root_weight[None, None, :]).astype(jnp.bfloat16)
    scaled_im = (imag_part * root_weight[None, None, :]).astype(jnp.bfloat16)
    stacked = jnp.concatenate([scaled_re, scaled_im], axis=1)
    partial_value = lax.psum_scatter(
        cross_matrices(stacked), "pts", scatter_dimension=0, tiled=True
    )
    return lax.psum(partial_value, "tm")


def solution(mesh):
    nt, np_ = mesh.shape["tm"], mesh.shape["pts"]

    def per_device(codes, scales, weights, freq_indices):
        rows, points = codes.shape
        fits = (
            nt == NT
            and np_ == 2 * NZ
            and freq_indices.shape[0] == 2 * nt * np_
            and points % LANES == 0
            and rows % (2 * NFFT) == NFFT + HALF
            and rows >= 16 * HOP
            and 4 * (rows // HOP) + 1 <= SLOTS
        )
        if fits:
            return fused(codes, scales, weights, freq_indices, points * np_)
        return general(codes, scales, weights, freq_indices)

    return jax.shard_map(
        per_device,
        mesh=mesh,
        in_specs=(P("tm", "pts"), P("tm"), P("pts"), P()),
        out_specs=P("pts", None, None, None),
        check_vma=False,
    )
```

```python
import functools
import math

import jax
import jax.numpy as jnp
from jax import lax
from jax.experimental import pallas as pl
from jax.experimental.pallas import tpu as pltpu
from jax.sharding import PartitionSpec as P

NFFT = 256
HOP = NFFT // 2
HALF = HOP // 2
LANES = 128
SLOTS = 96
KEPT = 72
NT = 4
NZ = 4
QUARTERS = 4
FULL = 3
ROW_PARTS = ((0, 72),)
PIECES = len(ROW_PARTS)
ZSETS = ((0, 3), (1, 2))
ORDERS = (
    ((0, 0), (0, 1), (3, 0), (3, 1)),
    ((1, 0), (1, 1), (2, 0), (2, 1)),
    ((0, 0), (0, 1), (3, 0), (3, 1)),
    ((1, 1), (2, 0), (1, 0), (2, 1)),
)
MESH = pl.DeviceIdType.MESH


def make_tables(freq_indices):
    sample = jnp.arange(NFFT, dtype=jnp.int32)
    phases = freq_indices[:, None] * sample[None, :] % NFFT
    angles = phases.astype(jnp.float32) * (2.0 * math.pi / NFFT)
    hann_window = 0.5 - 0.5 * jnp.cos(sample.astype(jnp.float32) * (2.0 * math.pi / NFFT))
    cosine_table = (0.25 * hann_window[None, :] * jnp.cos(angles)).astype(jnp.bfloat16)
    sine_table = (-0.25 * hann_window[None, :] * jnp.sin(angles)).astype(jnp.bfloat16)
    return (cosine_table, sine_table)


def turn_waves(turn):
    angle = turn.astype(jnp.float32) * (2.0 * math.pi / NFFT)
    quarter = (turn + NFFT // 8) // (NFFT // 4)
    count = quarter.astype(jnp.float32)
    x = ((angle - count * 1.5703125) - count * 4.837512969970703125e-4) - count * 7.549789948768648e-8
    y = x * x
    sine = x + x * y * (-1.0 / 6.0 + y * (1.0 / 120.0 + y * (-1.0 / 5040.0 + y * (1.0 / 362880.0))))
    cosine = 1.0 + y * (-0.5 + y * (1.0 / 24.0 + y * (-1.0 / 720.0 + y * (1.0 / 40320.0))))
    swap = quarter % 2 == 1
    low = jnp.where(swap, sine, cosine)
    high = jnp.where(swap, cosine, sine)
    return (
        jnp.where((quarter + 1) % 4 >= 2, -low, low),
        jnp.where(quarter % 4 >= 2, -high, high),
    )


def fold(matrix):
    lane = lax.broadcasted_iota(jnp.int32, (KEPT, LANES), 1)
    rest = jnp.zeros((LANES - (SLOTS - KEPT), LANES), jnp.float32)
    turned = jnp.concatenate([matrix[KEPT:], rest], axis=0).T
    corner = turned[KEPT:SLOTS]
    corners = jnp.concatenate([pltpu.roll(corner, LANES - 8 * m, 1) for m in (1, 2, 3)], axis=0)
    side = pltpu.roll(turned[:KEPT], SLOTS, 1)
    return jnp.where(lane < SLOTS, matrix[:KEPT], jnp.where(lane < LANES - 8, side, corners))


def unfold(folded):
    lane = lax.broadcasted_iota(jnp.int32, (KEPT, LANES), 1)
    top = jnp.where(lane < SLOTS, folded, 0.0)
    side = jnp.where(lane < SLOTS - KEPT, pltpu.roll(folded, LANES - SLOTS, 1), 0.0)
    size = SLOTS - KEPT
    corner = jnp.zeros((size, LANES), jnp.float32)
    for m in (1, 2, 3):
        moved = pltpu.roll(folded[(m - 1) * size:m * size], 8 * m, 1)
        here = lane[:size]
        corner = jnp.where((here >= 8 * m - 8) & (here < 8 * m), moved, corner)
    rest = jnp.zeros((LANES - SLOTS, LANES), jnp.float32)
    turned = jnp.concatenate([side, corner, rest], axis=0).T
    return jnp.concatenate([top, turned[:size]], axis=0)


def kernel(
    total_points,
    codes_hbm, scales_hbm, weights_hbm, freq_hbm, out_ref,
    codes_ref, scales_v, weights_v, freq_ref, spread, vals, table, sbuf, rbuf, sfirst, rfirst, slast, rlast, hops, spbuf, sprecv, stage,
    part, corebuf, summed, zbuf, part2, corebuf2, summed2, zbuf2, homebuf, gath,
    load_s, halo_s, halo_r, tm_s, tm_r, first_s, first_r, last_s, last_r, hop_s, hop_r, sp_s, sp_r, core_s, core_r, z_s, z_r, core2_s, core2_r, z2_s, z2_r, home_s, home_r, g_s, g_r,
):
    rows, points = codes_ref.shape
    t = lax.axis_index("tm")
    p = lax.axis_index("pts")
    z = p // 2
    c = p % 2
    odd = t % 2
    partner = p + 1 - 2 * c
    lane_tiles = points // LANES
    blocks = rows // HOP
    pairs = blocks // 2
    padded = rows + HALF

    early = (10 * HOP)
    late = rows - early - HALF
    edge_at = (1 - odd) * (rows - HALF)
    early_at = odd * (rows - early)
    late_at = odd * HALF + (1 - odd) * early

    def load(at, count, sem):
        at = pl.ds(pl.multiple_of(at, HALF), count)
        return pltpu.make_async_copy(codes_hbm.at[at], codes_ref.at[at], load_s.at[sem])

    load_scales = pltpu.make_async_copy(scales_hbm, scales_v, load_s.at[3])
    load_weights = pltpu.make_async_copy(weights_hbm, weights_v, load_s.at[4])
    load_freq = pltpu.make_async_copy(freq_hbm, freq_ref, load_s.at[5])
    load_edge = load(edge_at, HALF, 0)
    load_early = load(early_at, early, 1)
    load_late = load(late_at, late, 2)
    barrier = pltpu.get_barrier_semaphore()
    for d in range(1, NT):
        pl.semaphore_signal(barrier, inc=1, device_id=(t ^ d, p), device_id_type=MESH)
    pl.semaphore_signal(barrier, inc=1, device_id=(t, partner), device_id_type=MESH)
    for d in range(1, NZ):
        pl.semaphore_signal(barrier, inc=1, device_id=(t, (z + d) % NZ * 2 + c), device_id_type=MESH)
    load_freq.start()
    load_scales.start()
    load_edge.start()
    load_early.start()
    load_weights.start()
    load_late.start()

    sample = lax.broadcasted_iota(jnp.int32, (8, NFFT), 1)
    sub = lax.broadcasted_iota(jnp.int32, (8, NFFT), 0)
    window_shape = 0.25 * (0.5 - 0.5 * turn_waves(sample)[0])

    def octet_table(dest, q):
        bins = jnp.zeros((8, NFFT), jnp.int32)
        for j in range(4):
            dest_p = ORDERS[q][j][0] * 2 + ORDERS[q][j][1]
            bins = jnp.where(sub // 2 == j, freq_ref[dest_p * 2 * NT + dest * 2 + q // 2], bins)
        cosine, sine = turn_waves(bins * sample % NFFT)
        return window_shape * jnp.where(sub % 2 == 0, cosine, -sine)

    load_scales.wait()
    for g in range(-(-rows // HOP)):
        size = min(HOP, rows - g * HOP)
        line = scales_v[g * HOP:g * HOP + size].reshape(1, size)
        spread[g * HOP:g * HOP + size, :] = jnp.broadcast_to(line, (LANES, size)).T

    offset = odd * HALF

    def dequantize(i, carry):
        at = pl.ds(pl.multiple_of(i * HALF, HALF), HALF)
        to = pl.ds(pl.multiple_of(i * HALF + offset, HALF), HALF)
        scale = spread[at, :]
        for lane in range(lane_tiles):
            cols = slice(lane * LANES, (lane + 1) * LANES)
            vals[to, cols] = (codes_ref[at, cols].astype(jnp.float32) * scale).astype(jnp.bfloat16)
        return carry

    load_edge.wait()
    dequantize(edge_at // HALF, 0)
    halo_from = (1 - odd) * (rows - HALF) + odd * HALF
    halo_to = odd * rows
    halo_mine = (1 - odd) * rows

    def halo_copy(dst):
        return pltpu.make_async_remote_copy(
            src_ref=vals.at[pl.ds(pl.multiple_of(halo_from, HALF), HALF)],
            dst_ref=vals.at[pl.ds(pl.multiple_of(dst, HALF), HALF)],
            send_sem=halo_s, recv_sem=halo_r,
            device_id=(t ^ 1, p), device_id_type=MESH,
        )

    load_early.wait()
    lax.fori_loop(early_at // HALF, (early_at + early) // HALF, dequantize, 0)
    load_weights.wait()
    root_weight = jnp.sqrt(weights_v[...].reshape(1, points) / total_points)

    def spectrum(i):
        window = vals[pl.ds(pl.multiple_of(i * HOP, HOP), NFFT), :]
        return jnp.dot(table[...], window, preferred_element_type=jnp.float32) * root_weight

    def octets(result, dest, q):
        return result[dest * 32 + q * 8:dest * 32 + q * 8 + 8]

    def pair_tiles(jj, first, second):
        for dest in range(NT):
            for q in range(FULL):
                both = jnp.concatenate([octets(first, dest, q), octets(second, dest, q)], axis=0)
                sbuf[q, dest, jj] = both.astype(jnp.bfloat16)

    def spectra(u, carry):
        low = odd * (pairs - 2 - 2 * u) + (1 - odd) * 2 * u
        results = [spectrum(2 * low + r) for r in range(4)]
        pair_tiles(low, results[0], results[1])
        pair_tiles(low + 1, results[2], results[3])
        v = odd * (quads - 1 - u) + (1 - odd) * u
        for dest in range(NT):
            last = [octets(r, dest, FULL) for r in results]
            sfirst[dest, v] = jnp.concatenate([o[:4] for o in last], axis=0).astype(jnp.bfloat16)
            slast[dest, v] = jnp.concatenate([o[4:] for o in last], axis=0).astype(jnp.bfloat16)
        return carry

    def spectra_pair():
        jj = (1 - odd) * (pairs - 1)
        first, second = spectrum(2 * jj), spectrum(2 * jj + 1)
        pair_tiles(jj, first, second)
        for dest in range(NT):
            one, two = octets(first, dest, FULL), octets(second, dest, FULL)
            mixed = jnp.concatenate([one[:4], two[:4], one[4:], two[4:]], axis=0)
            sfirst[dest, quads] = mixed.astype(jnp.bfloat16)

    quads = pairs // 2
    q_cut = 1
    cuts = (0, 2 * q_cut, pairs - 1, pairs)
    partners = (3, 1, 2)

    def tiles_of(who, piece):
        count = cuts[piece + 1] - cuts[piece]
        flip = who % 2
        return flip * (pairs - cuts[piece + 1]) + (1 - flip) * cuts[piece], count

    def exchange(q, piece, d, source):
        at, count = tiles_of(source, piece)
        return pltpu.make_async_remote_copy(
            src_ref=sbuf.at[q, t ^ d, pl.ds(at, count)],
            dst_ref=rbuf.at[q, source, pl.ds(at, count)],
            send_sem=tm_s.at[q, piece, d - 1], recv_sem=tm_r.at[q, piece, d - 1],
            device_id=(t ^ d, p), device_id_type=MESH,
        )

    def exchange_first(d, source):
        return pltpu.make_async_remote_copy(
            src_ref=sfirst.at[t ^ d], dst_ref=rfirst.at[source],
            send_sem=first_s.at[d - 1], recv_sem=first_r.at[d - 1],
            device_id=(t ^ d, p), device_id_type=MESH,
        )

    last_cuts = (0, 4, quads)

    def exchange_last(piece, d, source):
        at = pl.ds(last_cuts[piece], last_cuts[piece + 1] - last_cuts[piece])
        return pltpu.make_async_remote_copy(
            src_ref=slast.at[t ^ d, at], dst_ref=rlast.at[source, at],
            send_sem=last_s.at[piece, d - 1], recv_sem=last_r.at[piece, d - 1],
            device_id=(t ^ d, p), device_id_type=MESH,
        )

    middle = (t == 1) | (t == 2)
    outer = (t == 0) | (t == 3)

    def owner(lane):
        if 2 * lane + 1 == lane_tiles:
            return (NT - 1) * (1 - c)
        return (NT - 1) * int(2 * lane + 1 > lane_tiles)

    def lanes(lane):
        return pl.ds(lane * LANES, LANES)

    def hop_copy(lane, source, dest):
        return pltpu.make_async_remote_copy(
            src_ref=vals.at[pl.ds(pl.multiple_of(odd * (padded - HOP), HOP), HOP), lanes(lane)],
            dst_ref=hops.at[pl.ds(pl.multiple_of((source - 1) * HOP, HOP), HOP), lanes(lane)],
            send_sem=hop_s.at[lane], recv_sem=hop_r.at[source - 1, lane],
            device_id=(dest, p), device_id_type=MESH,
        )

    def straddle(lane, d):
        return pltpu.make_async_remote_copy(
            src_ref=spbuf.at[t ^ d, :, :, lanes(lane)],
            dst_ref=sprecv.at[:, :, lanes(lane)],
            send_sem=sp_s.at[lane, d - 1], recv_sem=sp_r.at[lane],
            device_id=(t ^ d, p), device_id_type=MESH,
        )

    def send(q, piece):
        for d in partners:
            exchange(q, piece, d, t).start()


    pl.semaphore_wait(barrier, NT + NZ - 1)
    halo_copy(halo_to).start()

    @pl.when(middle)
    def _():
        for lane in range(lane_tiles):
            hop_copy(lane, t, owner(lane)).start()

    load_freq.wait()
    for dest in range(NT):
        for half in range(2):
            at = dest * 32 + half * 16
            pair = [octet_table(dest, 2 * half), octet_table(dest, 2 * half + 1)]
            table[at:at + 16, :] = jnp.concatenate(pair, axis=0).astype(jnp.bfloat16)

    lax.fori_loop(0, q_cut, spectra, 0)
    send(0, 0)
    load_late.wait()
    lax.fori_loop(late_at // HALF, (late_at + late) // HALF, dequantize, 0)
    lax.fori_loop(q_cut, quads, spectra, 0)
    send(0, 1)
    halo_copy(halo_mine).wait_recv()
    spectra_pair()
    send(0, 2)

    @pl.when(outer)
    def _():
        for lane in range(lane_tiles):
            @pl.when(t == owner(lane))
            def _():
                for source in (1, 2):
                    hop_copy(lane, source, owner(lane)).wait_recv()
        result = jnp.dot(table[...], hops[...], preferred_element_type=jnp.float32)
        result = (result * root_weight).astype(jnp.bfloat16)
        for dest in range(NT):
            for h in range(2):
                spbuf[dest, h] = result[dest * 32 + h * 16:dest * 32 + h * 16 + 16]
        for lane in range(lane_tiles):
            @pl.when(t == owner(lane))
            def _():
                for d in partners:
                    straddle(lane, d).start()
                sprecv[:, :, lanes(lane)] = spbuf[t, :, :, lanes(lane)]

    for piece in range(3):
        send(1, piece)

    for lane in range(lane_tiles):
        for s in range(8):
            stage[lane, s * SLOTS + SLOTS - 8:(s + 1) * SLOTS, :] = jnp.zeros((8, LANES), jnp.float32)

    def place(b, octet):
        for lane in range(lane_tiles):
            stage[lane, pl.ds(b, 8, stride=SLOTS), :] = octet[:, lane * LANES:(lane + 1) * LANES]

    def unpack(source_ref, q, who, piece):
        at, count = tiles_of(who, piece)
        base = who * blocks + who // 2

        def one(i, carry):
            tile = source_ref[q, who, i].astype(jnp.float32)
            place(base + 2 * i, tile[:8])
            place(base + 2 * i + 1, tile[8:])
            return carry

        lax.fori_loop(at, at + count, one, 0)

    def place_four(half, b, octet):
        for lane in range(lane_tiles):
            at = pl.ds(half * 4 * SLOTS + b, 4, stride=SLOTS)
            stage[lane, at, :] = octet[:, lane * LANES:(lane + 1) * LANES]

    def unpack_fours(source_ref, half, who, first, last):
        base = who * blocks + who // 2 + 2 * (who % 2)

        def one(v, carry):
            tile = source_ref[who, v].astype(jnp.float32)
            for r in range(4):
                place_four(half, base + 4 * v + r, tile[4 * r:4 * r + 4])
            return carry

        lax.fori_loop(first, last, one, 0)

    def unpack_mixed(source_ref, who):
        base = who * blocks + who // 2 + (1 - who % 2) * 2 * (pairs - 1)
        tile = source_ref[who, quads].astype(jnp.float32)
        for r in range(4):
            place_four(r // 2, base + r % 2, tile[4 * r:4 * r + 4])

    def gram(j):
        at = pl.ds(pl.multiple_of(j * 2 * SLOTS, 2 * SLOTS), 2 * SLOTS)
        stacked = jnp.concatenate(
            [stage[lane, at, :].astype(jnp.bfloat16) for lane in range(lane_tiles)], axis=1
        )
        fill = jnp.zeros((LANES - SLOTS, points), jnp.bfloat16)
        wide = jnp.concatenate([stacked[:SLOTS], fill, stacked[SLOTS:], fill], axis=0)
        prod = lax.dot_general(
            stacked, wide, (((1,), (1,)), ((), ())), preferred_element_type=jnp.float32
        )
        real = prod[:SLOTS, :LANES] + prod[SLOTS:, LANES:]
        imag = prod[:SLOTS, LANES:] - prod[SLOTS:, :LANES]
        return fold(real + imag)

    def rows_of(h):
        return pl.ds(*ROW_PARTS[h])

    def to_core(q, h):
        return pltpu.make_async_remote_copy(
            src_ref=part.at[q, 1 - c, :, rows_of(h)], dst_ref=corebuf.at[q, :, rows_of(h)],
            send_sem=core_s.at[q, h], recv_sem=core_r.at[q, h],
            device_id=(t, partner), device_id_type=MESH,
        )

    def to_z(q, s, h, source):
        return pltpu.make_async_remote_copy(
            src_ref=summed.at[q, s, rows_of(h)], dst_ref=zbuf.at[q, source, rows_of(h)],
            send_sem=z_s.at[q, s, h], recv_sem=z_r.at[q, source, h],
            device_id=(t, ZSETS[q % 2][s] * 2 + c), device_id_type=MESH,
        )

    def home_of(e):
        return (1 - e) * (2 - c) + e * (1 + c)

    def to_core2(e, h):
        return pltpu.make_async_remote_copy(
            src_ref=part2.at[e, 1 - c, rows_of(h)], dst_ref=corebuf2.at[e, rows_of(h)],
            send_sem=core2_s.at[e, h], recv_sem=core2_r.at[e, h],
            device_id=(t, partner), device_id_type=MESH,
        )

    def to_z2(h, source):
        return pltpu.make_async_remote_copy(
            src_ref=summed2.at[0, rows_of(h)], dst_ref=zbuf2.at[source, rows_of(h)],
            send_sem=z2_s.at[h], recv_sem=z2_r.at[source, h],
            device_id=(t, home_of(0) * 2 + c), device_id_type=MESH,
        )

    def to_home(d, source_z, source_t):
        return pltpu.make_async_remote_copy(
            src_ref=summed2.at[1], dst_ref=homebuf.at[source_z, source_t],
            send_sem=home_s.at[d], recv_sem=home_r.at[source_z, source_t],
            device_id=(t ^ d, home_of(1) * 2 + c), device_id_type=MESH,
        )

    def gram2(e, side):
        part2[e, side] = gram((1 - e) * (1 - side) + e * (2 + side))

    def core_sum2(e, h):
        to_core2(e, h).wait_recv()
        at = rows_of(h)
        summed2[e, at] = part2[e, c, at] + corebuf2[e, at]

    def core_stage2(h):
        core_sum2(0, h)

        @pl.when(z != home_of(0))
        def _():
            to_z2(h, z).start()

    def home_stage():
        for h in range(PIECES):
            core_sum2(1, h)
        for d in partners:
            to_home(d, z, t).start()

        @pl.when(z != home_of(1))
        def _():
            to_home(0, z, t).start()

    def z_stage2(h):
        @pl.when(z == home_of(0))
        def _():
            at = rows_of(h)
            total = summed2[0, at]
            for d in range(1, NZ):
                other = (z + d) % NZ
                to_z2(h, other).wait_recv()
                total = total + zbuf2[other, at]
            gath[t, 1, at] = total
            for d in partners:
                to_tm(1, h, d, t).start()

    def to_tm(k, h, d, source):
        return pltpu.make_async_remote_copy(
            src_ref=gath.at[source, k, rows_of(h)], dst_ref=gath.at[source, k, rows_of(h)],
            send_sem=g_s.at[k, h, d - 1], recv_sem=g_r.at[k, h, d - 1],
            device_id=(t ^ d, p), device_id_type=MESH,
        )

    def receive(q, pieces):
        for piece in pieces:
            for d in partners:
                exchange(q, piece, d, t ^ d).wait_recv()
                unpack(rbuf, q, t ^ d, piece)

    def own(q):
        for piece in range(3):
            unpack(sbuf, q, t, piece)

    def straddling(q):
        if q == 0:
            for lane in range(lane_tiles):
                @pl.when(t != owner(lane))
                def _():
                    straddle(lane, 1).wait_recv()
        at = q % 2 * 8
        place(2 * blocks, sprecv[q // 2].astype(jnp.float32)[at:at + 8])

    def core_stage(q, h):
        to_core(q, h).wait_recv()
        for s in range(2):
            at = rows_of(h)
            summed[q, s, at] = part[q, c, s, at] + corebuf[q, s, at]

            @pl.when(z != ZSETS[q % 2][s])
            def _():
                to_z(q, s, h, z).start()

    def at_home(q):
        return (z == ZSETS[q % 2][0]) | (z == ZSETS[q % 2][1])

    def z_stage(q, h):
        for s in range(2):
            home = ZSETS[q % 2][s]

            @pl.when(z == home)
            def _():
                at = rows_of(h)
                total = summed[q, s, at]
                for other in range(NZ):
                    if other != home:
                        to_z(q, s, h, other).wait_recv()
                        total = total + zbuf[q, other, at]
                gath[t, q // 2, at] = total

    def spread_result(q, h):
        @pl.when(at_home(q))
        def _():
            for d in partners:
                to_tm(q // 2, h, d, t).start()

    def send_first():
        for d in partners:
            exchange_first(d, t).start()

    def send_last():
        for piece in range(2):
            for d in partners:
                exchange_last(piece, d, t).start()

    for q in range(FULL):
        if q == 1:
            for piece in range(3):
                send(2, piece)
        if q == 2:
            send_first()
        own(q)
        receive(q, (0,))
        straddling(q)
        if q >= 1:
            for h in range(PIECES):
                z_stage(q - 1, h)
        receive(q, (1, 2))
        for s in range(2):
            part[q, 1 - c, s] = gram(2 * s + 1 - c)
        for h in range(PIECES):
            to_core(q, h).start()
        for s in range(2):
            part[q, c, s] = gram(2 * s + c)
        for h in range(PIECES):
            core_stage(q, h)

    send_last()
    unpack_fours(sfirst, 0, t, 0, quads)
    unpack_mixed(sfirst, t)
    unpack_fours(slast, 1, t, 0, quads)
    straddling(FULL)
    for d in partners:
        exchange_first(d, t ^ d).wait_recv()
        unpack_fours(rfirst, 0, t ^ d, 0, quads)
        unpack_mixed(rfirst, t ^ d)
    gram2(0, 1 - c)
    for h in range(PIECES):
        to_core2(0, h).start()
    gram2(0, c)
    for piece in range(2):
        for d in partners:
            exchange_last(piece, d, t ^ d).wait_recv()
            unpack_fours(rlast, 1, t ^ d, last_cuts[piece], last_cuts[piece + 1])
        if piece == 0:
            for h in range(PIECES):
                core_stage2(h)
                spread_result(0, h)
                spread_result(1, h)
    gram2(1, 1 - c)
    for h in range(PIECES):
        to_core2(1, h).start()
    gram2(1, c)
    home_stage()
    for h in range(PIECES):
        z_stage(2, h)
        spread_result(2, h)
    for h in range(PIECES):
        z_stage2(h)
    halo_copy(halo_to).wait_send()
    for d in partners:
        exchange_first(d, t).wait_send()
        for piece in range(2):
            exchange_last(piece, d, t).wait_send()
    for q in range(FULL):
        for piece in range(3):
            for d in partners:
                exchange(q, piece, d, t).wait_send()
        for h in range(PIECES):
            to_core(q, h).wait_send()
        for s in range(2):
            @pl.when(z != ZSETS[q % 2][s])
            def _():
                for h in range(PIECES):
                    to_z(q, s, h, z).wait_send()
    for lane in range(lane_tiles):
        @pl.when(middle)
        def _():
            hop_copy(lane, t, owner(lane)).wait_send()

        @pl.when(t == owner(lane))
        def _():
            for d in partners:
                straddle(lane, d).wait_send()

    for h in range(PIECES):
        to_core2(0, h).wait_send()

        @pl.when(z != home_of(0))
        def _():
            to_z2(h, z).wait_send()

        for d in partners:
            to_tm(0, h, d, t).wait_send()

    def gathered(k):
        out_ref[t * 2 + k] = unfold(gath[t, k])
        for d in (1, 2, 3):
            for h in range(PIECES):
                to_tm(k, h, d, t ^ d).wait_recv()
            out_ref[(t ^ d) * 2 + k] = unfold(gath[t ^ d, k])

    gathered(0)

    @pl.when(z != home_of(1))
    def _():
        gathered(1)
        for h in range(PIECES):
            for d in partners:
                to_tm(1, h, d, t).wait_send()

    @pl.when(z == home_of(1))
    def _():
        for d in range(NT):
            source = t ^ d
            if d == 0:
                total = summed2[1]
            else:
                to_home(d, z, source).wait_recv()
                total = homebuf[z, source]
            for step in range(1, NZ):
                other = (z + step) % NZ
                to_home(d, other, source).wait_recv()
                total = total + homebuf[other, source]
            out_ref[source * 2 + 1] = unfold(total)

    for h in range(PIECES):
        to_core2(1, h).wait_send()
    for d in partners:
        to_home(d, z, t).wait_send()

    @pl.when(z != home_of(1))
    def _():
        to_home(0, z, t).wait_send()


def finish(sums_ref, out_hbm, both, sems):
    freqs = sums_ref.shape[0]
    count = out_hbm.shape[1]

    def copy(part):
        size = freqs // 2 * 2 * count
        at = pl.ds(part * size, size)
        return pltpu.make_async_copy(both.at[at], out_hbm.at[at], sems.at[part])

    for part in range(2):
        for f in range(part * freqs // 2, (part + 1) * freqs // 2):
            ordered = sums_ref[f]
            fill = jnp.zeros((LANES - SLOTS, LANES), jnp.float32)
            mirrored = jnp.concatenate([ordered, fill], axis=0).T[:SLOTS]
            first = f * 2 * count
            both[pl.ds(first, count, stride=2), :] = 0.5 * (ordered + mirrored)[:count, :count]
            both[pl.ds(first + 1, count, stride=2), :] = 0.5 * (ordered - mirrored)[:count, :count]
        copy(part).start()
    for part in range(2):
        copy(part).wait()


def fused(codes, scales, weights, freq_indices, total_points):
    rows, points = codes.shape
    blocks = rows // HOP
    pairs = blocks // 2
    lane_tiles = points // LANES
    count = rows * NT // HOP - 1
    f32, bf16 = jnp.float32, jnp.bfloat16
    dma = pltpu.SemaphoreType.DMA
    hbm = pl.BlockSpec(memory_space=pltpu.HBM)
    vmem = pl.BlockSpec(memory_space=pltpu.VMEM)
    pinned = [
        pltpu.with_memory_space_constraint(x, pltpu.HBM) for x in (codes, scales, weights, freq_indices)
    ]
    sums = pl.pallas_call(
        functools.partial(kernel, total_points),
        out_shape=jax.ShapeDtypeStruct((2 * NT, SLOTS, LANES), f32),
        in_specs=[hbm, hbm, hbm, hbm],
        out_specs=vmem,
        scratch_shapes=[
            pltpu.VMEM((rows, points), bf16),
            pltpu.VMEM((rows,), f32),
            pltpu.VMEM((points,), f32),
            pltpu.SMEM(freq_indices.shape, jnp.int32),
            pltpu.VMEM((rows, LANES), f32),
            pltpu.VMEM((rows + HALF, points), bf16),
            pltpu.VMEM((2 * NT * QUARTERS * 4, NFFT), bf16),
            pltpu.VMEM((FULL, NT, pairs, 16, points), bf16),
            pltpu.VMEM((FULL, NT, pairs, 16, points), bf16),
            pltpu.VMEM((NT, pairs // 2 + 1, 16, points), bf16),
            pltpu.VMEM((NT, pairs // 2 + 1, 16, points), bf16),
            pltpu.VMEM((NT, pairs // 2, 16, points), bf16),
            pltpu.VMEM((NT, pairs // 2, 16, points), bf16),
            pltpu.VMEM((NFFT, points), bf16),
            pltpu.VMEM((NT, 2, 16, points), bf16),
            pltpu.VMEM((2, 16, points), bf16),
            pltpu.VMEM((points // LANES, 8 * SLOTS, LANES), f32),
            pltpu.VMEM((FULL, 2, 2, KEPT, LANES), f32),
            pltpu.VMEM((FULL, 2, KEPT, LANES), f32),
            pltpu.VMEM((FULL, 2, KEPT, LANES), f32),
            pltpu.VMEM((FULL, NZ, KEPT, LANES), f32),
            pltpu.VMEM((2, 2, KEPT, LANES), f32),
            pltpu.VMEM((2, KEPT, LANES), f32),
            pltpu.VMEM((2, KEPT, LANES), f32),
            pltpu.VMEM((NZ, KEPT, LANES), f32),
            pltpu.VMEM((NZ, NT, KEPT, LANES), f32),
            pltpu.VMEM((NT, 2, KEPT, LANES), f32),
            dma((6,)),
            dma, dma,
            dma((FULL, 3, NT - 1)), dma((FULL, 3, NT - 1)),
            dma((NT - 1,)), dma((NT - 1,)),
            dma((2, NT - 1)), dma((2, NT - 1)),
            dma((lane_tiles,)), dma((2, lane_tiles)),
            dma((lane_tiles, NT - 1)), dma((lane_tiles,)),
            dma((FULL, PIECES)), dma((FULL, PIECES)),
            dma((FULL, 2, PIECES)), dma((FULL, NZ, PIECES)),
            dma((2, PIECES)), dma((2, PIECES)),
            dma((PIECES,)), dma((NZ, PIECES)),
            dma((NT,)), dma((NZ, NT)),
            dma((2, PIECES, NT - 1)), dma((2, PIECES, NT - 1)),
        ],
        compiler_params=pltpu.CompilerParams(
            collective_id=0, has_side_effects=True, vmem_limit_bytes=40 * 2**20
        ),
        name="spectra_cross",
    )(*pinned)
    full = pl.pallas_call(
        finish,
        out_shape=jax.ShapeDtypeStruct((2 * NT * 2 * count, count), f32),
        in_specs=[vmem],
        out_specs=hbm,
        scratch_shapes=[pltpu.VMEM((2 * NT * 2 * count, count), f32), dma((2,))],
        name="hermitian_parts",
    )(pltpu.with_memory_space_constraint(sums, pltpu.VMEM))
    return full.reshape(2 * NT, count, 2, count).transpose(0, 2, 1, 3)


def cross_matrices(stacked):
    blocks = stacked.shape[1] // 2
    products = jnp.einsum("fip,fjp->fij", stacked, stacked, preferred_element_type=jnp.float32)
    matrix_re = products[:, :blocks, :blocks] + products[:, blocks:, blocks:]
    matrix_im = products[:, :blocks, blocks:] - products[:, blocks:, :blocks]
    return jnp.stack([matrix_re, matrix_im], axis=1)


def general(codes, scales, weights, freq_indices):
    values = (codes.astype(jnp.float32) * scales[:, None]).astype(jnp.bfloat16)
    regrouped = lax.all_to_all(values, "tm", split_axis=1, concat_axis=0, tiled=True)
    point_count = regrouped.shape[1]
    own_weights = lax.dynamic_slice_in_dim(
        weights, lax.axis_index("tm") * point_count, point_count, 0
    )
    total_points = weights.shape[0] * lax.axis_size("pts")
    root_weight = jnp.sqrt(own_weights / total_points)
    cosine_table, sine_table = make_tables(freq_indices)
    hop_rows = regrouped.reshape(-1, NFFT // 2, point_count)
    windows = jnp.concatenate([hop_rows[:-1], hop_rows[1:]], axis=1)
    real_part = jnp.einsum("fn,bnp->fbp", cosine_table, windows, preferred_element_type=jnp.float32)
    imag_part = jnp.einsum("fn,bnp->fbp", sine_table, windows, preferred_element_type=jnp.float32)
    scaled_re = (real_part * root_weight[None, None, :]).astype(jnp.bfloat16)
    scaled_im = (imag_part * root_weight[None, None, :]).astype(jnp.bfloat16)
    stacked = jnp.concatenate([scaled_re, scaled_im], axis=1)
    partial_value = lax.psum_scatter(
        cross_matrices(stacked), "pts", scatter_dimension=0, tiled=True
    )
    return lax.psum(partial_value, "tm")


def solution(mesh):
    nt, np_ = mesh.shape["tm"], mesh.shape["pts"]

    def per_device(codes, scales, weights, freq_indices):
        rows, points = codes.shape
        fits = (
            nt == NT
            and np_ == 2 * NZ
            and freq_indices.shape[0] == 2 * nt * np_
            and points % LANES == 0
            and rows % (2 * NFFT) == NFFT + HALF
            and rows >= 16 * HOP
            and 4 * (rows // HOP) + 1 <= SLOTS
        )
        if fits:
            return fused(codes, scales, weights, freq_indices, points * np_)
        return general(codes, scales, weights, freq_indices)

    return jax.shard_map(
        per_device,
        mesh=mesh,
        in_specs=(P("tm", "pts"), P("tm"), P("pts"), P()),
        out_specs=P("pts", None, None, None),
        check_vma=False,
    )
```

```python
import functools
import math

import jax
import jax.numpy as jnp
from jax import lax
from jax.experimental import pallas as pl
from jax.experimental.pallas import tpu as pltpu
from jax.sharding import PartitionSpec as P

NFFT = 256
HOP = NFFT // 2
HALF = HOP // 2
LANES = 128
SLOTS = 96
KEPT = 64
SPAN = 89
NT = 4
NZ = 4
QUARTERS = 4
FULL = 3
ROW_PARTS = ((0, 64),)
PIECES = len(ROW_PARTS)
ZSETS = ((0, 3), (1, 2))
ORDERS = (
    ((0, 0), (0, 1), (3, 0), (3, 1)),
    ((1, 0), (1, 1), (2, 0), (2, 1)),
    ((0, 0), (0, 1), (3, 0), (3, 1)),
    ((1, 1), (2, 0), (1, 0), (2, 1)),
)
MESH = pl.DeviceIdType.MESH


def make_tables(freq_indices):
    sample = jnp.arange(NFFT, dtype=jnp.int32)
    phases = freq_indices[:, None] * sample[None, :] % NFFT
    angles = phases.astype(jnp.float32) * (2.0 * math.pi / NFFT)
    hann_window = 0.5 - 0.5 * jnp.cos(sample.astype(jnp.float32) * (2.0 * math.pi / NFFT))
    cosine_table = (0.25 * hann_window[None, :] * jnp.cos(angles)).astype(jnp.bfloat16)
    sine_table = (-0.25 * hann_window[None, :] * jnp.sin(angles)).astype(jnp.bfloat16)
    return (cosine_table, sine_table)


def turn_waves(turn):
    angle = turn.astype(jnp.float32) * (2.0 * math.pi / NFFT)
    quarter = (turn + NFFT // 8) // (NFFT // 4)
    count = quarter.astype(jnp.float32)
    x = ((angle - count * 1.5703125) - count * 4.837512969970703125e-4) - count * 7.549789948768648e-8
    y = x * x
    sine = x + x * y * (-1.0 / 6.0 + y * (1.0 / 120.0 + y * (-1.0 / 5040.0 + y * (1.0 / 362880.0))))
    cosine = 1.0 + y * (-0.5 + y * (1.0 / 24.0 + y * (-1.0 / 720.0 + y * (1.0 / 40320.0))))
    swap = quarter % 2 == 1
    low = jnp.where(swap, sine, cosine)
    high = jnp.where(swap, cosine, sine)
    return (
        jnp.where((quarter + 1) % 4 >= 2, -low, low),
        jnp.where(quarter % 4 >= 2, -high, high),
    )


def fold(matrix):
    lane = lax.broadcasted_iota(jnp.int32, (KEPT, LANES), 1)
    size = SLOTS - KEPT
    first = 2 * SPAN - KEPT
    rest = jnp.zeros((LANES - size, LANES), jnp.float32)
    turned = jnp.concatenate([matrix[KEPT:], rest], axis=0).T
    corner = turned[KEPT:SLOTS]
    corners = jnp.concatenate(
        [pltpu.roll(corner, first, 1), pltpu.roll(corner, 2 * first - LANES, 1)], axis=0
    )
    side = pltpu.roll(turned[:KEPT], SPAN, 1)
    return jnp.where(lane < SPAN, matrix[:KEPT], jnp.where(lane < first, side, corners))


def unfold(folded):
    lane = lax.broadcasted_iota(jnp.int32, (KEPT, LANES), 1)
    size = SLOTS - KEPT
    here = lane[:size]
    wide = LANES - (2 * SPAN - KEPT)
    top = jnp.where(lane < SPAN, folded, 0.0)
    side = jnp.where(lane < SPAN - KEPT, pltpu.roll(folded, LANES - SPAN, 1), 0.0)
    corner = jnp.where(
        here < wide, pltpu.roll(folded[:size], wide, 1), pltpu.roll(folded[size:], 2 * wide, 1)
    )
    corner = jnp.where(here < SPAN - KEPT, corner, 0.0)
    rest = jnp.zeros((LANES - SLOTS, LANES), jnp.float32)
    turned = jnp.concatenate([side, corner, rest], axis=0).T
    return jnp.concatenate([top, turned[:size]], axis=0)


def kernel(
    total_points,
    codes_hbm, scales_hbm, weights_hbm, freq_hbm, out_ref,
    codes_ref, scales_v, weights_v, freq_ref, spread, vals, table, sbuf, rbuf, sfirst, rfirst, slast, rlast, hops, spbuf, sprecv, stage,
    part, corebuf, summed, zbuf, part2, corebuf2, summed2, zbuf2, homebuf, gath,
    load_s, halo_s, halo_r, tm_s, tm_r, first_s, first_r, last_s, last_r, hop_s, hop_r, sp_s, sp_r, core_s, core_r, z_s, z_r, core2_s, core2_r, z2_s, z2_r, home_s, home_r, g_s, g_r,
):
    rows, points = codes_ref.shape
    t = lax.axis_index("tm")
    p = lax.axis_index("pts")
    z = p // 2
    c = p % 2
    odd = t % 2
    partner = p + 1 - 2 * c
    lane_tiles = points // LANES
    blocks = rows // HOP
    pairs = blocks // 2
    padded = rows + HALF

    early = (10 * HOP)
    late = rows - early - HALF
    edge_at = (1 - odd) * (rows - HALF)
    early_at = odd * (rows - early)
    late_at = odd * HALF + (1 - odd) * early

    def load(at, count, sem):
        at = pl.ds(pl.multiple_of(at, HALF), count)
        return pltpu.make_async_copy(codes_hbm.at[at], codes_ref.at[at], load_s.at[sem])

    load_scales = pltpu.make_async_copy(scales_hbm, scales_v, load_s.at[3])
    load_weights = pltpu.make_async_copy(weights_hbm, weights_v, load_s.at[4])
    load_freq = pltpu.make_async_copy(freq_hbm, freq_ref, load_s.at[5])
    load_edge = load(edge_at, HALF, 0)
    load_early = load(early_at, early, 1)
    load_late = load(late_at, late, 2)
    barrier = pltpu.get_barrier_semaphore()
    for d in range(1, NT):
        pl.semaphore_signal(barrier, inc=1, device_id=(t ^ d, p), device_id_type=MESH)
    pl.semaphore_signal(barrier, inc=1, device_id=(t, partner), device_id_type=MESH)
    for d in range(1, NZ):
        pl.semaphore_signal(barrier, inc=1, device_id=(t, (z + d) % NZ * 2 + c), device_id_type=MESH)
    load_freq.start()
    load_scales.start()
    load_edge.start()
    load_early.start()
    load_weights.start()
    load_late.start()

    sample = lax.broadcasted_iota(jnp.int32, (8, NFFT), 1)
    sub = lax.broadcasted_iota(jnp.int32, (8, NFFT), 0)
    window_shape = 0.25 * (0.5 - 0.5 * turn_waves(sample)[0])

    def octet_table(dest, q):
        bins = jnp.zeros((8, NFFT), jnp.int32)
        for j in range(4):
            dest_p = ORDERS[q][j][0] * 2 + ORDERS[q][j][1]
            bins = jnp.where(sub // 2 == j, freq_ref[dest_p * 2 * NT + dest * 2 + q // 2], bins)
        cosine, sine = turn_waves(bins * sample % NFFT)
        return window_shape * jnp.where(sub % 2 == 0, cosine, -sine)

    load_scales.wait()
    for g in range(-(-rows // HOP)):
        size = min(HOP, rows - g * HOP)
        line = scales_v[g * HOP:g * HOP + size].reshape(1, size)
        spread[g * HOP:g * HOP + size, :] = jnp.broadcast_to(line, (LANES, size)).T

    offset = odd * HALF

    def dequantize(i, carry):
        at = pl.ds(pl.multiple_of(i * HALF, HALF), HALF)
        to = pl.ds(pl.multiple_of(i * HALF + offset, HALF), HALF)
        scale = spread[at, :]
        for lane in range(lane_tiles):
            cols = slice(lane * LANES, (lane + 1) * LANES)
            vals[to, cols] = (codes_ref[at, cols].astype(jnp.float32) * scale).astype(jnp.bfloat16)
        return carry

    load_edge.wait()
    dequantize(edge_at // HALF, 0)
    halo_from = (1 - odd) * (rows - HALF) + odd * HALF
    halo_to = odd * rows
    halo_mine = (1 - odd) * rows

    def halo_copy(dst):
        return pltpu.make_async_remote_copy(
            src_ref=vals.at[pl.ds(pl.multiple_of(halo_from, HALF), HALF)],
            dst_ref=vals.at[pl.ds(pl.multiple_of(dst, HALF), HALF)],
            send_sem=halo_s, recv_sem=halo_r,
            device_id=(t ^ 1, p), device_id_type=MESH,
        )

    load_early.wait()
    lax.fori_loop(early_at // HALF, (early_at + early) // HALF, dequantize, 0)
    load_weights.wait()
    root_weight = jnp.sqrt(weights_v[...].reshape(1, points) / total_points)

    def spectrum(i):
        window = vals[pl.ds(pl.multiple_of(i * HOP, HOP), NFFT), :]
        return jnp.dot(table[...], window, preferred_element_type=jnp.float32) * root_weight

    def octets(result, dest, q):
        return result[dest * 32 + q * 8:dest * 32 + q * 8 + 8]

    def pair_tiles(jj, first, second):
        for dest in range(NT):
            for q in range(FULL):
                both = jnp.concatenate([octets(first, dest, q), octets(second, dest, q)], axis=0)
                sbuf[q, dest, jj] = both.astype(jnp.bfloat16)

    def spectra(u, carry):
        low = odd * (pairs - 2 - 2 * u) + (1 - odd) * 2 * u
        results = [spectrum(2 * low + r) for r in range(4)]
        pair_tiles(low, results[0], results[1])
        pair_tiles(low + 1, results[2], results[3])
        v = odd * (quads - 1 - u) + (1 - odd) * u
        for dest in range(NT):
            last = [octets(r, dest, FULL) for r in results]
            sfirst[dest, v] = jnp.concatenate([o[:4] for o in last], axis=0).astype(jnp.bfloat16)
            slast[dest, v] = jnp.concatenate([o[4:] for o in last], axis=0).astype(jnp.bfloat16)
        return carry

    def spectra_pair():
        jj = (1 - odd) * (pairs - 1)
        first, second = spectrum(2 * jj), spectrum(2 * jj + 1)
        pair_tiles(jj, first, second)
        for dest in range(NT):
            one, two = octets(first, dest, FULL), octets(second, dest, FULL)
            mixed = jnp.concatenate([one[:4], two[:4], one[4:], two[4:]], axis=0)
            sfirst[dest, quads] = mixed.astype(jnp.bfloat16)

    quads = pairs // 2
    q_cut = 1
    cuts = (0, 2 * q_cut, pairs - 1, pairs)
    partners = (3, 1, 2)

    def tiles_of(who, piece):
        count = cuts[piece + 1] - cuts[piece]
        flip = who % 2
        return flip * (pairs - cuts[piece + 1]) + (1 - flip) * cuts[piece], count

    def exchange(q, piece, d, source):
        at, count = tiles_of(source, piece)
        return pltpu.make_async_remote_copy(
            src_ref=sbuf.at[q, t ^ d, pl.ds(at, count)],
            dst_ref=rbuf.at[q, source, pl.ds(at, count)],
            send_sem=tm_s.at[q, piece, d - 1], recv_sem=tm_r.at[q, piece, d - 1],
            device_id=(t ^ d, p), device_id_type=MESH,
        )

    def exchange_first(d, source):
        return pltpu.make_async_remote_copy(
            src_ref=sfirst.at[t ^ d], dst_ref=rfirst.at[source],
            send_sem=first_s.at[d - 1], recv_sem=first_r.at[d - 1],
            device_id=(t ^ d, p), device_id_type=MESH,
        )

    last_cuts = (0, 4, quads)

    def exchange_last(piece, d, source):
        at = pl.ds(last_cuts[piece], last_cuts[piece + 1] - last_cuts[piece])
        return pltpu.make_async_remote_copy(
            src_ref=slast.at[t ^ d, at], dst_ref=rlast.at[source, at],
            send_sem=last_s.at[piece, d - 1], recv_sem=last_r.at[piece, d - 1],
            device_id=(t ^ d, p), device_id_type=MESH,
        )

    middle = (t == 1) | (t == 2)
    outer = (t == 0) | (t == 3)

    def owner(lane):
        if 2 * lane + 1 == lane_tiles:
            return (NT - 1) * (1 - c)
        return (NT - 1) * int(2 * lane + 1 > lane_tiles)

    def lanes(lane):
        return pl.ds(lane * LANES, LANES)

    def hop_copy(lane, source, dest):
        return pltpu.make_async_remote_copy(
            src_ref=vals.at[pl.ds(pl.multiple_of(odd * (padded - HOP), HOP), HOP), lanes(lane)],
            dst_ref=hops.at[pl.ds(pl.multiple_of((source - 1) * HOP, HOP), HOP), lanes(lane)],
            send_sem=hop_s.at[lane], recv_sem=hop_r.at[source - 1, lane],
            device_id=(dest, p), device_id_type=MESH,
        )

    def straddle(lane, d):
        return pltpu.make_async_remote_copy(
            src_ref=spbuf.at[t ^ d, :, :, lanes(lane)],
            dst_ref=sprecv.at[:, :, lanes(lane)],
            send_sem=sp_s.at[lane, d - 1], recv_sem=sp_r.at[lane],
            device_id=(t ^ d, p), device_id_type=MESH,
        )

    def send(q, piece):
        for d in partners:
            exchange(q, piece, d, t).start()


    pl.semaphore_wait(barrier, NT + NZ - 1)
    halo_copy(halo_to).start()

    @pl.when(middle)
    def _():
        for lane in range(lane_tiles):
            hop_copy(lane, t, owner(lane)).start()

    load_freq.wait()
    for dest in range(NT):
        for half in range(2):
            at = dest * 32 + half * 16
            pair = [octet_table(dest, 2 * half), octet_table(dest, 2 * half + 1)]
            table[at:at + 16, :] = jnp.concatenate(pair, axis=0).astype(jnp.bfloat16)

    lax.fori_loop(0, q_cut, spectra, 0)
    send(0, 0)
    load_late.wait()
    lax.fori_loop(late_at // HALF, (late_at + late) // HALF, dequantize, 0)
    lax.fori_loop(q_cut, quads, spectra, 0)
    send(0, 1)
    halo_copy(halo_mine).wait_recv()
    spectra_pair()
    send(0, 2)

    @pl.when(outer)
    def _():
        for lane in range(lane_tiles):
            @pl.when(t == owner(lane))
            def _():
                for source in (1, 2):
                    hop_copy(lane, source, owner(lane)).wait_recv()
        result = jnp.dot(table[...], hops[...], preferred_element_type=jnp.float32)
        result = (result * root_weight).astype(jnp.bfloat16)
        for dest in range(NT):
            for h in range(2):
                spbuf[dest, h] = result[dest * 32 + h * 16:dest * 32 + h * 16 + 16]
        for lane in range(lane_tiles):
            @pl.when(t == owner(lane))
            def _():
                for d in partners:
                    straddle(lane, d).start()
                sprecv[:, :, lanes(lane)] = spbuf[t, :, :, lanes(lane)]

    for piece in range(3):
        send(1, piece)

    for lane in range(lane_tiles):
        for s in range(8):
            stage[lane, s * SLOTS + SLOTS - 8:(s + 1) * SLOTS, :] = jnp.zeros((8, LANES), jnp.float32)

    def place(b, octet):
        for lane in range(lane_tiles):
            stage[lane, pl.ds(b, 8, stride=SLOTS), :] = octet[:, lane * LANES:(lane + 1) * LANES]

    def unpack(source_ref, q, who, piece):
        at, count = tiles_of(who, piece)
        base = who * blocks + who // 2

        def one(i, carry):
            tile = source_ref[q, who, i].astype(jnp.float32)
            place(base + 2 * i, tile[:8])
            place(base + 2 * i + 1, tile[8:])
            return carry

        lax.fori_loop(at, at + count, one, 0)

    def place_four(half, b, octet):
        for lane in range(lane_tiles):
            at = pl.ds(half * 4 * SLOTS + b, 4, stride=SLOTS)
            stage[lane, at, :] = octet[:, lane * LANES:(lane + 1) * LANES]

    def unpack_fours(source_ref, half, who, first, last):
        base = who * blocks + who // 2 + 2 * (who % 2)

        def one(v, carry):
            tile = source_ref[who, v].astype(jnp.float32)
            for r in range(4):
                place_four(half, base + 4 * v + r, tile[4 * r:4 * r + 4])
            return carry

        lax.fori_loop(first, last, one, 0)

    def unpack_mixed(source_ref, who):
        base = who * blocks + who // 2 + (1 - who % 2) * 2 * (pairs - 1)
        tile = source_ref[who, quads].astype(jnp.float32)
        for r in range(4):
            place_four(r // 2, base + r % 2, tile[4 * r:4 * r + 4])

    def gram(j):
        at = pl.ds(pl.multiple_of(j * 2 * SLOTS, 2 * SLOTS), 2 * SLOTS)
        stacked = jnp.concatenate(
            [stage[lane, at, :].astype(jnp.bfloat16) for lane in range(lane_tiles)], axis=1
        )
        fill = jnp.zeros((LANES - SLOTS, points), jnp.bfloat16)
        wide = jnp.concatenate([stacked[:SLOTS], fill, stacked[SLOTS:], fill], axis=0)
        prod = lax.dot_general(
            stacked, wide, (((1,), (1,)), ((), ())), preferred_element_type=jnp.float32
        )
        real = prod[:SLOTS, :LANES] + prod[SLOTS:, LANES:]
        imag = prod[:SLOTS, LANES:] - prod[SLOTS:, :LANES]
        return fold(real + imag)

    def rows_of(h):
        return pl.ds(*ROW_PARTS[h])

    def to_core(q, h):
        return pltpu.make_async_remote_copy(
            src_ref=part.at[q, 1 - c, :, rows_of(h)], dst_ref=corebuf.at[q, :, rows_of(h)],
            send_sem=core_s.at[q, h], recv_sem=core_r.at[q, h],
            device_id=(t, partner), device_id_type=MESH,
        )

    def to_z(q, s, h, source):
        return pltpu.make_async_remote_copy(
            src_ref=summed.at[q, s, rows_of(h)], dst_ref=zbuf.at[q, source, rows_of(h)],
            send_sem=z_s.at[q, s, h], recv_sem=z_r.at[q, source, h],
            device_id=(t, ZSETS[q % 2][s] * 2 + c), device_id_type=MESH,
        )

    def home_of(e):
        return (1 - e) * (2 - c) + e * (1 + c)

    def to_core2(e, h):
        return pltpu.make_async_remote_copy(
            src_ref=part2.at[e, 1 - c, rows_of(h)], dst_ref=corebuf2.at[e, rows_of(h)],
            send_sem=core2_s.at[e, h], recv_sem=core2_r.at[e, h],
            device_id=(t, partner), device_id_type=MESH,
        )

    def to_z2(h, source):
        return pltpu.make_async_remote_copy(
            src_ref=summed2.at[0, rows_of(h)], dst_ref=zbuf2.at[source, rows_of(h)],
            send_sem=z2_s.at[h], recv_sem=z2_r.at[source, h],
            device_id=(t, home_of(0) * 2 + c), device_id_type=MESH,
        )

    def to_home(d, source_z, source_t):
        return pltpu.make_async_remote_copy(
            src_ref=summed2.at[1], dst_ref=homebuf.at[source_z, source_t],
            send_sem=home_s.at[d], recv_sem=home_r.at[source_z, source_t],
            device_id=(t ^ d, home_of(1) * 2 + c), device_id_type=MESH,
        )

    def gram2(e, side):
        part2[e, side] = gram((1 - e) * (1 - side) + e * (2 + side))

    def core_sum2(e, h):
        to_core2(e, h).wait_recv()
        at = rows_of(h)
        summed2[e, at] = part2[e, c, at] + corebuf2[e, at]

    def core_stage2(h):
        core_sum2(0, h)

        @pl.when(z != home_of(0))
        def _():
            to_z2(h, z).start()

    def home_stage():
        for h in range(PIECES):
            core_sum2(1, h)
        for d in partners:
            to_home(d, z, t).start()

        @pl.when(z != home_of(1))
        def _():
            to_home(0, z, t).start()

    def z_stage2(h):
        @pl.when(z == home_of(0))
        def _():
            at = rows_of(h)
            total = summed2[0, at]
            for d in range(1, NZ):
                other = (z + d) % NZ
                to_z2(h, other).wait_recv()
                total = total + zbuf2[other, at]
            gath[t, 1, at] = total
            for d in partners:
                to_tm(1, h, d, t).start()

    def to_tm(k, h, d, source):
        return pltpu.make_async_remote_copy(
            src_ref=gath.at[source, k, rows_of(h)], dst_ref=gath.at[source, k, rows_of(h)],
            send_sem=g_s.at[k, h, d - 1], recv_sem=g_r.at[k, h, d - 1],
            device_id=(t ^ d, p), device_id_type=MESH,
        )

    def receive(q, pieces):
        for piece in pieces:
            for d in partners:
                exchange(q, piece, d, t ^ d).wait_recv()
                unpack(rbuf, q, t ^ d, piece)

    def own(q):
        for piece in range(3):
            unpack(sbuf, q, t, piece)

    def straddling(q):
        if q == 0:
            for lane in range(lane_tiles):
                @pl.when(t != owner(lane))
                def _():
                    straddle(lane, 1).wait_recv()
        at = q % 2 * 8
        place(2 * blocks, sprecv[q // 2].astype(jnp.float32)[at:at + 8])

    def core_stage(q, h):
        to_core(q, h).wait_recv()
        for s in range(2):
            at = rows_of(h)
            summed[q, s, at] = part[q, c, s, at] + corebuf[q, s, at]

            @pl.when(z != ZSETS[q % 2][s])
            def _():
                to_z(q, s, h, z).start()

    def at_home(q):
        return (z == ZSETS[q % 2][0]) | (z == ZSETS[q % 2][1])

    def z_stage(q, h):
        for s in range(2):
            home = ZSETS[q % 2][s]

            @pl.when(z == home)
            def _():
                at = rows_of(h)
                total = summed[q, s, at]
                for other in range(NZ):
                    if other != home:
                        to_z(q, s, h, other).wait_recv()
                        total = total + zbuf[q, other, at]
                gath[t, q // 2, at] = total

    def spread_result(q, h):
        @pl.when(at_home(q))
        def _():
            for d in partners:
                to_tm(q // 2, h, d, t).start()

    def send_first():
        for d in partners:
            exchange_first(d, t).start()

    def send_last():
        for piece in range(2):
            for d in partners:
                exchange_last(piece, d, t).start()

    for q in range(FULL):
        if q == 1:
            for piece in range(3):
                send(2, piece)
        if q == 2:
            send_first()
        own(q)
        receive(q, (0,))
        straddling(q)
        if q >= 1:
            for h in range(PIECES):
                z_stage(q - 1, h)
        receive(q, (1, 2))
        for s in range(2):
            part[q, 1 - c, s] = gram(2 * s + 1 - c)
        for h in range(PIECES):
            to_core(q, h).start()
        for s in range(2):
            part[q, c, s] = gram(2 * s + c)
        for h in range(PIECES):
            core_stage(q, h)

    send_last()
    unpack_fours(sfirst, 0, t, 0, quads)
    unpack_mixed(sfirst, t)
    unpack_fours(slast, 1, t, 0, quads)
    straddling(FULL)
    for d in partners:
        exchange_first(d, t ^ d).wait_recv()
        unpack_fours(rfirst, 0, t ^ d, 0, quads)
        unpack_mixed(rfirst, t ^ d)
    gram2(0, 1 - c)
    for h in range(PIECES):
        to_core2(0, h).start()
    gram2(0, c)
    for piece in range(2):
        for d in partners:
            exchange_last(piece, d, t ^ d).wait_recv()
            unpack_fours(rlast, 1, t ^ d, last_cuts[piece], last_cuts[piece + 1])
        if piece == 0:
            for h in range(PIECES):
                core_stage2(h)
                spread_result(0, h)
                spread_result(1, h)
    gram2(1, 1 - c)
    for h in range(PIECES):
        to_core2(1, h).start()
    gram2(1, c)
    home_stage()
    for h in range(PIECES):
        z_stage(2, h)
        spread_result(2, h)
    for h in range(PIECES):
        z_stage2(h)
    halo_copy(halo_to).wait_send()
    for d in partners:
        exchange_first(d, t).wait_send()
        for piece in range(2):
            exchange_last(piece, d, t).wait_send()
    for q in range(FULL):
        for piece in range(3):
            for d in partners:
                exchange(q, piece, d, t).wait_send()
        for h in range(PIECES):
            to_core(q, h).wait_send()
        for s in range(2):
            @pl.when(z != ZSETS[q % 2][s])
            def _():
                for h in range(PIECES):
                    to_z(q, s, h, z).wait_send()
    for lane in range(lane_tiles):
        @pl.when(middle)
        def _():
            hop_copy(lane, t, owner(lane)).wait_send()

        @pl.when(t == owner(lane))
        def _():
            for d in partners:
                straddle(lane, d).wait_send()

    for h in range(PIECES):
        to_core2(0, h).wait_send()

        @pl.when(z != home_of(0))
        def _():
            to_z2(h, z).wait_send()

        for d in partners:
            to_tm(0, h, d, t).wait_send()

    def gathered(k):
        out_ref[t * 2 + k] = unfold(gath[t, k])
        for d in (1, 2, 3):
            for h in range(PIECES):
                to_tm(k, h, d, t ^ d).wait_recv()
            out_ref[(t ^ d) * 2 + k] = unfold(gath[t ^ d, k])

    gathered(0)

    @pl.when(z != home_of(1))
    def _():
        gathered(1)
        for h in range(PIECES):
            for d in partners:
                to_tm(1, h, d, t).wait_send()

    @pl.when(z == home_of(1))
    def _():
        for d in range(NT):
            source = t ^ d
            if d == 0:
                total = summed2[1]
            else:
                to_home(d, z, source).wait_recv()
                total = homebuf[z, source]
            for step in range(1, NZ):
                other = (z + step) % NZ
                to_home(d, other, source).wait_recv()
                total = total + homebuf[other, source]
            out_ref[source * 2 + 1] = unfold(total)

    for h in range(PIECES):
        to_core2(1, h).wait_send()
    for d in partners:
        to_home(d, z, t).wait_send()

    @pl.when(z != home_of(1))
    def _():
        to_home(0, z, t).wait_send()


def finish(sums_ref, out_hbm, both, sems):
    freqs = sums_ref.shape[0]
    count = out_hbm.shape[1]

    def copy(part):
        size = freqs // 2 * 2 * count
        at = pl.ds(part * size, size)
        return pltpu.make_async_copy(both.at[at], out_hbm.at[at], sems.at[part])

    for part in range(2):
        for f in range(part * freqs // 2, (part + 1) * freqs // 2):
            ordered = sums_ref[f]
            fill = jnp.zeros((LANES - SLOTS, LANES), jnp.float32)
            mirrored = jnp.concatenate([ordered, fill], axis=0).T[:SLOTS]
            first = f * 2 * count
            both[pl.ds(first, count, stride=2), :] = 0.5 * (ordered + mirrored)[:count, :count]
            both[pl.ds(first + 1, count, stride=2), :] = 0.5 * (ordered - mirrored)[:count, :count]
        copy(part).start()
    for part in range(2):
        copy(part).wait()


def fused(codes, scales, weights, freq_indices, total_points):
    rows, points = codes.shape
    blocks = rows // HOP
    pairs = blocks // 2
    lane_tiles = points // LANES
    count = rows * NT // HOP - 1
    f32, bf16 = jnp.float32, jnp.bfloat16
    dma = pltpu.SemaphoreType.DMA
    hbm = pl.BlockSpec(memory_space=pltpu.HBM)
    vmem = pl.BlockSpec(memory_space=pltpu.VMEM)
    pinned = [
        pltpu.with_memory_space_constraint(x, pltpu.HBM) for x in (codes, scales, weights, freq_indices)
    ]
    sums = pl.pallas_call(
        functools.partial(kernel, total_points),
        out_shape=jax.ShapeDtypeStruct((2 * NT, SLOTS, LANES), f32),
        in_specs=[hbm, hbm, hbm, hbm],
        out_specs=vmem,
        scratch_shapes=[
            pltpu.VMEM((rows, points), bf16),
            pltpu.VMEM((rows,), f32),
            pltpu.VMEM((points,), f32),
            pltpu.SMEM(freq_indices.shape, jnp.int32),
            pltpu.VMEM((rows, LANES), f32),
            pltpu.VMEM((rows + HALF, points), bf16),
            pltpu.VMEM((2 * NT * QUARTERS * 4, NFFT), bf16),
            pltpu.VMEM((FULL, NT, pairs, 16, points), bf16),
            pltpu.VMEM((FULL, NT, pairs, 16, points), bf16),
            pltpu.VMEM((NT, pairs // 2 + 1, 16, points), bf16),
            pltpu.VMEM((NT, pairs // 2 + 1, 16, points), bf16),
            pltpu.VMEM((NT, pairs // 2, 16, points), bf16),
            pltpu.VMEM((NT, pairs // 2, 16, points), bf16),
            pltpu.VMEM((NFFT, points), bf16),
            pltpu.VMEM((NT, 2, 16, points), bf16),
            pltpu.VMEM((2, 16, points), bf16),
            pltpu.VMEM((points // LANES, 8 * SLOTS, LANES), f32),
            pltpu.VMEM((FULL, 2, 2, KEPT, LANES), f32),
            pltpu.VMEM((FULL, 2, KEPT, LANES), f32),
            pltpu.VMEM((FULL, 2, KEPT, LANES), f32),
            pltpu.VMEM((FULL, NZ, KEPT, LANES), f32),
            pltpu.VMEM((2, 2, KEPT, LANES), f32),
            pltpu.VMEM((2, KEPT, LANES), f32),
            pltpu.VMEM((2, KEPT, LANES), f32),
            pltpu.VMEM((NZ, KEPT, LANES), f32),
            pltpu.VMEM((NZ, NT, KEPT, LANES), f32),
            pltpu.VMEM((NT, 2, KEPT, LANES), f32),
            dma((6,)),
            dma, dma,
            dma((FULL, 3, NT - 1)), dma((FULL, 3, NT - 1)),
            dma((NT - 1,)), dma((NT - 1,)),
            dma((2, NT - 1)), dma((2, NT - 1)),
            dma((lane_tiles,)), dma((2, lane_tiles)),
            dma((lane_tiles, NT - 1)), dma((lane_tiles,)),
            dma((FULL, PIECES)), dma((FULL, PIECES)),
            dma((FULL, 2, PIECES)), dma((FULL, NZ, PIECES)),
            dma((2, PIECES)), dma((2, PIECES)),
            dma((PIECES,)), dma((NZ, PIECES)),
            dma((NT,)), dma((NZ, NT)),
            dma((2, PIECES, NT - 1)), dma((2, PIECES, NT - 1)),
        ],
        compiler_params=pltpu.CompilerParams(
            collective_id=0, has_side_effects=True, vmem_limit_bytes=40 * 2**20
        ),
        name="spectra_cross",
    )(*pinned)
    full = pl.pallas_call(
        finish,
        out_shape=jax.ShapeDtypeStruct((2 * NT * 2 * count, count), f32),
        in_specs=[vmem],
        out_specs=hbm,
        scratch_shapes=[pltpu.VMEM((2 * NT * 2 * count, count), f32), dma((2,))],
        name="hermitian_parts",
    )(pltpu.with_memory_space_constraint(sums, pltpu.VMEM))
    return full.reshape(2 * NT, count, 2, count).transpose(0, 2, 1, 3)


def cross_matrices(stacked):
    blocks = stacked.shape[1] // 2
    products = jnp.einsum("fip,fjp->fij", stacked, stacked, preferred_element_type=jnp.float32)
    matrix_re = products[:, :blocks, :blocks] + products[:, blocks:, blocks:]
    matrix_im = products[:, :blocks, blocks:] - products[:, blocks:, :blocks]
    return jnp.stack([matrix_re, matrix_im], axis=1)


def general(codes, scales, weights, freq_indices):
    values = (codes.astype(jnp.float32) * scales[:, None]).astype(jnp.bfloat16)
    regrouped = lax.all_to_all(values, "tm", split_axis=1, concat_axis=0, tiled=True)
    point_count = regrouped.shape[1]
    own_weights = lax.dynamic_slice_in_dim(
        weights, lax.axis_index("tm") * point_count, point_count, 0
    )
    total_points = weights.shape[0] * lax.axis_size("pts")
    root_weight = jnp.sqrt(own_weights / total_points)
    cosine_table, sine_table = make_tables(freq_indices)
    hop_rows = regrouped.reshape(-1, NFFT // 2, point_count)
    windows = jnp.concatenate([hop_rows[:-1], hop_rows[1:]], axis=1)
    real_part = jnp.einsum("fn,bnp->fbp", cosine_table, windows, preferred_element_type=jnp.float32)
    imag_part = jnp.einsum("fn,bnp->fbp", sine_table, windows, preferred_element_type=jnp.float32)
    scaled_re = (real_part * root_weight[None, None, :]).astype(jnp.bfloat16)
    scaled_im = (imag_part * root_weight[None, None, :]).astype(jnp.bfloat16)
    stacked = jnp.concatenate([scaled_re, scaled_im], axis=1)
    partial_value = lax.psum_scatter(
        cross_matrices(stacked), "pts", scatter_dimension=0, tiled=True
    )
    return lax.psum(partial_value, "tm")


def solution(mesh):
    nt, np_ = mesh.shape["tm"], mesh.shape["pts"]

    def per_device(codes, scales, weights, freq_indices):
        rows, points = codes.shape
        fits = (
            nt == NT
            and np_ == 2 * NZ
            and freq_indices.shape[0] == 2 * nt * np_
            and points % LANES == 0
            and rows % (2 * NFFT) == NFFT + HALF
            and rows >= 16 * HOP
            and NT * (rows // HOP) + 1 <= SPAN
        )
        if fits:
            return fused(codes, scales, weights, freq_indices, points * np_)
        return general(codes, scales, weights, freq_indices)

    return jax.shard_map(
        per_device,
        mesh=mesh,
        in_specs=(P("tm", "pts"), P("tm"), P("pts"), P()),
        out_specs=P("pts", None, None, None),
        check_vma=False,
    )
```

```python
import functools
import math

import jax
import jax.numpy as jnp
from jax import lax
from jax.experimental import pallas as pl
from jax.experimental.pallas import tpu as pltpu
from jax.sharding import PartitionSpec as P

NFFT = 256
HOP = NFFT // 2
HALF = HOP // 2
LANES = 128
SLOTS = 96
KEPT = 64
SPAN = 89
NT = 4
NZ = 4
QUARTERS = 4
FULL = 3
ROW_PARTS = ((0, 64),)
PIECES = len(ROW_PARTS)
ZSETS = ((0, 3), (1, 2))
ORDERS = (
    ((0, 0), (0, 1), (3, 0), (3, 1)),
    ((1, 0), (1, 1), (2, 0), (2, 1)),
    ((0, 0), (0, 1), (3, 0), (3, 1)),
    ((1, 1), (2, 0), (1, 0), (2, 1)),
)
MESH = pl.DeviceIdType.MESH


def make_tables(freq_indices):
    sample = jnp.arange(NFFT, dtype=jnp.int32)
    phases = freq_indices[:, None] * sample[None, :] % NFFT
    angles = phases.astype(jnp.float32) * (2.0 * math.pi / NFFT)
    hann_window = 0.5 - 0.5 * jnp.cos(sample.astype(jnp.float32) * (2.0 * math.pi / NFFT))
    cosine_table = (0.25 * hann_window[None, :] * jnp.cos(angles)).astype(jnp.bfloat16)
    sine_table = (-0.25 * hann_window[None, :] * jnp.sin(angles)).astype(jnp.bfloat16)
    return (cosine_table, sine_table)


def turn_waves(turn):
    angle = turn.astype(jnp.float32) * (2.0 * math.pi / NFFT)
    quarter = (turn + NFFT // 8) // (NFFT // 4)
    count = quarter.astype(jnp.float32)
    x = ((angle - count * 1.5703125) - count * 4.837512969970703125e-4) - count * 7.549789948768648e-8
    y = x * x
    sine = x + x * y * (-1.0 / 6.0 + y * (1.0 / 120.0 + y * (-1.0 / 5040.0 + y * (1.0 / 362880.0))))
    cosine = 1.0 + y * (-0.5 + y * (1.0 / 24.0 + y * (-1.0 / 720.0 + y * (1.0 / 40320.0))))
    swap = quarter % 2 == 1
    low = jnp.where(swap, sine, cosine)
    high = jnp.where(swap, cosine, sine)
    return (
        jnp.where((quarter + 1) % 4 >= 2, -low, low),
        jnp.where(quarter % 4 >= 2, -high, high),
    )


def fold(matrix):
    lane = lax.broadcasted_iota(jnp.int32, (KEPT, LANES), 1)
    size = SLOTS - KEPT
    first = 2 * SPAN - KEPT
    rest = jnp.zeros((LANES - size, LANES), jnp.float32)
    turned = jnp.concatenate([matrix[KEPT:], rest], axis=0).T
    corner = turned[KEPT:SLOTS]
    corners = jnp.concatenate(
        [pltpu.roll(corner, first, 1), pltpu.roll(corner, 2 * first - LANES, 1)], axis=0
    )
    side = pltpu.roll(turned[:KEPT], SPAN, 1)
    return jnp.where(lane < SPAN, matrix[:KEPT], jnp.where(lane < first, side, corners))


def unfold(folded):
    lane = lax.broadcasted_iota(jnp.int32, (KEPT, LANES), 1)
    size = SLOTS - KEPT
    here = lane[:size]
    wide = LANES - (2 * SPAN - KEPT)
    top = jnp.where(lane < SPAN, folded, 0.0)
    side = jnp.where(lane < SPAN - KEPT, pltpu.roll(folded, LANES - SPAN, 1), 0.0)
    corner = jnp.where(
        here < wide, pltpu.roll(folded[:size], wide, 1), pltpu.roll(folded[size:], 2 * wide, 1)
    )
    corner = jnp.where(here < SPAN - KEPT, corner, 0.0)
    rest = jnp.zeros((LANES - SLOTS, LANES), jnp.float32)
    turned = jnp.concatenate([side, corner, rest], axis=0).T
    return jnp.concatenate([top, turned[:size]], axis=0)


def kernel(
    total_points,
    codes_hbm, scales_hbm, weights_hbm, freq_hbm, out_ref,
    codes_ref, scales_v, weights_v, freq_ref, spread, vals, table, sbuf, rbuf, sfirst, rfirst, slast, rlast, hops, spbuf, sprecv, stage,
    part, corebuf, summed, zbuf, part2, corebuf2, summed2, zbuf2, homebuf, gath,
    load_s, halo_s, halo_r, tm_s, tm_r, first_s, first_r, last_s, last_r, hop_s, hop_r, sp_s, sp_r, core_s, core_r, z_s, z_r, core2_s, core2_r, z2_s, z2_r, home_s, home_r, g_s, g_r,
):
    rows, points = codes_ref.shape
    t = lax.axis_index("tm")
    p = lax.axis_index("pts")
    z = p // 2
    c = p % 2
    odd = t % 2
    partner = p + 1 - 2 * c
    lane_tiles = points // LANES
    blocks = rows // HOP
    pairs = blocks // 2
    padded = rows + HALF

    early = (10 * HOP)
    late = rows - early - HALF
    edge_at = (1 - odd) * (rows - HALF)
    early_at = odd * (rows - early)
    late_at = odd * HALF + (1 - odd) * early

    def load(at, count, sem):
        at = pl.ds(pl.multiple_of(at, HALF), count)
        return pltpu.make_async_copy(codes_hbm.at[at], codes_ref.at[at], load_s.at[sem])

    load_scales = pltpu.make_async_copy(scales_hbm, scales_v, load_s.at[3])
    load_weights = pltpu.make_async_copy(weights_hbm, weights_v, load_s.at[4])
    load_freq = pltpu.make_async_copy(freq_hbm, freq_ref, load_s.at[5])
    load_edge = load(edge_at, HALF, 0)
    load_early = load(early_at, early, 1)
    load_late = load(late_at, late, 2)
    barrier = pltpu.get_barrier_semaphore()
    for d in range(1, NT):
        pl.semaphore_signal(barrier, inc=1, device_id=(t ^ d, p), device_id_type=MESH)
    pl.semaphore_signal(barrier, inc=1, device_id=(t, partner), device_id_type=MESH)
    for d in range(1, NZ):
        pl.semaphore_signal(barrier, inc=1, device_id=(t, (z + d) % NZ * 2 + c), device_id_type=MESH)
    load_freq.start()
    load_scales.start()
    load_edge.start()
    load_early.start()
    load_weights.start()
    load_late.start()

    sample = lax.broadcasted_iota(jnp.int32, (8, NFFT), 1)
    sub = lax.broadcasted_iota(jnp.int32, (8, NFFT), 0)
    window_shape = 0.25 * (0.5 - 0.5 * turn_waves(sample)[0])

    def octet_table(dest, q):
        bins = jnp.zeros((8, NFFT), jnp.int32)
        for j in range(4):
            dest_p = ORDERS[q][j][0] * 2 + ORDERS[q][j][1]
            bins = jnp.where(sub // 2 == j, freq_ref[dest_p * 2 * NT + dest * 2 + q // 2], bins)
        cosine, sine = turn_waves(bins * sample % NFFT)
        return window_shape * jnp.where(sub % 2 == 0, cosine, -sine)

    load_scales.wait()
    for g in range(-(-rows // HOP)):
        size = min(HOP, rows - g * HOP)
        line = scales_v[g * HOP:g * HOP + size].reshape(1, size)
        spread[g * HOP:g * HOP + size, :] = jnp.broadcast_to(line, (LANES, size)).T

    offset = odd * HALF

    def dequantize(i, carry):
        at = pl.ds(pl.multiple_of(i * HALF, HALF), HALF)
        to = pl.ds(pl.multiple_of(i * HALF + offset, HALF), HALF)
        scale = spread[at, :]
        for lane in range(lane_tiles):
            cols = slice(lane * LANES, (lane + 1) * LANES)
            vals[to, cols] = (codes_ref[at, cols].astype(jnp.float32) * scale).astype(jnp.bfloat16)
        return carry

    load_edge.wait()
    dequantize(edge_at // HALF, 0)
    halo_from = (1 - odd) * (rows - HALF) + odd * HALF
    halo_to = odd * rows
    halo_mine = (1 - odd) * rows

    def halo_copy(dst):
        return pltpu.make_async_remote_copy(
            src_ref=vals.at[pl.ds(pl.multiple_of(halo_from, HALF), HALF)],
            dst_ref=vals.at[pl.ds(pl.multiple_of(dst, HALF), HALF)],
            send_sem=halo_s, recv_sem=halo_r,
            device_id=(t ^ 1, p), device_id_type=MESH,
        )

    load_early.wait()
    lax.fori_loop(early_at // HALF, (early_at + early) // HALF, dequantize, 0)
    load_weights.wait()
    root_weight = jnp.sqrt(weights_v[...].reshape(1, points) / total_points)

    def spectrum(i):
        window = vals[pl.ds(pl.multiple_of(i * HOP, HOP), NFFT), :]
        return jnp.dot(table[...], window, preferred_element_type=jnp.float32) * root_weight

    def octets(result, dest, q):
        return result[dest * 32 + q * 8:dest * 32 + q * 8 + 8]

    def pair_tiles(jj, first, second):
        for dest in range(NT):
            for q in range(FULL):
                both = jnp.concatenate([octets(first, dest, q), octets(second, dest, q)], axis=0)
                sbuf[q, dest, jj] = both.astype(jnp.bfloat16)

    def spectra(u, carry):
        low = odd * (pairs - 2 - 2 * u) + (1 - odd) * 2 * u
        results = [spectrum(2 * low + r) for r in range(4)]
        pair_tiles(low, results[0], results[1])
        pair_tiles(low + 1, results[2], results[3])
        v = odd * (quads - 1 - u) + (1 - odd) * u
        for dest in range(NT):
            last = [octets(r, dest, FULL) for r in results]
            sfirst[dest, v] = jnp.concatenate([o[:4] for o in last], axis=0).astype(jnp.bfloat16)
            slast[dest, v] = jnp.concatenate([o[4:] for o in last], axis=0).astype(jnp.bfloat16)
        return carry

    def spectra_pair():
        jj = (1 - odd) * (pairs - 1)
        first, second = spectrum(2 * jj), spectrum(2 * jj + 1)
        pair_tiles(jj, first, second)
        for dest in range(NT):
            one, two = octets(first, dest, FULL), octets(second, dest, FULL)
            mixed = jnp.concatenate([one[:4], two[:4], one[4:], two[4:]], axis=0)
            sfirst[dest, quads] = mixed.astype(jnp.bfloat16)

    quads = pairs // 2
    q_cut = 1
    cuts = (0, 2 * q_cut, pairs - 1, pairs)
    partners = (3, 1, 2)

    def tiles_of(who, piece):
        count = cuts[piece + 1] - cuts[piece]
        flip = who % 2
        return flip * (pairs - cuts[piece + 1]) + (1 - flip) * cuts[piece], count

    def exchange(q, piece, d, source):
        at, count = tiles_of(source, piece)
        return pltpu.make_async_remote_copy(
            src_ref=sbuf.at[q, t ^ d, pl.ds(at, count)],
            dst_ref=rbuf.at[q, source, pl.ds(at, count)],
            send_sem=tm_s.at[q, piece, d - 1], recv_sem=tm_r.at[q, piece, d - 1],
            device_id=(t ^ d, p), device_id_type=MESH,
        )

    def exchange_first(d, source):
        return pltpu.make_async_remote_copy(
            src_ref=sfirst.at[t ^ d], dst_ref=rfirst.at[source],
            send_sem=first_s.at[d - 1], recv_sem=first_r.at[d - 1],
            device_id=(t ^ d, p), device_id_type=MESH,
        )

    last_cuts = (0, 4, quads)

    def exchange_last(piece, d, source):
        at = pl.ds(last_cuts[piece], last_cuts[piece + 1] - last_cuts[piece])
        return pltpu.make_async_remote_copy(
            src_ref=slast.at[t ^ d, at], dst_ref=rlast.at[source, at],
            send_sem=last_s.at[piece, d - 1], recv_sem=last_r.at[piece, d - 1],
            device_id=(t ^ d, p), device_id_type=MESH,
        )

    middle = (t == 1) | (t == 2)
    outer = (t == 0) | (t == 3)

    def owner(lane):
        if 2 * lane + 1 == lane_tiles:
            return (NT - 1) * (1 - c)
        return (NT - 1) * int(2 * lane + 1 > lane_tiles)

    def lanes(lane):
        return pl.ds(lane * LANES, LANES)

    def hop_copy(lane, source, dest):
        return pltpu.make_async_remote_copy(
            src_ref=vals.at[pl.ds(pl.multiple_of(odd * (padded - HOP), HOP), HOP), lanes(lane)],
            dst_ref=hops.at[pl.ds(pl.multiple_of((source - 1) * HOP, HOP), HOP), lanes(lane)],
            send_sem=hop_s.at[lane], recv_sem=hop_r.at[source - 1, lane],
            device_id=(dest, p), device_id_type=MESH,
        )

    def straddle(lane, d):
        return pltpu.make_async_remote_copy(
            src_ref=spbuf.at[t ^ d, :, :, lanes(lane)],
            dst_ref=sprecv.at[:, :, lanes(lane)],
            send_sem=sp_s.at[lane, d - 1], recv_sem=sp_r.at[lane],
            device_id=(t ^ d, p), device_id_type=MESH,
        )

    def send(q, piece):
        for d in partners:
            exchange(q, piece, d, t).start()


    pl.semaphore_wait(barrier, NT + NZ - 1)
    halo_copy(halo_to).start()

    @pl.when(middle)
    def _():
        for lane in range(lane_tiles):
            hop_copy(lane, t, owner(lane)).start()

    load_freq.wait()
    for dest in range(NT):
        for half in range(2):
            at = dest * 32 + half * 16
            pair = [octet_table(dest, 2 * half), octet_table(dest, 2 * half + 1)]
            table[at:at + 16, :] = jnp.concatenate(pair, axis=0).astype(jnp.bfloat16)

    lax.fori_loop(0, q_cut, spectra, 0)
    send(0, 0)
    load_late.wait()
    lax.fori_loop(late_at // HALF, (late_at + late) // HALF, dequantize, 0)
    lax.fori_loop(q_cut, quads, spectra, 0)
    send(0, 1)
    halo_copy(halo_mine).wait_recv()
    spectra_pair()
    send(0, 2)

    @pl.when(outer)
    def _():
        for lane in range(lane_tiles):
            @pl.when(t == owner(lane))
            def _():
                for source in (1, 2):
                    hop_copy(lane, source, owner(lane)).wait_recv()
        result = jnp.dot(table[...], hops[...], preferred_element_type=jnp.float32)
        result = (result * root_weight).astype(jnp.bfloat16)
        for dest in range(NT):
            for h in range(2):
                spbuf[dest, h] = result[dest * 32 + h * 16:dest * 32 + h * 16 + 16]
        for lane in range(lane_tiles):
            @pl.when(t == owner(lane))
            def _():
                for d in partners:
                    straddle(lane, d).start()
                sprecv[:, :, lanes(lane)] = spbuf[t, :, :, lanes(lane)]

    for piece in range(3):
        send(1, piece)

    for lane in range(lane_tiles):
        for s in range(8):
            stage[lane, s * SLOTS + SLOTS - 8:(s + 1) * SLOTS, :] = jnp.zeros((8, LANES), jnp.float32)

    def place(b, octet):
        for lane in range(lane_tiles):
            stage[lane, pl.ds(b, 8, stride=SLOTS), :] = octet[:, lane * LANES:(lane + 1) * LANES]

    def unpack(source_ref, q, who, piece):
        at, count = tiles_of(who, piece)
        base = who * blocks + who // 2

        def one(i, carry):
            tile = source_ref[q, who, i].astype(jnp.float32)
            place(base + 2 * i, tile[:8])
            place(base + 2 * i + 1, tile[8:])
            return carry

        lax.fori_loop(at, at + count, one, 0)

    def place_four(half, b, octet):
        for lane in range(lane_tiles):
            at = pl.ds(half * 4 * SLOTS + b, 4, stride=SLOTS)
            stage[lane, at, :] = octet[:, lane * LANES:(lane + 1) * LANES]

    def unpack_fours(source_ref, half, who, first, last):
        base = who * blocks + who // 2 + 2 * (who % 2)

        def one(v, carry):
            tile = source_ref[who, v].astype(jnp.float32)
            for r in range(4):
                place_four(half, base + 4 * v + r, tile[4 * r:4 * r + 4])
            return carry

        lax.fori_loop(first, last, one, 0)

    def unpack_mixed(source_ref, who):
        base = who * blocks + who // 2 + (1 - who % 2) * 2 * (pairs - 1)
        tile = source_ref[who, quads].astype(jnp.float32)
        for r in range(4):
            place_four(r // 2, base + r % 2, tile[4 * r:4 * r + 4])

    def gram(j):
        at = pl.ds(pl.multiple_of(j * 2 * SLOTS, 2 * SLOTS), 2 * SLOTS)
        stacked = jnp.concatenate(
            [stage[lane, at, :].astype(jnp.bfloat16) for lane in range(lane_tiles)], axis=1
        )
        fill = jnp.zeros((LANES - SLOTS, points), jnp.bfloat16)
        wide = jnp.concatenate([stacked[:SLOTS], fill, stacked[SLOTS:], fill], axis=0)
        prod = lax.dot_general(
            stacked, wide, (((1,), (1,)), ((), ())), preferred_element_type=jnp.float32
        )
        real = prod[:SLOTS, :LANES] + prod[SLOTS:, LANES:]
        imag = prod[:SLOTS, LANES:] - prod[SLOTS:, :LANES]
        return fold(real + imag)

    def rows_of(h):
        return pl.ds(*ROW_PARTS[h])

    def to_core(q, h):
        return pltpu.make_async_remote_copy(
            src_ref=part.at[q, 1 - c, :, rows_of(h)], dst_ref=corebuf.at[q, :, rows_of(h)],
            send_sem=core_s.at[q, h], recv_sem=core_r.at[q, h],
            device_id=(t, partner), device_id_type=MESH,
        )

    def to_z(q, s, h, source):
        return pltpu.make_async_remote_copy(
            src_ref=summed.at[q, s, rows_of(h)], dst_ref=zbuf.at[q, source, rows_of(h)],
            send_sem=z_s.at[q, s, h], recv_sem=z_r.at[q, source, h],
            device_id=(t, ZSETS[q % 2][s] * 2 + c), device_id_type=MESH,
        )

    def home_of(e):
        return (1 - e) * (2 - c) + e * (1 + c)

    def to_core2(e, h):
        return pltpu.make_async_remote_copy(
            src_ref=part2.at[e, 1 - c, rows_of(h)], dst_ref=corebuf2.at[e, rows_of(h)],
            send_sem=core2_s.at[e, h], recv_sem=core2_r.at[e, h],
            device_id=(t, partner), device_id_type=MESH,
        )

    def to_z2(h, source):
        return pltpu.make_async_remote_copy(
            src_ref=summed2.at[0, rows_of(h)], dst_ref=zbuf2.at[source, rows_of(h)],
            send_sem=z2_s.at[h], recv_sem=z2_r.at[source, h],
            device_id=(t, home_of(0) * 2 + c), device_id_type=MESH,
        )

    def to_home(d, source_z, source_t):
        return pltpu.make_async_remote_copy(
            src_ref=summed2.at[1], dst_ref=homebuf.at[source_z, source_t],
            send_sem=home_s.at[d], recv_sem=home_r.at[source_z, source_t],
            device_id=(t ^ d, home_of(1) * 2 + c), device_id_type=MESH,
        )

    def gram2(e, side):
        part2[e, side] = gram((1 - e) * (1 - side) + e * (2 + side))

    def core_sum2(e, h):
        to_core2(e, h).wait_recv()
        at = rows_of(h)
        summed2[e, at] = part2[e, c, at] + corebuf2[e, at]

    def core_stage2(h):
        core_sum2(0, h)

        @pl.when(z != home_of(0))
        def _():
            to_z2(h, z).start()

    def home_stage():
        for h in range(PIECES):
            core_sum2(1, h)
        for d in partners:
            to_home(d, z, t).start()

        @pl.when(z != home_of(1))
        def _():
            to_home(0, z, t).start()

    def z_stage2(h):
        @pl.when(z == home_of(0))
        def _():
            at = rows_of(h)
            total = summed2[0, at]
            for d in range(1, NZ):
                other = (z + d) % NZ
                to_z2(h, other).wait_recv()
                total = total + zbuf2[other, at]
            gath[t, 1, at] = total
            for d in partners:
                to_tm(1, h, d, t).start()

    def to_tm(k, h, d, source):
        return pltpu.make_async_remote_copy(
            src_ref=gath.at[source, k, rows_of(h)], dst_ref=gath.at[source, k, rows_of(h)],
            send_sem=g_s.at[k, h, d - 1], recv_sem=g_r.at[k, h, d - 1],
            device_id=(t ^ d, p), device_id_type=MESH,
        )

    def receive(q, pieces):
        for piece in pieces:
            for d in partners:
                exchange(q, piece, d, t ^ d).wait_recv()
                unpack(rbuf, q, t ^ d, piece)

    def own(q):
        for piece in range(3):
            unpack(sbuf, q, t, piece)

    def straddling(q):
        if q == 0:
            for lane in range(lane_tiles):
                @pl.when(t != owner(lane))
                def _():
                    straddle(lane, 1).wait_recv()
        at = q % 2 * 8
        place(2 * blocks, sprecv[q // 2].astype(jnp.float32)[at:at + 8])

    def core_stage(q, h):
        to_core(q, h).wait_recv()
        for s in range(2):
            at = rows_of(h)
            summed[q, s, at] = part[q, c, s, at] + corebuf[q, s, at]

            @pl.when(z != ZSETS[q % 2][s])
            def _():
                to_z(q, s, h, z).start()

    def at_home(q):
        return (z == ZSETS[q % 2][0]) | (z == ZSETS[q % 2][1])

    def z_stage(q, h):
        for s in range(2):
            home = ZSETS[q % 2][s]

            @pl.when(z == home)
            def _():
                at = rows_of(h)
                total = summed[q, s, at]
                for other in range(NZ):
                    if other != home:
                        to_z(q, s, h, other).wait_recv()
                        total = total + zbuf[q, other, at]
                gath[t, q // 2, at] = total

    def spread_result(q, h):
        @pl.when(at_home(q))
        def _():
            for d in partners:
                to_tm(q // 2, h, d, t).start()

    def send_first():
        for d in partners:
            exchange_first(d, t).start()

    def send_last():
        for piece in range(2):
            for d in partners:
                exchange_last(piece, d, t).start()

    for q in range(FULL):
        if q == 1:
            for piece in range(3):
                send(2, piece)
        if q == 2:
            send_first()
        own(q)
        receive(q, (0,))
        straddling(q)
        if q >= 1:
            for h in range(PIECES):
                z_stage(q - 1, h)
        receive(q, (1, 2))
        for s in range(2):
            part[q, 1 - c, s] = gram(2 * s + 1 - c)
        for h in range(PIECES):
            to_core(q, h).start()
        for s in range(2):
            part[q, c, s] = gram(2 * s + c)
        for h in range(PIECES):
            core_stage(q, h)

    send_last()
    unpack_fours(sfirst, 0, t, 0, quads)
    unpack_mixed(sfirst, t)
    unpack_fours(slast, 1, t, 0, quads)
    straddling(FULL)
    for d in partners:
        exchange_first(d, t ^ d).wait_recv()
        unpack_fours(rfirst, 0, t ^ d, 0, quads)
        unpack_mixed(rfirst, t ^ d)
    gram2(0, 1 - c)
    for h in range(PIECES):
        to_core2(0, h).start()
    gram2(0, c)
    for piece in range(2):
        for d in partners:
            exchange_last(piece, d, t ^ d).wait_recv()
            unpack_fours(rlast, 1, t ^ d, last_cuts[piece], last_cuts[piece + 1])
        if piece == 0:
            for h in range(PIECES):
                core_stage2(h)
                spread_result(0, h)
                spread_result(1, h)
    gram2(1, 1 - c)
    for h in range(PIECES):
        to_core2(1, h).start()
    gram2(1, c)
    home_stage()
    for h in range(PIECES):
        z_stage(2, h)
        spread_result(2, h)
    for h in range(PIECES):
        z_stage2(h)
    halo_copy(halo_to).wait_send()
    for d in partners:
        exchange_first(d, t).wait_send()
        for piece in range(2):
            exchange_last(piece, d, t).wait_send()
    for q in range(FULL):
        for piece in range(3):
            for d in partners:
                exchange(q, piece, d, t).wait_send()
        for h in range(PIECES):
            to_core(q, h).wait_send()
        for s in range(2):
            @pl.when(z != ZSETS[q % 2][s])
            def _():
                for h in range(PIECES):
                    to_z(q, s, h, z).wait_send()
    for lane in range(lane_tiles):
        @pl.when(middle)
        def _():
            hop_copy(lane, t, owner(lane)).wait_send()

        @pl.when(t == owner(lane))
        def _():
            for d in partners:
                straddle(lane, d).wait_send()

    for h in range(PIECES):
        to_core2(0, h).wait_send()

        @pl.when(z != home_of(0))
        def _():
            to_z2(h, z).wait_send()

        for d in partners:
            to_tm(0, h, d, t).wait_send()

    def gathered(k):
        out_ref[t * 2 + k] = unfold(gath[t, k])
        for d in (1, 2, 3):
            for h in range(PIECES):
                to_tm(k, h, d, t ^ d).wait_recv()
            out_ref[(t ^ d) * 2 + k] = unfold(gath[t ^ d, k])

    gathered(0)

    @pl.when(z != home_of(1))
    def _():
        gathered(1)
        for h in range(PIECES):
            for d in partners:
                to_tm(1, h, d, t).wait_send()

    @pl.when(z == home_of(1))
    def _():
        for d in range(NT):
            source = t ^ d
            if d == 0:
                total = summed2[1]
            else:
                to_home(d, z, source).wait_recv()
                total = homebuf[z, source]
            for step in range(1, NZ):
                other = (z + step) % NZ
                to_home(d, other, source).wait_recv()
                total = total + homebuf[other, source]
            out_ref[source * 2 + 1] = unfold(total)

    for h in range(PIECES):
        to_core2(1, h).wait_send()
    for d in partners:
        to_home(d, z, t).wait_send()

    @pl.when(z != home_of(1))
    def _():
        to_home(0, z, t).wait_send()


def finish(sums_ref, out_hbm, both, sems):
    freqs = sums_ref.shape[0]
    count = out_hbm.shape[1]

    def copy(part):
        size = freqs // 2 * 2 * count
        at = pl.ds(part * size, size)
        return pltpu.make_async_copy(both.at[at], out_hbm.at[at], sems.at[part])

    for part in range(2):
        for f in range(part * freqs // 2, (part + 1) * freqs // 2):
            ordered = sums_ref[f]
            fill = jnp.zeros((LANES - SLOTS, LANES), jnp.float32)
            mirrored = jnp.concatenate([ordered, fill], axis=0).T[:SLOTS]
            first = f * 2 * count
            both[pl.ds(first, count, stride=2), :] = 0.5 * (ordered + mirrored)[:count, :count]
            both[pl.ds(first + 1, count, stride=2), :] = 0.5 * (ordered - mirrored)[:count, :count]
        copy(part).start()
    for part in range(2):
        copy(part).wait()


def fused(codes, scales, weights, freq_indices, total_points):
    rows, points = codes.shape
    blocks = rows // HOP
    pairs = blocks // 2
    lane_tiles = points // LANES
    count = rows * NT // HOP - 1
    f32, bf16 = jnp.float32, jnp.bfloat16
    dma = pltpu.SemaphoreType.DMA
    hbm = pl.BlockSpec(memory_space=pltpu.HBM)
    vmem = pl.BlockSpec(memory_space=pltpu.VMEM)
    pinned = [
        pltpu.with_memory_space_constraint(x, pltpu.HBM) for x in (codes, scales, weights, freq_indices)
    ]
    sums = pl.pallas_call(
        functools.partial(kernel, total_points),
        out_shape=jax.ShapeDtypeStruct((2 * NT, SLOTS, LANES), f32),
        in_specs=[hbm, hbm, hbm, hbm],
        out_specs=vmem,
        scratch_shapes=[
            pltpu.VMEM((rows, points), bf16),
            pltpu.VMEM((rows,), f32),
            pltpu.VMEM((points,), f32),
            pltpu.SMEM(freq_indices.shape, jnp.int32),
            pltpu.VMEM((rows, LANES), f32),
            pltpu.VMEM((rows + HALF, points), bf16),
            pltpu.VMEM((2 * NT * QUARTERS * 4, NFFT), bf16),
            pltpu.VMEM((FULL, NT, pairs, 16, points), bf16),
            pltpu.VMEM((FULL, NT, pairs, 16, points), bf16),
            pltpu.VMEM((NT, pairs // 2 + 1, 16, points), bf16),
            pltpu.VMEM((NT, pairs // 2 + 1, 16, points), bf16),
            pltpu.VMEM((NT, pairs // 2, 16, points), bf16),
            pltpu.VMEM((NT, pairs // 2, 16, points), bf16),
            pltpu.VMEM((NFFT, points), bf16),
            pltpu.VMEM((NT, 2, 16, points), bf16),
            pltpu.VMEM((2, 16, points), bf16),
            pltpu.VMEM((points // LANES, 12 * SLOTS, LANES), f32),
            pltpu.VMEM((FULL, 2, 2, KEPT, LANES), f32),
            pltpu.VMEM((FULL, 2, KEPT, LANES), f32),
            pltpu.VMEM((FULL, 2, KEPT, LANES), f32),
            pltpu.VMEM((FULL, NZ, KEPT, LANES), f32),
            pltpu.VMEM((2, 2, KEPT, LANES), f32),
            pltpu.VMEM((2, KEPT, LANES), f32),
            pltpu.VMEM((2, KEPT, LANES), f32),
            pltpu.VMEM((NZ, KEPT, LANES), f32),
            pltpu.VMEM((NZ, NT, KEPT, LANES), f32),
            pltpu.VMEM((NT, 2, KEPT, LANES), f32),
            dma((6,)),
            dma, dma,
            dma((FULL, 3, NT - 1)), dma((FULL, 3, NT - 1)),
            dma((NT - 1,)), dma((NT - 1,)),
            dma((2, NT - 1)), dma((2, NT - 1)),
            dma((lane_tiles,)), dma((2, lane_tiles)),
            dma((lane_tiles, NT - 1)), dma((lane_tiles,)),
            dma((FULL, PIECES)), dma((FULL, PIECES)),
            dma((FULL, 2, PIECES)), dma((FULL, NZ, PIECES)),
            dma((2, PIECES)), dma((2, PIECES)),
            dma((PIECES,)), dma((NZ, PIECES)),
            dma((NT,)), dma((NZ, NT)),
            dma((2, PIECES, NT - 1)), dma((2, PIECES, NT - 1)),
        ],
        compiler_params=pltpu.CompilerParams(
            collective_id=0, has_side_effects=True, vmem_limit_bytes=40 * 2**20
        ),
        name="spectra_cross",
    )(*pinned)
    full = pl.pallas_call(
        finish,
        out_shape=jax.ShapeDtypeStruct((2 * NT * 2 * count, count), f32),
        in_specs=[vmem],
        out_specs=hbm,
        scratch_shapes=[pltpu.VMEM((2 * NT * 2 * count + 16, count), f32), dma((2,))],
        name="hermitian_parts",
    )(pltpu.with_memory_space_constraint(sums, pltpu.VMEM))
    return full.reshape(2 * NT, count, 2, count).transpose(0, 2, 1, 3)


def cross_matrices(stacked):
    blocks = stacked.shape[1] // 2
    products = jnp.einsum("fip,fjp->fij", stacked, stacked, preferred_element_type=jnp.float32)
    matrix_re = products[:, :blocks, :blocks] + products[:, blocks:, blocks:]
    matrix_im = products[:, :blocks, blocks:] - products[:, blocks:, :blocks]
    return jnp.stack([matrix_re, matrix_im], axis=1)


def general(codes, scales, weights, freq_indices):
    values = (codes.astype(jnp.float32) * scales[:, None]).astype(jnp.bfloat16)
    regrouped = lax.all_to_all(values, "tm", split_axis=1, concat_axis=0, tiled=True)
    point_count = regrouped.shape[1]
    own_weights = lax.dynamic_slice_in_dim(
        weights, lax.axis_index("tm") * point_count, point_count, 0
    )
    total_points = weights.shape[0] * lax.axis_size("pts")
    root_weight = jnp.sqrt(own_weights / total_points)
    cosine_table, sine_table = make_tables(freq_indices)
    hop_rows = regrouped.reshape(-1, NFFT // 2, point_count)
    windows = jnp.concatenate([hop_rows[:-1], hop_rows[1:]], axis=1)
    real_part = jnp.einsum("fn,bnp->fbp", cosine_table, windows, preferred_element_type=jnp.float32)
    imag_part = jnp.einsum("fn,bnp->fbp", sine_table, windows, preferred_element_type=jnp.float32)
    scaled_re = (real_part * root_weight[None, None, :]).astype(jnp.bfloat16)
    scaled_im = (imag_part * root_weight[None, None, :]).astype(jnp.bfloat16)
    stacked = jnp.concatenate([scaled_re, scaled_im], axis=1)
    partial_value = lax.psum_scatter(
        cross_matrices(stacked), "pts", scatter_dimension=0, tiled=True
    )
    return lax.psum(partial_value, "tm")


def solution(mesh):
    nt, np_ = mesh.shape["tm"], mesh.shape["pts"]

    def per_device(codes, scales, weights, freq_indices):
        rows, points = codes.shape
        fits = (
            nt == NT
            and np_ == 2 * NZ
            and freq_indices.shape[0] == 2 * nt * np_
            and points % LANES == 0
            and rows % (2 * NFFT) == NFFT + HALF
            and rows >= 16 * HOP
            and NT * (rows // HOP) + 1 <= SPAN
        )
        if fits:
            return fused(codes, scales, weights, freq_indices, points * np_)
        return general(codes, scales, weights, freq_indices)

    return jax.shard_map(
        per_device,
        mesh=mesh,
        in_specs=(P("tm", "pts"), P("tm"), P("pts"), P()),
        out_specs=P("pts", None, None, None),
        check_vma=False,
    )
```
